32 devices in a mesh: task: 2 (over core), dp: 16 (over z, y, x).
Axes of the slice: x: 2, y: 2, z: 4, core: 2. Of those that a mesh axis runs over, the one named last changes fastest.
Arguments:
- entries: bfloat16 [294912, 64], P('dp'), may hold values from -6 to 6
- lengths: int32 [16, 12288], P('dp'), may hold values from 1 to 64, 18432 in all within a row
- labels: int32 [2, 24576], P('task', 'dp'), may hold values from 0 to 1
- spec_w1: bfloat16 [2, 2, 512, 256], P('task', None, 'dp'), may hold values from -0.25 to 0.25
- spec_w2: bfloat16 [2, 2, 256, 256], P('task', None, 'dp'), may hold values from -0.375 to 0.375
- spec_gain: bfloat16 [2, 2, 256], P('task'), may hold values from 0.5 to 1.5
- spec_shift: bfloat16 [2, 2, 256], P('task'), may hold values from -0.59765625 to 0.59765625
- shared_w1: bfloat16 [2, 512, 256], P('task', 'dp'), may hold values from -0.25 to 0.25
- shared_w2: bfloat16 [2, 256, 256], P('task', 'dp'), may hold values from -0.375 to 0.375
- shared_gain: bfloat16 [2, 256], P('task'), may hold values from 0.5 to 1.5
- shared_shift: bfloat16 [2, 256], P('task'), may hold values from -0.59765625 to 0.59765625
- gate_w: bfloat16 [2, 512, 4], P('task'), may hold values from -0.25 to 0.25
- tower_w1: bfloat16 [2, 256, 128], P('task'), may hold values from -0.375 to 0.375
- tower_w2: bfloat16 [2, 128, 64], P('task'), may hold values from -0.5 to 0.5
- tower_w3: bfloat16 [2, 64], P('task'), may hold values from -0.75 to 0.75
Outputs:
- predictions: float32 [2, 24576], P('task', 'dp')
- entry_grads: bfloat16 [294912, 64], P('dp')
- spec_w1_grad: float32 [2, 2, 512, 256], P('task', None, 'dp')
- spec_w2_grad: float32 [2, 2, 256, 256], P('task', None, 'dp')
- spec_gain_grad: float32 [2, 2, 256], P('task')
- spec_shift_grad: float32 [2, 2, 256], P('task')
- shared_w1_grad: float32 [2, 512, 256], P('task', 'dp')
- shared_w2_grad: float32 [2, 256, 256], P('task', 'dp')
- shared_gain_grad: float32 [2, 256], P('task')
- shared_shift_grad: float32 [2, 256], P('task')
- gate_grad: float32 [2, 512, 4], P('task')
- tower1_grad: float32 [2, 256, 128], P('task')
- tower2_grad: float32 [2, 128, 64], P('task')
- tower3_grad: float32 [2, 64], P('task')
The draws below stay inside these ranges and needn't reach their ends.
Inputs may be any that keep to these rules, and one draw needn't show every extreme that they name: Each index of dp: its 12288 bag lengths sum to exactly 18432, and its longest bag has exactly 64 rows.
All inputs are finite; a program needn't handle non-finite values.
Results may differ from the reference program's by a relative error of at most 0.012.
Values may be sent and summed in bfloat16 or wider, within the bound.
No kernel may reach another device: no remote copies, remote signals or barrier semaphores. Data moves between devices by JAX's collectives and lax.ppermute only.
A program may use at most 128 MiB of HBM per device.

```python
import math
import jax
import jax.numpy as jnp
import numpy as np
from jax import lax

TASKS = 2
EXPERTS = 2
GATES = 4
EMB = 64
D = 512
HID = 256
TOWER1 = 128
TOWER2 = 64
EV_DEV = 1536
LMAX = 64
ENT_DEV = 18432
BAGS_DEV = 12288
EVENTS = 24576
ENTRIES = 294912
N_DP = 16


def set_ends(array, key, smallest, largest):
    dims = array.shape
    spot = [jax.random.randint(jax.random.fold_in(key, axis), (), 0, dims[axis]) for axis in range(len(dims))]
    array = array.at[tuple(spot)].set(smallest)
    longest = dims.index(max(dims))
    spot[longest] = (spot[longest] + 1) % dims[longest]
    return array.at[tuple(spot)].set(largest)


def steps_of(stream_key, extent, cuts, least, largest):
    gain, own = 1.0, jax.random.fold_in(stream_key, 6)
    for axis_at, parts in cuts:
        draws = jnp.exp(jax.random.uniform(jax.random.fold_in(own, axis_at), (parts,), jnp.float32, least / len(cuts), largest / len(cuts)))
        gain = gain * jnp.repeat(draws, extent[axis_at] // parts).reshape([-1 if axis == axis_at else 1 for axis in range(len(extent))])
    return gain


def length_profile(count, total, limit, skew):
    loads = [(1 << 20) // math.isqrt(standing ** skew) + 1 for standing in range(2, count + 1)]
    surplus, given = total - limit - (count - 1), [1] * (count - 1)
    while surplus > 0:
        free = [i for i in range(count - 1) if given[i] < limit]
        whole, budget = sum([loads[i] for i in free]), surplus
        for i in free:
            more = min(limit - given[i], max(1, budget * loads[i] // whole), surplus)
            given[i] = given[i] + more
            surplus = surplus - more
    return np.array([limit] + given)


def uneven_parts(rng, amount, total, bound, slope):
    if amount == 2:
        one = jax.random.randint(rng, (), max(1, total - bound), min(bound, total - 1) + 1)
        return jnp.stack([one, total - one])
    sizes = jnp.asarray(length_profile(amount, total, bound, slope), jnp.int32)
    twos = (amount - 1) // 2
    donor, sink = sizes[1:1 + 2 * twos:2], sizes[2:2 + 2 * twos:2]
    slack = jnp.minimum(donor - 1, bound - sink)
    moved = jax.random.randint(jax.random.fold_in(rng, 1), (twos,), 0, 1 << 20) % (slack + 1)
    sizes = sizes.at[1:1 + 2 * twos:2].set(donor - moved).at[2:2 + 2 * twos:2].set(sink + moved)
    return sizes[jax.random.permutation(jax.random.fold_in(rng, 2), amount)]


def centred(key, shape, width, reach, split=(), kind=jnp.bfloat16):
    result = width * jax.random.normal(key, shape, jnp.float32)
    if split:
        result = result * steps_of(key, shape, split, -0.22, 0.18)
    return jnp.clip(result, -reach, reach).astype(kind)


def setup_inputs(seed: int = 0) -> dict:
    splits = jax.random.split(jax.random.key(seed), 16)
    entries = centred(splits[0], (ENTRIES, EMB), 0.6, 6.0, ((0, 16),))
    lengths = jax.vmap(lambda own: uneven_parts(own, BAGS_DEV, ENT_DEV, LMAX, 2))(jax.random.split(splits[1], N_DP)).reshape((N_DP, BAGS_DEV)).astype(jnp.int32)
    labels = set_ends(jax.random.randint(splits[2], (TASKS, EVENTS), 0, 2), jax.random.fold_in(splits[2], 1), 0, 1).astype(jnp.int32)
    spec_w1 = centred(splits[3], (TASKS, EXPERTS, D, HID), D ** -0.5, 0.25, ((0, 2), (2, 16)))
    spec_w2 = centred(splits[4], (TASKS, EXPERTS, HID, HID), HID ** -0.5, 0.375, ((0, 2), (2, 16)))
    spec_gain = jnp.clip(1.0 + 0.1 * jax.random.normal(splits[5], (TASKS, EXPERTS, HID), jnp.float32), 0.5, 1.5).astype(jnp.bfloat16)
    spec_shift = centred(splits[6], (TASKS, EXPERTS, HID), 0.1, 0.59765625, ((0, 2),))
    shared_w1 = centred(splits[7], (TASKS, D, HID), D ** -0.5, 0.25, ((0, 2), (1, 16)))
    shared_w2 = centred(splits[8], (TASKS, HID, HID), HID ** -0.5, 0.375, ((0, 2), (1, 16)))
    shared_gain = jnp.clip(1.0 + 0.1 * jax.random.normal(splits[9], (TASKS, HID), jnp.float32), 0.5, 1.5).astype(jnp.bfloat16)
    shared_shift = centred(splits[10], (TASKS, HID), 0.1, 0.59765625, ((0, 2),))
    gate_w = centred(splits[11], (TASKS, D, GATES), D ** -0.5, 0.25, ((0, 2),))
    tower_w1 = centred(splits[12], (TASKS, HID, TOWER1), HID ** -0.5, 0.375, ((0, 2),))
    tower_w2 = centred(splits[13], (TASKS, TOWER1, TOWER2), TOWER1 ** -0.5, 0.5, ((0, 2),))
    tower_w3 = centred(splits[14], (TASKS, TOWER2), TOWER2 ** -0.5, 0.75, ((0, 2),))
    return dict(entries=entries, lengths=lengths, labels=labels, spec_w1=spec_w1, spec_w2=spec_w2, spec_gain=spec_gain, spec_shift=spec_shift, shared_w1=shared_w1, shared_w2=shared_w2, shared_gain=shared_gain, shared_shift=shared_shift, gate_w=gate_w, tower_w1=tower_w1, tower_w2=tower_w2, tower_w3=tower_w3)


EPSILON = 1e-05

@jax.custom_vjp
def low(v):
    return lax.optimization_barrier(v.astype(jnp.bfloat16)).astype(jnp.float32)

@jax.custom_vjp
def low_back(v):
    return v

def low_keep(v):
    return (low(v), None)

def low_pass(kept, grad):
    return (grad,)

def back_keep(v):
    return (v, None)

def back_low(kept, grad):
    return (low(grad),)
low.defvjp(low_keep, low_pass)
low_back.defvjp(back_keep, back_low)

def gelu_act(value):
    return jax.nn.gelu(value, approximate=True)

def product(left, right):
    return jnp.dot(left, right, precision=lax.Precision.HIGHEST)

def expert(features, first_w, second_w, gain_vec, shift_vec):
    pre_one = low_back(product(features, first_w))
    hidden_one = low(gelu_act(pre_one))
    pre_two = low_back(product(hidden_one, second_w))
    act_two = gelu_act(pre_two)
    centered = act_two - lax.optimization_barrier(jnp.mean(act_two, axis=-1, keepdims=True))
    normed = centered * lax.rsqrt(lax.optimization_barrier(jnp.mean(centered * centered, axis=-1, keepdims=True)) + EPSILON)
    return normed * gain_vec + shift_vec

def block_loss(row_block, label_block, segment_ids, spec_first, spec_second, spec_gains, spec_shifts, shared_first, shared_second, shared_gains, shared_shifts, gate_matrix, tower_first, tower_second, tower_third):
    bag_sums = jax.ops.segment_sum(row_block, segment_ids, num_segments=BAGS_DEV, indices_are_sorted=True)
    features = low(bag_sums.reshape(EV_DEV, D))
    shared_outs = [low(expert(features, shared_first[member], shared_second[member], shared_gains[member], shared_shifts[member])) for member in range(TASKS)]
    loss_total = 0.0
    predictions = []
    for task_id in range(TASKS):
        branches = [expert(features, spec_first[task_id, member], spec_second[task_id, member], spec_gains[task_id, member], spec_shifts[task_id, member]) for member in range(EXPERTS)] + shared_outs
        gate_probs = jax.nn.softmax(low_back(product(features, gate_matrix[task_id])), axis=-1)
        mixture = gate_probs[:, 0:1] * branches[0]
        for member in range(1, GATES):
            mixture = mixture + gate_probs[:, member:member + 1] * branches[member]
        tower_in = low(mixture)
        act_three = low(gelu_act(low_back(product(tower_in, tower_first[task_id]))))
        act_four = low(gelu_act(low_back(product(act_three, tower_second[task_id]))))
        logits = product(act_four, tower_third[task_id])
        loss_total = loss_total + jnp.sum(jax.nn.softplus(logits) - label_block[task_id] * logits)
        predictions.append(jax.nn.sigmoid(logits))
    return (loss_total, jnp.stack(predictions))

def reference(entries, lengths, labels, spec_w1, spec_w2, spec_gain, spec_shift, shared_w1, shared_w2, shared_gain, shared_shift, gate_w, tower_w1, tower_w2, tower_w3):
    weights = tuple((weight.astype(jnp.float32) for weight in (spec_w1, spec_w2, spec_gain, spec_shift, shared_w1, shared_w2, shared_gain, shared_shift, gate_w, tower_w1, tower_w2, tower_w3)))
    row_blocks = entries.reshape(N_DP, ENT_DEV, EMB)
    label_blocks = jnp.transpose(labels.reshape(TASKS, N_DP, EV_DEV), (1, 0, 2))

    def step_fn(totals, inputs):
        row_block, len_block, label_block = inputs
        segment_ids = jnp.repeat(jnp.arange(BAGS_DEV, dtype=jnp.int32), len_block, total_repeat_length=ENT_DEV)
        label_float = label_block.astype(jnp.float32)

        def block_fn(rows_float, *params):
            return block_loss(rows_float, label_float, segment_ids, *params)
        loss_total, back_fn, predictions = jax.vjp(block_fn, row_block.astype(jnp.float32), *weights, has_aux=True)
        gradients = back_fn(jnp.ones_like(loss_total))
        totals = tuple((running + fresh for running, fresh in zip(totals, gradients[1:])))
        return (totals, (predictions, gradients[0].astype(jnp.bfloat16)))
    start = tuple((jnp.zeros_like(weight) for weight in weights))
    totals, (predictions, row_grads) = lax.scan(step_fn, start, (row_blocks, lengths, label_blocks))
    predictions = jnp.transpose(predictions, (1, 0, 2)).reshape(TASKS, EVENTS)
    return (predictions, row_grads.reshape(ENTRIES, EMB), totals[0], totals[1], totals[2], totals[3], totals[4], totals[5], totals[6], totals[7], totals[8], totals[9], totals[10], totals[11])
```

```python
import functools

import jax
import jax.numpy as jnp
from jax import lax
from jax.experimental import pallas as pl
from jax.experimental.pallas import tpu as pltpu
from jax.sharding import PartitionSpec as P

EXPERTS = 2
GATES = 4
D = 512
HID = 256
TOWER1 = 128
TOWER2 = 64
EMB = 64
FEATS = 8
LANES = 128
BAGS = 128
EVB = BAGS // FEATS
ROWS = 128
EPSILON = 1e-05
K0 = 0.7978845608028654
K1 = K0 * 0.044715
SLOTS = 3
BF = jnp.bfloat16
F32 = jnp.float32
VMEM_BYTES = 56 * 1024 * 1024

GATE_AT = 0
T1_AT = GATE_AT + D
T2_AT = T1_AT + HID
MISC_AT = T2_AT + TOWER1
LABEL_AT = MISC_AT + 16
GT1_AT = 0
GT2_AT = HID
GG_AT = GT2_AT + TOWER1 // 2
GM_AT = GG_AT + 32
G_ROWS = GM_AT + 16


def nn(left, right):
    return jnp.dot(left, right, preferred_element_type=F32)


def nt(left, right):
    return lax.dot_general(left, right, (((1,), (1,)), ((), ())), preferred_element_type=F32)


def tn(left, right):
    return lax.dot_general(left, right, (((0,), (0,)), ((), ())), preferred_element_type=F32)


def params(**kwargs):
    return pltpu.CompilerParams(vmem_limit_bytes=VMEM_BYTES, **kwargs)


def cost(flops, moved):
    return pl.CostEstimate(flops=int(flops), bytes_accessed=int(moved), transcendentals=0)


VSPEC = pl.BlockSpec(memory_space=pltpu.VMEM)
SSPEC = pl.BlockSpec(memory_space=pltpu.SMEM)


def one_hot(starts, ends, base):
    row = lax.broadcasted_iota(jnp.int32, (ROWS, 2 * BAGS), 0)
    inside = (row >= starts - base) & (row < ends - base)
    return jnp.where(inside, 1.0, 0.0).astype(BF)


def window(ref, block):
    first = ref[pl.ds(block, 1), :]
    second = ref[pl.ds(block + 1, 1), :]
    return jnp.concatenate([first, second], axis=1)


def pool_kernel(blocks, half_blocks, chunks, first_ref, begin_ref, pos_ref, len_ref, ent_ref, x_ref, st_ref, en_ref, acc_ref):
    position = pos_ref[0]
    k = lax.broadcasted_iota(jnp.int32, (BAGS, BAGS), 0)
    j = lax.broadcasted_iota(jnp.int32, (BAGS, BAGS), 1)
    natural = (j % EVB) * FEATS + j // EVB
    before = jnp.where(k < natural, 1.0, 0.0).astype(BF)
    same = jnp.where(k == natural, 1.0, 0.0).astype(BF)
    lens_f = len_ref[...].astype(F32)
    lens = lens_f.astype(BF)
    in_block = nn(lens, before)
    own = nn(lens, same)
    sums = jnp.sum(lens_f, axis=1, keepdims=True)
    high = jnp.floor(sums * (1.0 / 128.0))
    low = sums - high * 128.0
    bi = lax.broadcasted_iota(jnp.int32, (blocks, blocks), 0)
    bj = lax.broadcasted_iota(jnp.int32, (blocks, blocks), 1)
    lower = jnp.where(bj < bi, 1.0, 0.0).astype(BF)
    offset = 128.0 * nn(lower, jnp.broadcast_to(high, (blocks, BAGS)).astype(BF)) + nn(
        lower, jnp.broadcast_to(low, (blocks, BAGS)).astype(BF)
    )
    starts = offset + in_block
    st_ref[pl.ds(0, blocks), :] = starts.astype(jnp.int32)
    en_ref[pl.ds(0, blocks), :] = (starts + own).astype(jnp.int32)
    past = jnp.full((8, BAGS), chunks * ROWS, jnp.int32)
    st_ref[pl.ds(blocks, 8), :] = past
    en_ref[pl.ds(blocks, 8), :] = past

    base_block = position * half_blocks

    def clear(i, carry):
        at = pl.multiple_of((base_block + i) * BAGS, BAGS)
        acc_ref[pl.ds(at, BAGS), :] = jnp.zeros((BAGS, EMB), F32)
        return carry

    lax.fori_loop(0, half_blocks, clear, 0, unroll=4)

    low_chunk = begin_ref[base_block] // ROWS
    high_chunk = (begin_ref[base_block + half_blocks] + ROWS - 1) // ROWS
    step = 4

    def chunk(i, carry):
        for u in range(step):
            c = low_chunk + i * step + u
            inside = jnp.minimum(c, chunks - 1)
            block = first_ref[inside]
            at = pl.multiple_of(inside * ROWS, ROWS)
            picked = one_hot(window(st_ref, block), window(en_ref, block), c * ROWS)
            part = tn(picked, ent_ref[pl.ds(at, ROWS), :])
            to = pl.multiple_of(block * BAGS, BAGS)
            acc_ref[pl.ds(to, 2 * BAGS), :] += part
        return carry

    lax.fori_loop(0, (high_chunk - low_chunk + step - 1) // step, chunk, 0)

    def place(i, carry):
        at = pl.multiple_of((base_block + i) * BAGS, BAGS)
        to = pl.multiple_of(i * EVB, EVB)
        block = acc_ref[pl.ds(at, BAGS), :]
        for pair in range(FEATS // 2):
            left = block[2 * pair * EVB : (2 * pair + 1) * EVB]
            right = block[(2 * pair + 1) * EVB : (2 * pair + 2) * EVB]
            x_ref[pl.ds(to, EVB), pair * 2 * EMB : (pair + 1) * 2 * EMB] = jnp.concatenate(
                [left, right], axis=1
            ).astype(BF)
        return carry

    lax.fori_loop(0, half_blocks, place, 0, unroll=4)


def pool(first, begin, position, lengths, entries):
    blocks = lengths.shape[0]
    half_blocks = blocks // 2
    chunks = entries.shape[0] // ROWS
    return pl.pallas_call(
        functools.partial(pool_kernel, blocks, half_blocks, chunks),
        out_shape=(
            jax.ShapeDtypeStruct((half_blocks * EVB, D), BF),
            jax.ShapeDtypeStruct((blocks + 8, BAGS), jnp.int32),
            jax.ShapeDtypeStruct((blocks + 8, BAGS), jnp.int32),
        ),
        in_specs=[SSPEC, SSPEC, SSPEC, VSPEC, VSPEC],
        out_specs=(VSPEC, VSPEC, VSPEC),
        scratch_shapes=[pltpu.VMEM(((blocks + 1) * BAGS, EMB), F32)],
        compiler_params=params(),
        cost_estimate=cost(2e9, 5e6),
    )(first, begin, position, lengths, entries)


def expand_kernel(half_blocks, group, first_ref, pos_ref, st_ref, en_ref, own_ref, other_ref, out_ref, rows_ref):
    position = pos_ref[0]
    step = pl.program_id(0)

    @pl.when(step == 0)
    def _():
        for source, half in ((own_ref, position), (other_ref, 1 - position)):

            def place(i, carry):
                at = pl.multiple_of(i * EVB, EVB)
                to = pl.multiple_of((half * half_blocks + i) * BAGS, BAGS)
                for pair in range(FEATS // 2):
                    tile = source[pl.ds(at, EVB), pair * 2 * EMB : (pair + 1) * 2 * EMB]
                    rows_ref[pl.ds(to + 2 * pair * EVB, EVB), :] = tile[:, :EMB]
                    rows_ref[pl.ds(to + (2 * pair + 1) * EVB, EVB), :] = tile[:, EMB:]
                return carry

            lax.fori_loop(0, half_blocks, place, 0, unroll=4)
        rows_ref[pl.ds(2 * half_blocks * BAGS, BAGS), :] = jnp.zeros((BAGS, EMB), BF)

    for u in range(group):
        c = step * group + u
        block = first_ref[c]
        picked = one_hot(window(st_ref, block), window(en_ref, block), c * ROWS)
        at = pl.multiple_of(block * BAGS, BAGS)
        out_ref[u * ROWS : (u + 1) * ROWS, :] = nn(picked, rows_ref[pl.ds(at, 2 * BAGS), :]).astype(BF)


def expand(first, position, starts, ends, own, other, rows):
    blocks = starts.shape[0] - 8
    chunks = rows // ROWS
    group = 8
    while chunks % group:
        group //= 2
    return pl.pallas_call(
        functools.partial(expand_kernel, blocks // 2, group),
        grid=(chunks // group,),
        out_shape=jax.ShapeDtypeStruct((rows, EMB), BF),
        in_specs=[SSPEC, SSPEC, VSPEC, VSPEC, VSPEC, VSPEC],
        out_specs=pl.BlockSpec((group * ROWS, EMB), lambda i: (i, 0)),
        scratch_shapes=[pltpu.VMEM(((blocks + 1) * BAGS, EMB), BF)],
        compiler_params=params(dimension_semantics=("arbitrary",)),
        cost_estimate=cost(4e9, 6e6),
    )(first, position, starts, ends, own, other)


def gelu_both(v):
    square = v * v
    half = 0.5 * jnp.tanh(v * (K1 * square + K0)) + 0.5
    act = v * half
    slope = half + act * (1.0 - half) * (6.0 * K1 * square + 2.0 * K0)
    return act, slope


def row_mean(value):
    return jnp.mean(value, axis=-1, keepdims=True)


def row_sum(value):
    return jnp.sum(value, axis=-1, keepdims=True)


def col_sum(value):
    return jnp.sum(value, axis=0, keepdims=True)


def wide(ref, row):
    return jnp.concatenate([ref[row : row + 1, :], ref[row + 1 : row + 2, :]], axis=1)


def main_kernel(
    events,
    size,
    pos_ref,
    x_ref,
    own1_ref,
    own2_ref,
    oth1_ref,
    oth2_ref,
    own_ref,
    oth_ref,
    pred_ref,
    dx_ref,
    g1own_ref,
    g2own_ref,
    g1oth_ref,
    g2oth_ref,
    sown_ref,
    soth_ref,
    h_ref,
    e_ref,
    f_ref,
    n_ref,
    y_ref,
    s1_ref,
    s2_ref,
    q_ref,
    u1_ref,
    e2_ref,
    e1_ref,
    dl_ref,
    acc_ref,
    acc3_ref,
):
    position = pos_ref[0]
    first = (own1_ref, oth1_ref)
    second = (own2_ref, oth2_ref)
    packs = (own_ref, oth_ref)
    misc = [ref[MISC_AT : MISC_AT + 16, :].astype(F32) for ref in packs]
    gains = [[wide(misc[t], 2 * s) for s in range(SLOTS)] for t in range(2)]
    shifts = [[wide(misc[t], 2 * SLOTS + 2 * s) for s in range(SLOTS)] for t in range(2)]
    thirds = [misc[t][12:13, :] for t in range(2)]
    lane = lax.broadcasted_iota(jnp.int32, (size, LANES), 1)
    eye = (
        lax.broadcasted_iota(jnp.int32, (LANES, LANES), 0)
        == lax.broadcasted_iota(jnp.int32, (LANES, LANES), 1)
    ).astype(F32)
    acc_ref[...] = jnp.zeros_like(acc_ref)
    acc3_ref[...] = jnp.zeros_like(acc3_ref)
    tiles = size // LANES
    half_tiles = events // LANES

    def block(i, carry):
        at = pl.multiple_of(i * size, size)
        here = pl.ds(at, size)
        x = x_ref[here, :]
        for t in range(2):
            for s in range(SLOTS):
                m = t * SLOTS + s
                act, slope = gelu_both(nn(x, first[t][s]))
                s1_ref[m] = slope
                hidden = act.astype(BF)
                h_ref[m, here, :] = hidden
                act, slope = gelu_both(nn(hidden, second[t][s]))
                centred = act - row_mean(act)
                scale = lax.rsqrt(row_mean(centred * centred) + EPSILON)
                normed = centred * scale
                n_ref[m] = normed
                s2_ref[m] = slope * scale
                out = normed * gains[t][s] + shifts[t][s]
                if s == SLOTS - 1:
                    out = out.astype(BF).astype(F32)
                y_ref[m] = out
        mix_grads, probs = [], []
        dx = jnp.zeros((size, D), F32)
        for t in range(2):
            order = (t * SLOTS, t * SLOTS + 1, t * SLOTS + 2, (1 - t) * SLOTS + 2)
            pack = packs[t]
            gate = pack[GATE_AT : GATE_AT + D, :]
            t1 = pack[T1_AT : T1_AT + HID, :]
            t2 = pack[T2_AT : T2_AT + TOWER1, :]
            logits = jnp.where(lane < GATES, nn(x, gate), -1e30)
            raised = jnp.exp(logits - jnp.max(logits, axis=-1, keepdims=True))
            prob = raised / row_sum(raised)
            cols = [prob[:, k : k + 1] for k in range(GATES)]
            mixture = cols[0] * y_ref[order[0]]
            for k in range(1, GATES):
                mixture = mixture + cols[k] * y_ref[order[k]]
            q = mixture.astype(BF)
            q_ref[t, here, :] = q
            act, slope3 = gelu_both(nn(q, t1))
            u1 = act.astype(BF)
            u1_ref[t, here, :] = u1
            act, slope4 = gelu_both(nn(u1, t2))
            u2 = act.astype(BF).astype(F32)
            logit = row_sum(u2 * thirds[t])
            prediction = 1.0 / (1.0 + jnp.exp(-logit))
            label_cols = []
            for b in range(tiles):
                row = pack[pl.ds(LABEL_AT, 16), :].astype(F32)
                wanted = position * half_tiles + i * tiles + b
                pick = lax.broadcasted_iota(jnp.int32, (16, LANES), 0) == wanted
                line = col_sum(jnp.where(pick, row, 0.0))
                label_cols.append(row_sum(eye * line))
                part = prediction[b * LANES : (b + 1) * LANES]
                pred_ref[t, pl.ds(i * tiles + b, 1), :] = col_sum(eye * part)
            label = jnp.concatenate(label_cols, axis=0)
            d_logit = prediction - label
            acc3_ref[t : t + 1, :] += col_sum(d_logit * u2)
            e2 = (slope4 * (d_logit * thirds[t])).astype(BF)
            e2_ref[t, here, :] = e2
            e1 = (slope3 * nt(e2, t2)).astype(BF)
            e1_ref[t, here, :] = e1
            d_mix = nt(e1, t1)
            d_prob = [row_sum(d_mix * y_ref[order[k]]) for k in range(GATES)]
            weighted = cols[0] * d_prob[0]
            for k in range(1, GATES):
                weighted = weighted + cols[k] * d_prob[k]
            d_gate = jnp.zeros((size, LANES), F32)
            for k in range(GATES):
                d_gate = jnp.where(lane == k, cols[k] * (d_prob[k] - weighted), d_gate)
            d_gate = d_gate.astype(BF)
            dl_ref[t, here, :] = d_gate
            dx = dx + nt(d_gate, gate)
            mix_grads.append(d_mix)
            probs.append(cols)
        for t in range(2):
            for s in range(SLOTS):
                m = t * SLOTS + s
                up = probs[t][s] * mix_grads[t]
                if s == SLOTS - 1:
                    up = up + probs[1 - t][SLOTS] * mix_grads[1 - t]
                normed = n_ref[m]
                up_normed = up * normed
                acc_ref[m : m + 1, :] += col_sum(up_normed)
                acc_ref[8 + m : 9 + m, :] += col_sum(up)
                d_normed = up * gains[t][s]
                mean_one = row_mean(d_normed)
                mean_two = row_mean(up_normed * gains[t][s])
                e = (s2_ref[m] * (d_normed - mean_one - normed * mean_two)).astype(BF)
                e_ref[m, here, :] = e
                f = (s1_ref[m] * nt(e, second[t][s])).astype(BF)
                f_ref[m, here, :] = f
                dx = dx + nt(f, first[t][s])
        dx_ref[here, :] = dx.astype(BF)
        return carry

    lax.fori_loop(0, events // size, block, 0)

    x = x_ref[...]
    for t, (g1_ref, g2_ref, small_ref) in enumerate(
        ((g1own_ref, g2own_ref, sown_ref), (g1oth_ref, g2oth_ref, soth_ref))
    ):
        for s in range(SLOTS):
            m = t * SLOTS + s
            g2_ref[s] = tn(h_ref[m], e_ref[m]).astype(BF)
            g1_ref[s] = tn(x, f_ref[m]).astype(BF)
        small_ref[GT1_AT : GT1_AT + HID, :] = tn(q_ref[t], e1_ref[t]).astype(BF)
        grad2 = tn(u1_ref[t], e2_ref[t])
        half = TOWER1 // 2
        lanes = lax.broadcasted_iota(jnp.int32, (half, LANES), 1)
        small_ref[GT2_AT : GT2_AT + half, :] = jnp.where(
            lanes < TOWER2, grad2[:half], pltpu.roll(grad2[half:], TOWER2, 1)
        ).astype(BF)
        gate_grad = tn(dl_ref[t], x)[:8]
        for k in range(D // LANES):
            small_ref[GG_AT + 8 * k : GG_AT + 8 * (k + 1), :] = gate_grad[
                :, k * LANES : (k + 1) * LANES
            ].astype(BF)
        lines = []
        for kind in range(2):
            for s in range(SLOTS):
                m = 8 * kind + t * SLOTS + s
                for part in range(2):
                    lines.append(acc_ref[m : m + 1, part * LANES : (part + 1) * LANES])
        lines.append(acc3_ref[t : t + 1, :])
        lines.append(jnp.zeros((3, LANES), F32))
        small_ref[GM_AT : GM_AT + 16, :] = jnp.concatenate(lines, axis=0).astype(BF)


def layer(position, x, own1, own2, oth1, oth2, own_pack, oth_pack):
    events = x.shape[0]
    size = 128
    big = 2 * SLOTS
    grads1 = jax.ShapeDtypeStruct((SLOTS, D, HID), BF)
    grads2 = jax.ShapeDtypeStruct((SLOTS, HID, HID), BF)
    small = jax.ShapeDtypeStruct((G_ROWS, LANES), BF)
    return pl.pallas_call(
        functools.partial(main_kernel, events, size),
        out_shape=(
            jax.ShapeDtypeStruct((2, events // LANES, LANES), F32),
            jax.ShapeDtypeStruct((events, D), BF),
            grads1,
            grads2,
            grads1,
            grads2,
            small,
            small,
        ),
        in_specs=[SSPEC] + [VSPEC] * 7,
        out_specs=(VSPEC,) * 8,
        scratch_shapes=[
            pltpu.VMEM((big, events, HID), BF),
            pltpu.VMEM((big, events, HID), BF),
            pltpu.VMEM((big, events, HID), BF),
            pltpu.VMEM((big, size, HID), F32),
            pltpu.VMEM((big, size, HID), F32),
            pltpu.VMEM((big, size, HID), F32),
            pltpu.VMEM((big, size, HID), F32),
            pltpu.VMEM((2, events, HID), BF),
            pltpu.VMEM((2, events, TOWER1), BF),
            pltpu.VMEM((2, events, LANES), BF),
            pltpu.VMEM((2, events, TOWER1), BF),
            pltpu.VMEM((2, events, LANES), BF),
            pltpu.VMEM((16, HID), F32),
            pltpu.VMEM((8, LANES), F32),
        ],
        compiler_params=params(),
        cost_estimate=cost(events * big * 196608 * 6, 10e6),
    )(position, x, own1, own2, oth1, oth2, own_pack, oth_pack)


def sibling(value):
    return lax.ppermute(value, "task", [(0, 1), (1, 0)])


def flipped(value, mask):
    pairs = [(i, i ^ mask) for i in range(lax.axis_size("dp"))]
    return lax.ppermute(value, "dp", pairs)


def crossed(value, masks):
    n = lax.axis_size("dp")
    pairs = [(t * n + i, t * n + (i ^ masks[t])) for t in range(2) for i in range(n)]
    return lax.ppermute(value, ("task", "dp"), pairs)


def assemble_kernel(rows1, rows2, at_ref, *refs):
    pieces, (w1_ref, w2_ref) = refs[:-2], refs[-2:]
    for p, piece in enumerate(pieces):
        d = at_ref[p]
        for s in range(SLOTS):
            w1_ref[s, pl.ds(pl.multiple_of(d * rows1, rows1), rows1), :] = piece[s * rows1 : (s + 1) * rows1, :]
            low = SLOTS * rows1 + s * rows2
            w2_ref[s, pl.ds(pl.multiple_of(d * rows2, rows2), rows2), :] = piece[low : low + rows2, :]


def gather_weights(pack, rows1, rows2, me, position):
    n = lax.axis_size("dp")
    if rows2 % 16 or n < 4:
        every = lax.all_gather(pack, "dp", axis=0)
        cut = SLOTS * rows1
        w1 = every[:, :cut].reshape(n, SLOTS, rows1, HID).swapaxes(0, 1).reshape(SLOTS, D, HID)
        w2 = every[:, cut:].reshape(n, SLOTS, rows2, HID).swapaxes(0, 1).reshape(SLOTS, HID, HID)
        return w1, w2
    far = [pack] + [flipped(pack, 4 * k) for k in range(1, n // 4)]
    mid = [crossed(piece, (1, 2)) for piece in far]
    near = [crossed(piece, (2, 1)) for piece in far + mid]
    pieces = far + mid + near
    one, two = 1 + position, 2 - position
    at = [me ^ (4 * k) for k in range(n // 4)]
    at = at + [d ^ one for d in at]
    at = at + [d ^ two for d in at]
    return pl.pallas_call(
        functools.partial(assemble_kernel, rows1, rows2),
        out_shape=(
            jax.ShapeDtypeStruct((SLOTS, D, HID), BF),
            jax.ShapeDtypeStruct((SLOTS, HID, HID), BF),
        ),
        in_specs=[SSPEC] + [VSPEC] * n,
        out_specs=(VSPEC, VSPEC),
        compiler_params=params(),
        cost_estimate=cost(0, 3e6),
    )(jnp.stack(at), *pieces)


def sort_kernel(n, rows1, rows2, at_ref, a1_ref, a2_ref, b1_ref, b2_ref, keep_ref, send_ref):
    quarter = n // 4
    for p in range(n):
        out = keep_ref if p < n // 2 else send_ref
        q = p % (n // 2)
        d = at_ref[p]
        one = pl.ds(pl.multiple_of(d * rows1, rows1), rows1)
        two = pl.ds(pl.multiple_of(d * rows2, rows2), rows2)
        for s in range(SLOTS):
            total = a1_ref[s, one, :].astype(F32) + b1_ref[s, one, :].astype(F32)
            out[q // quarter, q % quarter, s * rows1 : (s + 1) * rows1, :] = total.astype(BF)
            total = a2_ref[s, two, :].astype(F32) + b2_ref[s, two, :].astype(F32)
            low = SLOTS * rows1 + s * rows2
            out[q // quarter, q % quarter, low : low + rows2, :] = total.astype(BF)


def added(one, two):
    return one.astype(F32) + two.astype(F32)


def scatter_grads(own1, own2, got1, got2, small, rows1, rows2, me, position):
    n = lax.axis_size("dp")
    if rows2 % 16 or n < 4:
        g1 = lax.psum_scatter(added(own1, got1), "dp", scatter_dimension=1, tiled=True)
        g2 = lax.psum_scatter(added(own2, got2), "dp", scatter_dimension=1, tiled=True)
        return g1, g2, lax.psum(small, "dp")
    quarter = n // 4
    one, two = 1 + position, 2 - position
    at = [me ^ (4 * k) for k in range(quarter)]
    at = at + [d ^ two for d in at]
    at = at + [d ^ one for d in at]
    rows = SLOTS * (rows1 + rows2)
    half = jax.ShapeDtypeStruct((2, quarter, rows, HID), BF)
    keep, send = pl.pallas_call(
        functools.partial(sort_kernel, n, rows1, rows2),
        out_shape=(half, half),
        in_specs=[SSPEC] + [VSPEC] * 4,
        out_specs=(VSPEC, VSPEC),
        compiler_params=params(),
        cost_estimate=cost(0, 5e6),
    )(jnp.stack(at), own1, own2, got1, got2)
    small = small.astype(BF)
    small = added(small, crossed(small, (1, 2))).astype(BF)
    total = added(keep, crossed(send, (1, 2))).astype(BF)
    small = added(small, crossed(small, (2, 1))).astype(BF)
    total = added(total[0], crossed(total[1], (2, 1))).astype(BF)
    mine, tiny = total[0].astype(F32), small.astype(F32)
    for k in range(1, quarter):
        tiny = tiny + flipped(small, 4 * k).astype(F32)
        mine = mine + flipped(total[k], 4 * k).astype(F32)
    cut = SLOTS * rows1
    return mine[:cut].reshape(SLOTS, rows1, HID), mine[cut:].reshape(SLOTS, rows2, HID), tiny


def swap_shared(gate, position):
    return jnp.where(position == 0, gate, gate[:, jnp.array([0, 1, 3, 2])])


def pack_small(labels, spec_gain, spec_shift, shared_gain, shared_shift, gate_w, tower_w1, tower_w2, tower_w3, position):
    gate = jnp.pad(swap_shared(gate_w[0], position), ((0, 0), (0, LANES - GATES)))
    second = jnp.pad(tower_w2[0], ((0, 0), (0, LANES - TOWER2)))
    third = jnp.pad(tower_w3, ((0, 3), (0, LANES - TOWER2)))
    lines = [
        part.reshape(-1, LANES)
        for part in (spec_gain[0], shared_gain[0], spec_shift[0], shared_shift[0])
    ]
    label = labels[0].astype(BF).reshape(-1, LANES)
    label = jnp.pad(label, ((0, 16 - label.shape[0]), (0, 0)))
    return jnp.concatenate([gate, tower_w1[0], second, *lines, third, label], axis=0)


def per_device(
    entries,
    lengths,
    labels,
    spec_w1,
    spec_w2,
    spec_gain,
    spec_shift,
    shared_w1,
    shared_w2,
    shared_gain,
    shared_shift,
    gate_w,
    tower_w1,
    tower_w2,
    tower_w3,
):
    position = lax.axis_index("task")
    me = lax.axis_index("dp")
    pos = position.reshape(1)
    rows1, rows2 = spec_w1.shape[2], spec_w2.shape[2]
    pack = jnp.concatenate(
        [part.reshape(-1, HID) for part in (spec_w1, shared_w1, spec_w2, shared_w2)], axis=0
    )
    small = pack_small(
        labels, spec_gain, spec_shift, shared_gain, shared_shift, gate_w, tower_w1, tower_w2, tower_w3, position
    )
    other_small = sibling(small)

    blocked = lengths.reshape(-1, BAGS)
    chunks = entries.shape[0] // ROWS
    ends = jnp.cumsum(jnp.sum(blocked, axis=1))
    begin = jnp.concatenate([jnp.zeros((1,), jnp.int32), ends])
    tops = jnp.arange(chunks, dtype=jnp.int32)[:, None] * ROWS
    first = jnp.sum((ends[None, :] <= tops).astype(jnp.int32), axis=1)
    x, starts, stops = pool(first, begin, pos, blocked, entries)

    own1, own2 = gather_weights(pack, rows1, rows2, me, position)
    oth1, oth2 = sibling(own1), sibling(own2)
    pred, dx, g1, g2, h1, h2, sown, soth = layer(pos, x, own1, own2, oth1, oth2, small, other_small)

    got1, got2, got_small = sibling(h1), sibling(h2), sibling(soth)
    w1_grad, w2_grad, tiny = scatter_grads(
        g1, g2, got1, got2, added(sown, got_small), rows1, rows2, me, position
    )
    entry_grads = expand(first, pos, starts, stops, dx, sibling(dx), entries.shape[0])

    mine = pred[0].reshape(-1)
    theirs = sibling(pred[1]).reshape(-1)
    predictions = jnp.where(
        position == 0, jnp.concatenate([mine, theirs]), jnp.concatenate([theirs, mine])
    )[None]

    t1 = tiny[GT1_AT : GT1_AT + HID]
    half = tiny[GT2_AT : GT2_AT + TOWER1 // 2]
    t2 = jnp.concatenate([half[:, :TOWER2], half[:, TOWER2:]], axis=0)
    gate = tiny[GG_AT : GG_AT + 32].reshape(D // LANES, 8, LANES)[:, :GATES]
    gate = swap_shared(gate.transpose(0, 2, 1).reshape(D, GATES), position)
    misc = tiny[GM_AT : GM_AT + 12].reshape(2, SLOTS, HID)
    t3 = tiny[GM_AT + 12 : GM_AT + 13, :TOWER2]
    return (
        predictions,
        entry_grads,
        w1_grad[None, :EXPERTS],
        w2_grad[None, :EXPERTS],
        misc[0, :EXPERTS][None],
        misc[1, :EXPERTS][None],
        w1_grad[EXPERTS:],
        w2_grad[EXPERTS:],
        misc[0, EXPERTS:],
        misc[1, EXPERTS:],
        gate[None],
        t1[None],
        t2[None],
        t3,
    )


def solution(mesh):
    placed = (
        P("dp", None),
        P("dp", None),
        P("task", "dp"),
        P("task", None, "dp", None),
        P("task", None, "dp", None),
        P("task", None, None),
        P("task", None, None),
        P("task", "dp", None),
        P("task", "dp", None),
        P("task", None),
        P("task", None),
        P("task", None, None),
        P("task", None, None),
        P("task", None, None),
        P("task", None),
    )
    return jax.shard_map(
        per_device,
        mesh=mesh,
        in_specs=placed,
        out_specs=(
            P("task", "dp"),
            P("dp", None),
            P("task", None, "dp", None),
            P("task", None, "dp", None),
            P("task", None, None),
            P("task", None, None),
            P("task", "dp", None),
            P("task", "dp", None),
            P("task", None),
            P("task", None),
            P("task", None, None),
            P("task", None, None),
            P("task", None, None),
            P("task", None),
        ),
        check_vma=False,
    )
```

```python
import functools

import jax
import jax.numpy as jnp
from jax import lax
from jax.experimental import pallas as pl
from jax.experimental.pallas import tpu as pltpu
from jax.sharding import PartitionSpec as P

EXPERTS = 2
GATES = 4
D = 512
HID = 256
TOWER1 = 128
TOWER2 = 64
EMB = 64
FEATS = 8
LANES = 128
BAGS = 128
EVB = BAGS // FEATS
ROWS = 128
EPSILON = 1e-05
K0 = 0.7978845608028654
K1 = K0 * 0.044715
SLOTS = 3
BIG = 2 * SLOTS
WIDE = BIG * HID
BF = jnp.bfloat16
F32 = jnp.float32
VMEM_BYTES = 56 * 1024 * 1024

T1_AT = 0
T2_AT = T1_AT + HID
GATE_AT = T2_AT + TOWER2
MISC_AT = GATE_AT + GATES * (D // LANES)
LABEL_AT = MISC_AT + 16
G_ROWS = LABEL_AT


def nn(left, right):
    return jnp.dot(left, right, preferred_element_type=F32)


def nt(left, right):
    return lax.dot_general(left, right, (((1,), (1,)), ((), ())), preferred_element_type=F32)


def tn(left, right):
    return lax.dot_general(left, right, (((0,), (0,)), ((), ())), preferred_element_type=F32)


def params(**kwargs):
    return pltpu.CompilerParams(vmem_limit_bytes=VMEM_BYTES, **kwargs)


def cost(flops, moved):
    return pl.CostEstimate(flops=int(flops), bytes_accessed=int(moved), transcendentals=0)


def shape(dims, kind=BF):
    return jax.ShapeDtypeStruct(dims, kind)


VSPEC = pl.BlockSpec(memory_space=pltpu.VMEM)
SSPEC = pl.BlockSpec(memory_space=pltpu.SMEM)
ASPEC = pl.BlockSpec(memory_space=pl.ANY)


def line(ref, row):
    both = ref[row : row + 1, :].astype(F32)
    return [both[:, :LANES], both[:, LANES:]]


def prep_kernel(
    blocks,
    chunks,
    pos_ref,
    len_ref,
    label_ref,
    sgain_ref,
    sshift_ref,
    ogain_ref,
    oshift_ref,
    gate_ref,
    t1_ref,
    t2_ref,
    t3_ref,
    st_ref,
    en_ref,
    meta_ref,
    small_ref,
):
    k = lax.broadcasted_iota(jnp.int32, (BAGS, BAGS), 0)
    j = lax.broadcasted_iota(jnp.int32, (BAGS, BAGS), 1)
    natural = (j % EVB) * FEATS + j // EVB
    before = jnp.where(k < natural, 1.0, 0.0).astype(BF)
    same = jnp.where(k == natural, 1.0, 0.0).astype(BF)
    lens_f = jnp.concatenate(
        [len_ref[:, b * BAGS : (b + 1) * BAGS] for b in range(blocks)], axis=0
    ).astype(F32)
    lens = lens_f.astype(BF)
    in_block = nn(lens, before)
    own = nn(lens, same)
    sums = jnp.sum(lens_f, axis=1, keepdims=True)
    high = jnp.floor(sums * (1.0 / 128.0))
    low = sums - high * 128.0
    bi = lax.broadcasted_iota(jnp.int32, (blocks, blocks), 0)
    bj = lax.broadcasted_iota(jnp.int32, (blocks, blocks), 1)
    lower = jnp.where(bj < bi, 1.0, 0.0).astype(BF)
    offset = 128.0 * nn(lower, jnp.broadcast_to(high, (blocks, BAGS)).astype(BF)) + nn(
        lower, jnp.broadcast_to(low, (blocks, BAGS)).astype(BF)
    )
    starts = offset + in_block
    st_ref[pl.ds(0, blocks), :] = starts.astype(jnp.int32)
    en_ref[pl.ds(0, blocks), :] = (starts + own).astype(jnp.int32)
    past = jnp.full((8, BAGS), chunks * ROWS, jnp.int32)
    st_ref[pl.ds(blocks, 8), :] = past
    en_ref[pl.ds(blocks, 8), :] = past
    lanes = meta_ref.shape[1]
    begins = jnp.concatenate([offset] * (lanes // BAGS), axis=1)
    row = lax.broadcasted_iota(jnp.int32, (blocks, lanes), 0)
    col = lax.broadcasted_iota(jnp.int32, (blocks, lanes), 1)
    begin = jnp.sum(jnp.where(row == col, begins, 0.0), axis=0, keepdims=True)
    spot = lax.broadcasted_iota(jnp.int32, (1, lanes), 1)
    begin = jnp.where(spot >= blocks, float(chunks * ROWS), begin)
    reached = jnp.where(begins <= (col * ROWS).astype(F32), 1.0, 0.0)
    first = jnp.sum(reached, axis=0, keepdims=True) - 1.0
    meta_ref[0:1, :] = begin.astype(jnp.int32)
    meta_ref[1:2, :] = first.astype(jnp.int32)
    small_ref[T1_AT : T1_AT + HID, :] = t1_ref[...]
    small_ref[T2_AT : T2_AT + TOWER2, :] = t2_ref[...]
    gate = gate_ref[...].astype(F32)
    turned = jnp.concatenate([gate[0:2], gate[3:4], gate[2:3]], axis=0)
    gate = jnp.where(pos_ref[0] == 0, gate, turned)
    lines = [gate[g : g + 1, p * LANES : (p + 1) * LANES] for g in range(GATES) for p in range(D // LANES)]
    lines += line(sgain_ref, 0) + line(sgain_ref, 1) + line(ogain_ref, 0)
    lines += line(sshift_ref, 0) + line(sshift_ref, 1) + line(oshift_ref, 0)
    lines += [jnp.concatenate([t3_ref[...].astype(F32)] * 2, axis=1), jnp.zeros((3, LANES), F32)]
    events = label_ref.shape[1]
    lines += [label_ref[:, p * LANES : (p + 1) * LANES].astype(F32) for p in range(events // LANES)]
    lines += [jnp.zeros((16 - events // LANES, LANES), F32)]
    small_ref[pl.ds(GATE_AT, 48), :] = jnp.concatenate(lines, axis=0).astype(BF)


def prepare(pos, lengths, labels, spec_gain, spec_shift, shared_gain, shared_shift, gate, t1, t2, t3, chunks):
    blocks = lengths.shape[1] // BAGS
    lanes = -(-max(blocks + 1, chunks) // LANES) * LANES
    return pl.pallas_call(
        functools.partial(prep_kernel, blocks, chunks),
        out_shape=(
            shape((blocks + 8, BAGS), jnp.int32),
            shape((blocks + 8, BAGS), jnp.int32),
            shape((2, lanes), jnp.int32),
            shape((LABEL_AT + 16, LANES)),
        ),
        in_specs=[SSPEC] + [VSPEC] * 10,
        out_specs=(VSPEC,) * 4,
        compiler_params=params(),
        cost_estimate=cost(1e9, 1e6),
    )(pos, lengths, labels, spec_gain, spec_shift, shared_gain, shared_shift, gate, t1, t2, t3)


def one_hot(starts, ends, base):
    row = lax.broadcasted_iota(jnp.int32, (ROWS, 2 * BAGS), 0)
    inside = (row >= starts - base) & (row < ends - base)
    return jnp.where(inside, 1.0, 0.0).astype(BF)


def window(ref, block):
    first = ref[pl.ds(block, 1), :]
    second = ref[pl.ds(block + 1, 1), :]
    return jnp.concatenate([first, second], axis=1)


def pool_kernel(skip, count, half_blocks, chunks, pos_ref, meta_ref, st_ref, en_ref, ent_ref, x_ref, acc_ref):
    base_block = pos_ref[0] * half_blocks + skip

    def clear(i, carry):
        at = pl.multiple_of((base_block + i) * BAGS, BAGS)
        acc_ref[:, pl.ds(at, BAGS)] = jnp.zeros((EMB, BAGS), F32)
        return carry

    lax.fori_loop(0, count, clear, 0, unroll=4)

    low_chunk = meta_ref[0, base_block] // ROWS
    high_chunk = (meta_ref[0, base_block + count] + ROWS - 1) // ROWS
    step = 4

    def chunk(i, carry):
        for u in range(step):
            c = low_chunk + i * step + u
            inside = jnp.minimum(c, chunks - 1)
            block = meta_ref[1, inside]
            at = pl.multiple_of(inside * ROWS, ROWS)
            picked = one_hot(window(st_ref, block), window(en_ref, block), c * ROWS)
            part = nn(ent_ref[:, pl.ds(at, ROWS)], picked)
            to = pl.multiple_of(block * BAGS, BAGS)
            acc_ref[:, pl.ds(to, 2 * BAGS)] += part
        return carry

    lax.fori_loop(0, (high_chunk - low_chunk + step - 1) // step, chunk, 0)

    def place(i, carry):
        at = pl.multiple_of((base_block + i) * BAGS, BAGS)
        to = pl.multiple_of(i * EVB, EVB)
        block = acc_ref[:, pl.ds(at, BAGS)].T
        for pair in range(FEATS // 2):
            left = block[2 * pair * EVB : (2 * pair + 1) * EVB]
            right = block[(2 * pair + 1) * EVB : (2 * pair + 2) * EVB]
            x_ref[pl.ds(to, EVB), pair * 2 * EMB : (pair + 1) * 2 * EMB] = jnp.concatenate(
                [left, right], axis=1
            ).astype(BF)
        return carry

    lax.fori_loop(0, count, place, 0, unroll=4)


def pool(part, parts, pos, meta, starts, ends, entries):
    blocks = starts.shape[0] - 8
    half_blocks = blocks // 2
    count = half_blocks // parts
    chunks = entries.shape[1] // ROWS
    return pl.pallas_call(
        functools.partial(pool_kernel, part * count, count, half_blocks, chunks),
        out_shape=shape((count * EVB, D)),
        in_specs=[SSPEC, SSPEC, VSPEC, VSPEC, VSPEC],
        out_specs=VSPEC,
        scratch_shapes=[pltpu.VMEM((EMB, (blocks + 1) * BAGS), F32)],
        compiler_params=params(),
        cost_estimate=cost(4e9, 5e6),
    )(pos, meta, starts, ends, entries)


def expand_kernel(half_blocks, group, pos_ref, meta_ref, st_ref, en_ref, own_ref, other_ref, out_ref, rows_ref):
    position = pos_ref[0]
    step = pl.program_id(0)

    @pl.when(step == 0)
    def _():
        for source, half in ((own_ref, position), (other_ref, 1 - position)):

            def place(i, carry):
                at = pl.multiple_of(i * EVB, EVB)
                to = pl.multiple_of((half * half_blocks + i) * BAGS, BAGS)
                parts = []
                for pair in range(FEATS // 2):
                    tile = source[pl.ds(at, EVB), pair * 2 * EMB : (pair + 1) * 2 * EMB]
                    parts += [tile[:, :EMB], tile[:, EMB:]]
                rows_ref[:, pl.ds(to, BAGS)] = jnp.concatenate(parts, axis=0).T
                return carry

            lax.fori_loop(0, half_blocks, place, 0, unroll=4)
        rows_ref[:, pl.ds(2 * half_blocks * BAGS, BAGS)] = jnp.zeros((EMB, BAGS), BF)

    for u in range(group):
        c = step * group + u
        block = meta_ref[1, c]
        picked = one_hot(window(st_ref, block), window(en_ref, block), c * ROWS)
        at = pl.multiple_of(block * BAGS, BAGS)
        out_ref[:, u * ROWS : (u + 1) * ROWS] = nt(rows_ref[:, pl.ds(at, 2 * BAGS)], picked).astype(BF)


def expand(pos, meta, starts, ends, own, other, rows):
    blocks = starts.shape[0] - 8
    chunks = rows // ROWS
    group = 16
    while chunks % group:
        group //= 2
    return pl.pallas_call(
        functools.partial(expand_kernel, blocks // 2, group),
        grid=(chunks // group,),
        out_shape=shape((EMB, rows)),
        in_specs=[SSPEC, SSPEC, VSPEC, VSPEC, VSPEC, VSPEC],
        out_specs=pl.BlockSpec((EMB, group * ROWS), lambda i: (0, i)),
        scratch_shapes=[pltpu.VMEM((EMB, (blocks + 1) * BAGS), BF)],
        compiler_params=params(dimension_semantics=("arbitrary",)),
        cost_estimate=cost(8e9, 6e6),
    )(pos, meta, starts, ends, own, other)


def gelu_both(v):
    square = v * v
    half = 0.5 * jnp.tanh(v * (K1 * square + K0)) + 0.5
    act = v * half
    slope = half + act * (1.0 - half) * (6.0 * K1 * square + 2.0 * K0)
    return act, slope


def col_sum(value):
    return jnp.sum(value, axis=0, keepdims=True)


def lane_tiles(events, body):
    def step(j, carry):
        body(j, pl.ds(pl.multiple_of(j * LANES, LANES), LANES))
        return carry

    lax.fori_loop(0, events // LANES, step, 0)


def main_kernel(xs, groups, outs, rows1, rows2, pos_ref, at_ref, *refs):
    refs = list(refs)
    take = lambda n: [refs.pop(0) for _ in range(n)]
    x_parts = take(xs)
    own_groups, oth_groups = take(groups), take(groups)
    packs = take(2)
    pred_ref, dx_ref = take(2)
    own_outs, oth_outs = take(outs), take(outs)
    smalls = take(2)
    x_ref, wc_ref, w2_ref, gain_ref, third_ref, lab_ref, pc_ref, pb_ref, s2_ref, y_ref, h_ref, e_ref, fc_ref = take(13)
    lg_ref, prob_ref, q_ref, pt_ref, u1_ref, p4_ref, e2_ref, e1_ref, du_ref, dm_ref, dmb_ref, acc_ref, acc3_ref, g_ref = take(14)
    position = pos_ref[0]
    events = x_ref.shape[1]

    def part(m):
        return slice(m * HID, (m + 1) * HID)

    size = events // xs
    for k, piece in enumerate(x_parts):
        x_ref[:, k * size : (k + 1) * size] = piece[...].T
    for t, whole in enumerate((own_groups, oth_groups)):
        p = 0
        for group in whole:
            for g in range(group.shape[0]):
                d = at_ref[t, p]
                p += 1
                one = pl.ds(pl.multiple_of(d * rows1, rows1), rows1)
                two = pl.ds(pl.multiple_of(d * rows2, rows2), rows2)
                for s in range(SLOTS):
                    wc_ref[one, part(t * SLOTS + s)] = group[g, s * rows1 : (s + 1) * rows1, :]
                    low = SLOTS * rows1 + s * rows2
                    w2_ref[t * SLOTS + s, two, :] = group[g, low : low + rows2, :]
    lines = []
    for t in range(2):
        block = packs[t][GATE_AT : GATE_AT + 16, :].astype(F32)
        for g in range(GATES):
            lines.append(
                jnp.concatenate([block[4 * g + p : 4 * g + p + 1, :] for p in range(D // LANES)], axis=1)
            )
        lines.append(jnp.zeros((8 - GATES, D), F32))
    gates = jnp.concatenate(lines, axis=0).astype(BF)
    wc_ref[:, WIDE:] = jnp.concatenate([gates, jnp.zeros((LANES - 16, D), BF)], axis=0).T
    fc_ref[WIDE:, :] = jnp.zeros((LANES, events), BF)
    acc_ref[...] = jnp.zeros_like(acc_ref)
    acc3_ref[...] = jnp.zeros_like(acc3_ref)
    for t in range(2):
        misc = packs[t][MISC_AT : MISC_AT + 16, :].astype(F32)
        for s in range(SLOTS):
            for kind in range(2):
                for half in range(2):
                    at = 2 * (kind * SLOTS + s) + half
                    to = ((kind * 2 + t) * SLOTS + s) * HID + half * LANES
                    gain_ref[to : to + LANES, :] = jnp.broadcast_to(misc[at : at + 1, :], (LANES, LANES)).T
        third = jnp.broadcast_to(misc[12:13, :], (LANES, LANES)).T
        third_ref[t * TOWER2 : (t + 1) * TOWER2, :] = third[:TOWER2]
        lab_ref[t * 16 : (t + 1) * 16, :] = packs[t][LABEL_AT : LABEL_AT + 16, :].astype(F32)

    for m in range(BIG):
        pc_ref[part(m), :] = tn(wc_ref[:, part(m)], x_ref[...])
    lg_ref[...] = nn(gates, x_ref[...])

    def first_gelu(j, here):
        for m in range(BIG):
            act, slope = gelu_both(pc_ref[part(m), here])
            pc_ref[part(m), here] = slope
            h_ref[part(m), here] = act.astype(BF)

    lane_tiles(events, first_gelu)
    for m in range(BIG):
        pb_ref[part(m), :] = tn(w2_ref[m], h_ref[part(m), :])

    def second_gelu(j, here):
        for m in range(BIG):
            act, slope = gelu_both(pb_ref[part(m), here])
            centred = act - col_sum(act) * (1.0 / HID)
            scale = lax.rsqrt(col_sum(centred * centred) * (1.0 / HID) + EPSILON)
            normed = centred * scale
            pb_ref[part(m), here] = normed
            s2_ref[part(m), here] = slope * scale
            out = normed * gain_ref[part(m), :] + gain_ref[part(BIG + m), :]
            if m % SLOTS == SLOTS - 1:
                out = out.astype(BF).astype(F32)
            y_ref[part(m), here] = out

    lane_tiles(events, second_gelu)
    orders = [(t * SLOTS, t * SLOTS + 1, t * SLOTS + 2, (1 - t) * SLOTS + 2) for t in range(2)]

    def mix(j, here):
        for t in range(2):
            logits = [lg_ref[8 * t + k : 8 * t + k + 1, here] for k in range(GATES)]
            top = jnp.maximum(jnp.maximum(logits[0], logits[1]), jnp.maximum(logits[2], logits[3]))
            raised = [jnp.exp(logit - top) for logit in logits]
            scale = 1.0 / (raised[0] + raised[1] + raised[2] + raised[3])
            mixture = None
            for k in range(GATES):
                prob = raised[k] * scale
                prob_ref[8 * t + k : 8 * t + k + 1, here] = prob
                term = prob * y_ref[part(orders[t][k]), here]
                mixture = term if mixture is None else mixture + term
            q_ref[part(t), here] = mixture.astype(BF)

    lane_tiles(events, mix)
    for t in range(2):
        pt_ref[t * TOWER1 : (t + 1) * TOWER1, :] = tn(packs[t][T1_AT : T1_AT + HID, :], q_ref[part(t), :])

    def tower_gelu(j, here):
        act, slope = gelu_both(pt_ref[:, here])
        pt_ref[:, here] = slope
        u1_ref[:, here] = act.astype(BF)

    lane_tiles(events, tower_gelu)
    for t in range(2):
        p4_ref[t * TOWER2 : (t + 1) * TOWER2, :] = nn(
            packs[t][T2_AT : T2_AT + TOWER2, :], u1_ref[t * TOWER1 : (t + 1) * TOWER1, :]
        )

    def head(j, here):
        act, slope = gelu_both(p4_ref[:, here])
        u2 = act.astype(BF).astype(F32)
        product = u2 * third_ref[...]
        deltas = []
        for t in range(2):
            logit = col_sum(product[t * TOWER2 : (t + 1) * TOWER2])
            prediction = 1.0 / (1.0 + jnp.exp(-logit))
            pred_ref[t, pl.ds(j, 1), :] = prediction
            label = lab_ref[pl.ds(t * 16 + position * (events // LANES) + j, 1), :]
            deltas.append(jnp.broadcast_to(prediction - label, (TOWER2, LANES)))
        delta = jnp.concatenate(deltas, axis=0)
        acc3_ref[...] += delta * u2
        e2_ref[:, here] = (slope * (delta * third_ref[...])).astype(BF)

    lane_tiles(events, head)
    for t in range(2):
        du_ref[t * TOWER1 : (t + 1) * TOWER1, :] = tn(
            packs[t][T2_AT : T2_AT + TOWER2, :], e2_ref[t * TOWER2 : (t + 1) * TOWER2, :]
        )

    def tower_back(j, here):
        e1_ref[:, here] = (pt_ref[:, here] * du_ref[:, here]).astype(BF)

    lane_tiles(events, tower_back)
    for t in range(2):
        dm_ref[part(t), :] = nn(packs[t][T1_AT : T1_AT + HID, :], e1_ref[t * TOWER1 : (t + 1) * TOWER1, :])

    def mix_back(j, here):
        codes = []
        probs = [[prob_ref[8 * t + k : 8 * t + k + 1, here] for k in range(GATES)] for t in range(2)]
        for t in range(2):
            mixed = dm_ref[part(t), here]
            dmb_ref[part(t), here] = mixed.astype(BF)
            d_prob = [col_sum(mixed * y_ref[part(orders[t][k]), here]) for k in range(GATES)]
            weighted = probs[t][0] * d_prob[0]
            for k in range(1, GATES):
                weighted = weighted + probs[t][k] * d_prob[k]
            codes += [probs[t][k] * (d_prob[k] - weighted) for k in range(GATES)]
            codes.append(jnp.zeros((8 - GATES, LANES), F32))
        fc_ref[WIDE : WIDE + 16, here] = jnp.concatenate(codes, axis=0).astype(BF)
        for m in range(BIG):
            t, s = divmod(m, SLOTS)
            up = probs[t][s] * dm_ref[part(t), here]
            if s == SLOTS - 1:
                up = up + probs[1 - t][SLOTS] * dm_ref[part(1 - t), here]
            normed = pb_ref[part(m), here]
            up_normed = up * normed
            acc_ref[part(m), :] += up_normed
            gain = gain_ref[part(m), :]
            d_normed = up * gain
            mean_one = col_sum(d_normed) * (1.0 / HID)
            mean_two = col_sum(d_normed * normed) * (1.0 / HID)
            e_ref[part(m), here] = (s2_ref[part(m), here] * (d_normed - mean_one - normed * mean_two)).astype(BF)

    lane_tiles(events, mix_back)
    for m in range(BIG):
        s2_ref[part(m), :] = nn(w2_ref[m], e_ref[part(m), :])

    def first_back(j, here):
        for m in range(BIG):
            fc_ref[part(m), here] = (pc_ref[part(m), here] * s2_ref[part(m), here]).astype(BF)

    lane_tiles(events, first_back)
    dx_ref[...] = nn(wc_ref[...], fc_ref[...]).astype(BF).T

    for t, outputs in enumerate((own_outs, oth_outs)):
        for s in range(SLOTS):
            m = t * SLOTS + s
            g_ref[:D, :] = nt(x_ref[...], fc_ref[part(m), :])
            g_ref[D:, :] = nt(h_ref[part(m), :], e_ref[part(m), :])
            p = 0
            for out in outputs:
                for g in range(out.shape[0]):
                    d = at_ref[t, p]
                    p += 1
                    one = pl.ds(pl.multiple_of(d * rows1, rows1), rows1)
                    two = pl.ds(pl.multiple_of(D + d * rows2, rows2), rows2)
                    out[g, s * rows1 : (s + 1) * rows1, :] = g_ref[one, :].astype(BF)
                    low = SLOTS * rows1 + s * rows2
                    out[g, low : low + rows2, :] = g_ref[two, :].astype(BF)
    gate_grad = nt(fc_ref[WIDE : WIDE + 16, :], x_ref[...])
    weights = prob_ref[...].astype(BF)
    shifts = [nt(weights, dmb_ref[part(t), :]) for t in range(2)]
    third_grad = col_sum(acc3_ref[...].T)
    for t in range(2):
        small = smalls[t]
        tower = slice(t * TOWER1, (t + 1) * TOWER1)
        half = slice(t * TOWER2, (t + 1) * TOWER2)
        small[T1_AT : T1_AT + HID, :] = nt(q_ref[part(t), :], e1_ref[tower, :]).astype(BF)
        small[T2_AT : T2_AT + TOWER2, :] = nt(e2_ref[half, :], u1_ref[tower, :]).astype(BF)
        lines = []
        for g in range(GATES):
            row = gate_grad[8 * t + g : 8 * t + g + 1, :]
            lines += [row[:, p * LANES : (p + 1) * LANES] for p in range(D // LANES)]
        for s in range(SLOTS):
            for k in range(2):
                at = (t * SLOTS + s) * HID + k * LANES
                lines.append(col_sum(acc_ref[at : at + LANES, :].T))
        for s in range(SLOTS):
            row = shifts[t][8 * t + s : 8 * t + s + 1, :]
            if s == SLOTS - 1:
                row = row + shifts[1 - t][8 * (1 - t) + SLOTS : 8 * (1 - t) + SLOTS + 1, :]
            lines += [row[:, :LANES], row[:, LANES:]]
        lines.append(third_grad if t == 0 else pltpu.roll(third_grad, TOWER2, 1))
        lines.append(jnp.zeros((3, LANES), F32))
        small[GATE_AT : GATE_AT + 32, :] = jnp.concatenate(lines, axis=0).astype(BF)


def layer(pos, at, x_parts, own_groups, oth_groups, own_pack, oth_pack, outs, rows1, rows2):
    events = sum(part.shape[0] for part in x_parts)
    rows = SLOTS * (rows1 + rows2)
    count, pieces = outs
    grads = (shape((pieces, rows, HID)),) * (2 * count)
    small = shape((G_ROWS, LANES))
    scratch = [
        ((D, events), BF),
        ((D, WIDE + LANES), BF),
        ((BIG, HID, HID), BF),
        ((2 * WIDE, LANES), F32),
        ((2 * TOWER2, LANES), F32),
        ((32, LANES), F32),
        ((WIDE, events), F32),
        ((WIDE, events), F32),
        ((WIDE, events), F32),
        ((WIDE, events), F32),
        ((WIDE, events), BF),
        ((WIDE, events), BF),
        ((WIDE + LANES, events), BF),
        ((16, events), F32),
        ((16, events), F32),
        ((2 * HID, events), BF),
        ((2 * TOWER1, events), F32),
        ((2 * TOWER1, events), BF),
        ((2 * TOWER2, events), F32),
        ((2 * TOWER2, events), BF),
        ((2 * TOWER1, events), BF),
        ((2 * TOWER1, events), F32),
        ((2 * HID, events), F32),
        ((2 * HID, events), BF),
        ((WIDE, LANES), F32),
        ((2 * TOWER2, LANES), F32),
        ((D + HID, HID), F32),
    ]
    n_in = len(x_parts) + len(own_groups) + len(oth_groups) + 2
    result = pl.pallas_call(
        functools.partial(main_kernel, len(x_parts), len(own_groups), count, rows1, rows2),
        out_shape=(shape((2, events // LANES, LANES), F32), shape((events, D))) + grads + (small, small),
        in_specs=[SSPEC, SSPEC] + [VSPEC] * n_in,
        out_specs=(VSPEC,) * (4 + 2 * count),
        scratch_shapes=[pltpu.VMEM(dims, kind) for dims, kind in scratch],
        compiler_params=params(),
        cost_estimate=cost(events * BIG * 196608 * 6, 10e6),
    )(pos, at, *x_parts, *own_groups, *oth_groups, own_pack, oth_pack)
    pred, dx = result[:2]
    return pred, dx, result[2 : 2 + count], result[2 + count : 2 + 2 * count], result[-2], result[-1]


def sibling(value):
    return lax.ppermute(value, "task", [(0, 1), (1, 0)])


def flipped(value, mask):
    pairs = [(i, i ^ mask) for i in range(lax.axis_size("dp"))]
    return lax.ppermute(value, "dp", pairs)


def crossed(value, masks):
    n = lax.axis_size("dp")
    pairs = [(t * n + i, t * n + (i ^ masks[t])) for t in range(2) for i in range(n)]
    return lax.ppermute(value, ("task", "dp"), pairs)


def stack_kernel(count, *refs):
    out = refs[-1]
    for k in range(count):
        out[k] = refs[k][...]


def stacked(pieces, after):
    return pl.pallas_call(
        functools.partial(stack_kernel, len(pieces)),
        out_shape=shape((len(pieces),) + pieces[0].shape, pieces[0].dtype),
        in_specs=[VSPEC] * len(pieces) + [ASPEC] * len(after),
        out_specs=VSPEC,
        compiler_params=params(),
        cost_estimate=cost(0, 1e6),
    )(*pieces, *after)


def table(me, position, quarter):
    one, two = 1 + position, 2 - position
    near = [me ^ (4 * k) for k in range(quarter)]
    return near + [d ^ two for d in near] + [d ^ one for d in near] + [d ^ one ^ two for d in near]


def sum_kernel(count, pieces, *refs):
    refs = list(refs)
    for terms, split in zip(count, pieces):
        arrays = [refs.pop(0) for _ in range(terms)]
        total = arrays[0][...].astype(F32)
        for array in arrays[1:]:
            total = total + array[...].astype(F32)
        refs.append((total, split))
    lists = refs[-len(count) :]
    outs = refs[: -len(count)]
    for total, split in lists:
        for cut in split:
            out = outs.pop(0)
            out[...] = (total if cut is None else total[cut]).astype(out.dtype)


def summed(lists, splits, outs):
    flat = [array for arrays in lists for array in arrays]
    return pl.pallas_call(
        functools.partial(sum_kernel, [len(arrays) for arrays in lists], splits),
        out_shape=tuple(outs),
        in_specs=[VSPEC] * len(flat),
        out_specs=(VSPEC,) * len(outs),
        compiler_params=params(),
        cost_estimate=cost(0, 4e6),
    )(*flat)


def last_kernel(quarter, rows1, rows2, pos_ref, *refs):
    refs = list(refs)
    total = refs[0][...].astype(F32)
    tiny = refs[quarter][...].astype(F32)
    for k in range(1, quarter):
        total = total + refs[k][...].astype(F32)
        tiny = tiny + refs[quarter + k][...].astype(F32)
    w1_ref, w2_ref, o1_ref, o2_ref, sg_ref, ss_ref, og_ref, os_ref, gate_ref, t1_ref, t2_ref, t3_ref = refs[2 * quarter :]
    cut = SLOTS * rows1
    for s in range(EXPERTS):
        w1_ref[s] = total[s * rows1 : (s + 1) * rows1]
        w2_ref[s] = total[cut + s * rows2 : cut + (s + 1) * rows2]
    o1_ref[...] = total[EXPERTS * rows1 : cut]
    o2_ref[...] = total[cut + EXPERTS * rows2 :]
    t1_ref[...] = tiny[T1_AT : T1_AT + HID]
    t2_ref[...] = tiny[T2_AT : T2_AT + TOWER2]
    gates = []
    for g in range(GATES):
        at = GATE_AT + 4 * g
        gates.append(jnp.concatenate([tiny[at + p : at + p + 1] for p in range(D // LANES)], axis=1))
    turned = pos_ref[0] != 0
    gate_ref[0:1, :] = gates[0]
    gate_ref[1:2, :] = gates[1]
    gate_ref[2:3, :] = jnp.where(turned, gates[3], gates[2])
    gate_ref[3:4, :] = jnp.where(turned, gates[2], gates[3])
    for kind, (spec, own) in enumerate(((sg_ref, og_ref), (ss_ref, os_ref))):
        for s in range(SLOTS):
            at = MISC_AT + 2 * (kind * SLOTS + s)
            row = jnp.concatenate([tiny[at : at + 1], tiny[at + 1 : at + 2]], axis=1)
            if s < EXPERTS:
                spec[s : s + 1, :] = row
            else:
                own[...] = row
    t3_ref[...] = tiny[MISC_AT + 12 : MISC_AT + 13, :TOWER2]


def finish(pos, parts, tinies, rows1, rows2):
    outs = (
        shape((EXPERTS, rows1, HID), F32),
        shape((EXPERTS, rows2, HID), F32),
        shape((rows1, HID), F32),
        shape((rows2, HID), F32),
        shape((EXPERTS, HID), F32),
        shape((EXPERTS, HID), F32),
        shape((1, HID), F32),
        shape((1, HID), F32),
        shape((GATES, D), F32),
        shape((HID, TOWER1), F32),
        shape((TOWER2, TOWER1), F32),
        shape((1, TOWER2), F32),
    )
    return pl.pallas_call(
        functools.partial(last_kernel, len(parts), rows1, rows2),
        out_shape=outs,
        in_specs=[SSPEC] + [VSPEC] * (2 * len(parts)),
        out_specs=(VSPEC,) * len(outs),
        compiler_params=params(),
        cost_estimate=cost(0, 4e6),
    )(pos, *parts, *tinies)


def per_device(
    entries,
    lengths,
    labels,
    spec_w1,
    spec_w2,
    spec_gain,
    spec_shift,
    shared_w1,
    shared_w2,
    shared_gain,
    shared_shift,
    gate_w,
    tower_w1,
    tower_w2,
    tower_w3,
):
    position = lax.axis_index("task")
    me = lax.axis_index("dp")
    n = lax.axis_size("dp")
    pos = position.reshape(1)
    rows1, rows2 = spec_w1.shape[2], spec_w2.shape[2]
    direct = rows2 % 16 == 0 and n % 4 == 0 and n & (n - 1) == 0
    pack = jnp.concatenate(
        [part.reshape(-1, HID) for part in (spec_w1, shared_w1, spec_w2, shared_w2)], axis=0
    )
    if direct:
        quarter = n // 4
        far = [pack] + [flipped(pack, 4 * k) for k in range(1, quarter)]

    rows = entries.shape[0]
    starts, ends, meta, small = prepare(
        pos,
        lengths,
        labels,
        spec_gain[0],
        spec_shift[0],
        shared_gain,
        shared_shift,
        gate_w[0].T,
        tower_w1[0],
        tower_w2[0].T,
        tower_w3,
        rows // ROWS,
    )
    other_small = sibling(small)
    turned = entries.T
    x_first = pool(0, 2, pos, meta, starts, ends, turned)
    x_second = pool(1, 2, pos, meta, starts, ends, turned)

    if direct:
        zc = stacked(far, [x_first])
        r1 = crossed(zc, (1, 2))
        r2 = crossed(zc, (2, 1))
        r3 = crossed(r1, (2, 1))
        own = [zc, r2, r1, r3]
        at = jnp.stack([jnp.stack(table(me, position, quarter)), jnp.stack(table(me, 1 - position, quarter))])
        outs, used1, used2 = (2, n // 2), rows1, rows2
    else:
        every = lax.all_gather(pack, "dp", axis=0)
        cut = SLOTS * rows1
        w1 = every[:, :cut].reshape(n, SLOTS, rows1, HID).swapaxes(0, 1).reshape(-1, HID)
        w2 = every[:, cut:].reshape(n, SLOTS, rows2, HID).swapaxes(0, 1).reshape(-1, HID)
        own = [jnp.concatenate([w1, w2], axis=0)[None]]
        at = jnp.zeros((2, 1), jnp.int32)
        outs, used1, used2 = (1, 1), D, HID
    other = [sibling(group) for group in own]
    pred, dx, own_grads, oth_grads, own_tiny, oth_tiny = layer(
        pos, at, [x_first, x_second], own, other, small, other_small, outs, used1, used2
    )

    got = [sibling(grad) for grad in oth_grads[::-1]][::-1]
    got_tiny = sibling(oth_tiny)
    other_dx = sibling(dx)
    if direct:
        block = (quarter, SLOTS * (rows1 + rows2), HID)
        tiny_out = shape((G_ROWS, LANES))
        keep, send = own_grads
        send, tiny = summed([[send, got[1]], [own_tiny, got_tiny]], [[None], [None]], [shape(send.shape), tiny_out])
        other_tiny = crossed(tiny, (1, 2))
        arrived = crossed(send, (1, 2))
        keep, send, tiny = summed(
            [[keep, got[0], arrived], [tiny, other_tiny]],
            [[slice(0, quarter), slice(quarter, 2 * quarter)], [None]],
            [shape(block), shape(block), tiny_out],
        )
        other_tiny = crossed(tiny, (2, 1))
        arrived = crossed(send, (2, 1))
        *parts, tiny = summed(
            [[keep, arrived], [tiny, other_tiny]],
            [list(range(quarter)), [None]],
            [shape(block[1:])] * quarter + [tiny_out],
        )
        tinies = [tiny] + [flipped(tiny, 4 * k) for k in range(1, quarter)]
        parts = [parts[0]] + [flipped(parts[k], 4 * k) for k in range(1, quarter)]
        grads = finish(pos, parts, tinies, rows1, rows2)
    else:
        whole = own_grads[0][0].astype(F32) + got[0][0].astype(F32)
        g1 = lax.psum_scatter(whole[: SLOTS * D].reshape(SLOTS, D, HID), "dp", scatter_dimension=1, tiled=True)
        g2 = lax.psum_scatter(whole[SLOTS * D :].reshape(SLOTS, HID, HID), "dp", scatter_dimension=1, tiled=True)
        part = jnp.concatenate([g1.reshape(-1, HID), g2.reshape(-1, HID)], axis=0)
        tiny = lax.psum(own_tiny.astype(F32) + got_tiny.astype(F32), "dp")
        grads = finish(pos, [part], [tiny], rows1, rows2)
    w1, w2, o1, o2, sg, ss, og, os, gate, t1, t2, t3 = grads
    entry_grads = expand(pos, meta, starts, ends, dx, other_dx, rows).T

    mine = pred[0].reshape(-1)
    theirs = sibling(pred[1]).reshape(-1)
    predictions = jnp.where(
        position == 0, jnp.concatenate([mine, theirs]), jnp.concatenate([theirs, mine])
    )[None]
    return (
        predictions,
        entry_grads,
        w1[None],
        w2[None],
        sg[None],
        ss[None],
        o1[None],
        o2[None],
        og,
        os,
        gate.T[None],
        t1[None],
        t2.T[None],
        t3,
    )


def solution(mesh):
    placed = (
        P("dp", None),
        P("dp", None),
        P("task", "dp"),
        P("task", None, "dp", None),
        P("task", None, "dp", None),
        P("task", None, None),
        P("task", None, None),
        P("task", "dp", None),
        P("task", "dp", None),
        P("task", None),
        P("task", None),
        P("task", None, None),
        P("task", None, None),
        P("task", None, None),
        P("task", None),
    )
    return jax.shard_map(
        per_device,
        mesh=mesh,
        in_specs=placed,
        out_specs=(
            P("task", "dp"),
            P("dp", None),
            P("task", None, "dp", None),
            P("task", None, "dp", None),
            P("task", None, None),
            P("task", None, None),
            P("task", "dp", None),
            P("task", "dp", None),
            P("task", None),
            P("task", None),
            P("task", None, None),
            P("task", None, None),
            P("task", None, None),
            P("task", None),
        ),
        check_vma=False,
    )
```

```python
import functools

import jax
import jax.numpy as jnp
from jax import lax
from jax.experimental import pallas as pl
from jax.experimental.pallas import tpu as pltpu
from jax.sharding import PartitionSpec as P

EXPERTS = 2
GATES = 4
D = 512
HID = 256
TOWER1 = 128
TOWER2 = 64
EMB = 64
FEATS = 8
LANES = 128
BAGS = 128
EVB = BAGS // FEATS
ROWS = 128
EPSILON = 1e-05
K0 = 0.7978845608028654
K1 = K0 * 0.044715
SLOTS = 3
BIG = 2 * SLOTS
WIDE = BIG * HID
BF = jnp.bfloat16
F32 = jnp.float32

T1_AT = 0
T2_AT = T1_AT + HID
GATE_AT = T2_AT + TOWER2
MISC_AT = GATE_AT + GATES * (D // LANES)
LABEL_AT = MISC_AT + 16
G_ROWS = LABEL_AT
SMALL_ROWS = G_ROWS // 2


def nn(left, right):
    return jnp.dot(left, right, preferred_element_type=F32)


def nt(left, right):
    return lax.dot_general(left, right, (((1,), (1,)), ((), ())), preferred_element_type=F32)


def tn(left, right):
    return lax.dot_general(left, right, (((0,), (0,)), ((), ())), preferred_element_type=F32)


def params(mib, **kwargs):
    return pltpu.CompilerParams(vmem_limit_bytes=mib * 1024 * 1024, **kwargs)


def cost(flops, moved):
    return pl.CostEstimate(flops=int(flops), bytes_accessed=int(moved), transcendentals=0)


def shape(dims, kind=BF):
    return jax.ShapeDtypeStruct(dims, kind)


VSPEC = pl.BlockSpec(memory_space=pltpu.VMEM)
SSPEC = pl.BlockSpec(memory_space=pltpu.SMEM)
ASPEC = pl.BlockSpec(memory_space=pl.ANY)


def line(ref, row):
    both = ref[row : row + 1, :].astype(F32)
    return [both[:, :LANES], both[:, LANES:]]


def prep_kernel(
    blocks,
    chunks,
    ids_ref,
    len_ref,
    label_ref,
    sgain_ref,
    sshift_ref,
    ogain_ref,
    oshift_ref,
    gate_ref,
    t1_ref,
    t2_ref,
    t3_ref,
    st_ref,
    en_ref,
    meta_ref,
    small_ref,
):
    k = lax.broadcasted_iota(jnp.int32, (BAGS, BAGS), 0)
    j = lax.broadcasted_iota(jnp.int32, (BAGS, BAGS), 1)
    natural = (j % EVB) * FEATS + j // EVB
    before = jnp.where(k < natural, 1.0, 0.0).astype(BF)
    same = jnp.where(k == natural, 1.0, 0.0).astype(BF)
    lens_f = jnp.concatenate(
        [len_ref[:, b * BAGS : (b + 1) * BAGS] for b in range(blocks)], axis=0
    ).astype(F32)
    lens = lens_f.astype(BF)
    in_block = nn(lens, before)
    own = nn(lens, same)
    sums = jnp.sum(lens_f, axis=1, keepdims=True)
    high = jnp.floor(sums * (1.0 / 128.0))
    low = sums - high * 128.0
    bi = lax.broadcasted_iota(jnp.int32, (blocks, blocks), 0)
    bj = lax.broadcasted_iota(jnp.int32, (blocks, blocks), 1)
    lower = jnp.where(bj < bi, 1.0, 0.0).astype(BF)
    offset = 128.0 * nn(lower, jnp.broadcast_to(high, (blocks, BAGS)).astype(BF)) + nn(
        lower, jnp.broadcast_to(low, (blocks, BAGS)).astype(BF)
    )
    starts = offset + in_block
    st_ref[pl.ds(0, blocks), :] = starts.astype(jnp.int32)
    en_ref[pl.ds(0, blocks), :] = (starts + own).astype(jnp.int32)
    past = jnp.full((8, BAGS), chunks * ROWS, jnp.int32)
    st_ref[pl.ds(blocks, 8), :] = past
    en_ref[pl.ds(blocks, 8), :] = past
    lanes = meta_ref.shape[1]
    begins = jnp.concatenate([offset] * (lanes // BAGS), axis=1)
    row = lax.broadcasted_iota(jnp.int32, (blocks, lanes), 0)
    col = lax.broadcasted_iota(jnp.int32, (blocks, lanes), 1)
    begin = jnp.sum(jnp.where(row == col, begins, 0.0), axis=0, keepdims=True)
    spot = lax.broadcasted_iota(jnp.int32, (1, lanes), 1)
    begin = jnp.where(spot >= blocks, float(chunks * ROWS), begin)
    reached = jnp.where(begins <= (col * ROWS).astype(F32), 1.0, 0.0)
    first = jnp.sum(reached, axis=0, keepdims=True) - 1.0
    meta_ref[0:1, :] = begin.astype(jnp.int32)
    meta_ref[1:2, :] = first.astype(jnp.int32)
    small_ref[T1_AT : T1_AT + HID, :] = t1_ref[...]
    small_ref[T2_AT : T2_AT + TOWER2, :] = t2_ref[...]
    gate = gate_ref[...].astype(F32)
    turned = jnp.concatenate([gate[0:2], gate[3:4], gate[2:3]], axis=0)
    gate = jnp.where(ids_ref[0] == 0, gate, turned)
    lines = [gate[g : g + 1, p * LANES : (p + 1) * LANES] for g in range(GATES) for p in range(D // LANES)]
    lines += line(sgain_ref, 0) + line(sgain_ref, 1) + line(ogain_ref, 0)
    lines += line(sshift_ref, 0) + line(sshift_ref, 1) + line(oshift_ref, 0)
    lines += [jnp.concatenate([t3_ref[...].astype(F32)] * 2, axis=1), jnp.zeros((3, LANES), F32)]
    events = label_ref.shape[1]
    lines += [label_ref[:, p * LANES : (p + 1) * LANES].astype(F32) for p in range(events // LANES)]
    lines += [jnp.zeros((16 - events // LANES, LANES), F32)]
    small_ref[pl.ds(GATE_AT, 48), :] = jnp.concatenate(lines, axis=0).astype(BF)


def prepare(ids, lengths, labels, spec_gain, spec_shift, shared_gain, shared_shift, gate, t1, t2, t3, chunks):
    blocks = lengths.shape[1] // BAGS
    lanes = -(-max(blocks + 1, chunks) // LANES) * LANES
    return pl.pallas_call(
        functools.partial(prep_kernel, blocks, chunks),
        out_shape=(
            shape((blocks + 8, BAGS), jnp.int32),
            shape((blocks + 8, BAGS), jnp.int32),
            shape((2, lanes), jnp.int32),
            shape((LABEL_AT + 16, LANES)),
        ),
        in_specs=[SSPEC] + [VSPEC] * 10,
        out_specs=(VSPEC,) * 4,
        compiler_params=params(56),
        cost_estimate=cost(1e9, 1e6),
    )(ids, lengths, labels, spec_gain, spec_shift, shared_gain, shared_shift, gate, t1, t2, t3)


def one_hot(starts, ends, base):
    row = lax.broadcasted_iota(jnp.int32, (ROWS, 2 * BAGS), 0).astype(F32).astype(BF)
    low = jnp.clip(starts - base, 0, ROWS).astype(F32).astype(BF)
    high = jnp.clip(ends - base, 0, ROWS).astype(F32).astype(BF)
    return jnp.where((row >= low) & (row < high), jnp.ones((), BF), jnp.zeros((), BF))


def window(ref, block):
    first = ref[pl.ds(block, 1), :]
    second = ref[pl.ds(block + 1, 1), :]
    return jnp.concatenate([first, second], axis=1)


def pool_kernel(skip, count, half_blocks, chunks, ids_ref, meta_ref, st_ref, en_ref, ent_ref, *refs):
    x_ref, acc_ref = refs[-2:]
    base_block = ids_ref[0] * half_blocks + skip

    def clear(i, carry):
        at = pl.multiple_of((base_block + i) * BAGS, BAGS)
        acc_ref[:, pl.ds(at, BAGS)] = jnp.zeros((EMB, BAGS), F32)
        return carry

    lax.fori_loop(0, count, clear, 0, unroll=True)

    low_chunk = meta_ref[0, base_block] // ROWS
    high_chunk = (meta_ref[0, base_block + count] + ROWS - 1) // ROWS
    step = 9

    def chunk(i, carry):
        for u in range(step):
            c = low_chunk + i * step + u
            inside = jnp.minimum(c, chunks - 1)
            block = meta_ref[1, inside]
            at = pl.multiple_of(inside * ROWS, ROWS)
            picked = one_hot(window(st_ref, block), window(en_ref, block), c * ROWS)
            part = nn(ent_ref[:, pl.ds(at, ROWS)], picked)
            to = pl.multiple_of(block * BAGS, BAGS)
            acc_ref[:, pl.ds(to, 2 * BAGS)] += part
        return carry

    lax.fori_loop(0, (high_chunk - low_chunk + step - 1) // step, chunk, 0)

    def place(i, carry):
        at = pl.multiple_of((base_block + i) * BAGS, BAGS)
        to = pl.multiple_of(i * EVB, EVB)
        block = acc_ref[:, pl.ds(at, BAGS)].T
        for pair in range(FEATS // 2):
            left = block[2 * pair * EVB : (2 * pair + 1) * EVB]
            right = block[(2 * pair + 1) * EVB : (2 * pair + 2) * EVB]
            x_ref[pl.ds(to, EVB), pair * 2 * EMB : (pair + 1) * 2 * EMB] = jnp.concatenate(
                [left, right], axis=1
            ).astype(BF)
        return carry

    lax.fori_loop(0, count, place, 0, unroll=12)


def pool(part, parts, ids, meta, starts, ends, entries, *after):
    blocks = starts.shape[0] - 8
    half_blocks = blocks // 2
    count = half_blocks // parts
    chunks = entries.shape[1] // ROWS
    return pl.pallas_call(
        functools.partial(pool_kernel, part * count, count, half_blocks, chunks),
        out_shape=shape((count * EVB, D)),
        in_specs=[SSPEC, SSPEC, VSPEC, VSPEC, VSPEC] + [ASPEC] * len(after),
        out_specs=VSPEC,
        scratch_shapes=[pltpu.VMEM((EMB, (blocks + 1) * BAGS), F32)],
        compiler_params=params(16),
        cost_estimate=cost(10e9, 5e6),
    )(ids, meta, starts, ends, entries, *after)


def expand_kernel(half_blocks, group, ids_ref, meta_ref, st_ref, en_ref, own_ref, other_ref, out_ref, rows_ref):
    position = ids_ref[0]
    step = pl.program_id(0)

    @pl.when(step == 0)
    def _():
        for source, half in ((own_ref, position), (other_ref, 1 - position)):

            def place(i, carry):
                at = pl.multiple_of(i * EVB, EVB)
                to = pl.multiple_of((half * half_blocks + i) * BAGS, BAGS)
                for pair in range(FEATS // 2):
                    tile = source[pl.ds(at, EVB), pair * 2 * EMB : (pair + 1) * 2 * EMB]
                    rows_ref[pl.ds(to + 2 * pair * EVB, EVB), :] = tile[:, :EMB]
                    rows_ref[pl.ds(to + (2 * pair + 1) * EVB, EVB), :] = tile[:, EMB:]
                return carry

            lax.fori_loop(0, half_blocks, place, 0, unroll=12)
        rows_ref[pl.ds(2 * half_blocks * BAGS, BAGS), :] = jnp.zeros((BAGS, EMB), BF)

    for u in range(group):
        c = step * group + u
        block = meta_ref[1, c]
        picked = one_hot(window(st_ref, block), window(en_ref, block), c * ROWS)
        at = pl.multiple_of(block * BAGS, BAGS)
        out_ref[:, u * ROWS : (u + 1) * ROWS] = nn(picked, rows_ref[pl.ds(at, 2 * BAGS), :]).astype(BF).T


def expand(ids, meta, starts, ends, own, other, rows):
    blocks = starts.shape[0] - 8
    chunks = rows // ROWS
    group = 36
    while chunks % group:
        group -= 1
    return pl.pallas_call(
        functools.partial(expand_kernel, blocks // 2, group),
        grid=(chunks // group,),
        out_shape=shape((EMB, rows)),
        in_specs=[SSPEC, SSPEC, VSPEC, VSPEC, VSPEC, VSPEC],
        out_specs=pl.BlockSpec((EMB, group * ROWS), lambda i: (0, i)),
        scratch_shapes=[pltpu.VMEM(((blocks + 1) * BAGS, EMB), BF)],
        compiler_params=params(24, dimension_semantics=("arbitrary",)),
        cost_estimate=cost(12e9, 6e6),
    )(ids, meta, starts, ends, own, other)


def gelu_both(v):
    square = v * v
    half = 0.5 * jnp.tanh(v * (K1 * square + K0)) + 0.5
    act = v * half
    slope = half + act * (1.0 - half) * (6.0 * K1 * square + 2.0 * K0)
    return act, slope


def col_sum(value):
    return jnp.sum(value, axis=0, keepdims=True)


def lane_tiles(events, body):
    def step(j, carry):
        body(j, pl.ds(pl.multiple_of(j * LANES, LANES), LANES))
        return carry

    lax.fori_loop(0, events // LANES, step, 0)


def main_kernel(xs, groups, plan, staged, rows1, rows2, ids_ref, *refs):
    refs = list(refs)
    take = lambda n: [refs.pop(0) for _ in range(n)]
    inputs = take(xs + 2 * groups + 2)
    preds = take(2)
    outputs = take(1 + 2 * len(plan))
    staging = take(len(inputs))
    sources = [pltpu.make_async_copy(a, b, refs[-1].at[k]) for k, (a, b) in enumerate(zip(inputs, staging))]
    for copy in sources:
        copy.start()
    x_parts = [(staging[k], sources[k]) for k in range(xs)]
    whole = list(zip(staging, sources))[xs : xs + 2 * groups]
    own_groups, oth_groups = whole[:groups], whole[groups:]
    packs = staging[-2:]
    results = take(len(outputs))
    targets = [pltpu.make_async_copy(a, b, refs[-2].at[k]) for k, (a, b) in enumerate(zip(results, outputs))]
    dx_ref = results[0]
    own_outs, oth_outs = results[1 : 1 + len(plan)], results[1 + len(plan) :]
    own_sent, oth_sent = targets[1 : 1 + len(plan)], targets[1 + len(plan) :]
    x_ref, wc_ref, w2_ref, gain_ref, third_ref, lab_ref, pc_ref, pb_ref, s2_ref, y_ref, h_ref, e_ref, fc_ref = take(13)
    lg_ref, prob_ref, q_ref, pt_ref, u1_ref, p4_ref, e2_ref, e1_ref, du_ref, dm_ref, dmb_ref, acc_ref, acc3_ref, g1_ref, g2_ref = take(15)
    position = ids_ref[0]
    events = x_ref.shape[1]
    quarter = D // rows1 // 4

    def part(m):
        return slice(m * HID, (m + 1) * HID)

    def rows_of(t, p):
        if not quarter:
            return pl.ds(0, rows1), pl.ds(0, rows2)
        where = position if t == 0 else 1 - position
        d = ids_ref[1] ^ (4 * (p % quarter))
        if (p // quarter) & 1:
            d = d ^ (2 - where)
        if p // quarter >= 2:
            d = d ^ (1 + where)
        return (
            pl.ds(pl.multiple_of(d * rows1, rows1), rows1),
            pl.ds(pl.multiple_of(d * rows2, rows2), rows2),
        )

    size = events // xs
    for k, (piece, copy) in enumerate(x_parts):
        copy.wait()
        x_ref[:, k * size : (k + 1) * size] = piece[...].T
    for t, whole in enumerate((own_groups, oth_groups)):
        p = 0
        for group, copy in whole:
            copy.wait()
            for g in range(group.shape[0]):
                one, two = rows_of(t, p)
                p += 1
                for s in range(SLOTS):
                    wc_ref[one, part(t * SLOTS + s)] = group[g, s * rows1 : (s + 1) * rows1, :]
                    low = SLOTS * rows1 + s * rows2
                    w2_ref[t * SLOTS + s, two, :] = group[g, low : low + rows2, :]
    sources[-2].wait()
    sources[-1].wait()
    lines = []
    for t in range(2):
        block = packs[t][GATE_AT : GATE_AT + 16, :].astype(F32)
        for g in range(GATES):
            lines.append(
                jnp.concatenate([block[4 * g + p : 4 * g + p + 1, :] for p in range(D // LANES)], axis=1)
            )
        lines.append(jnp.zeros((8 - GATES, D), F32))
    gates = jnp.concatenate(lines, axis=0).astype(BF)
    wc_ref[:, WIDE:] = jnp.concatenate([gates, jnp.zeros((LANES - 16, D), BF)], axis=0).T
    fc_ref[WIDE:, :] = jnp.zeros((LANES, events), BF)
    acc_ref[...] = jnp.zeros_like(acc_ref)
    acc3_ref[...] = jnp.zeros_like(acc3_ref)
    for t in range(2):
        misc = packs[t][MISC_AT : MISC_AT + 16, :].astype(F32)
        for s in range(SLOTS):
            for kind in range(2):
                for half in range(2):
                    at = 2 * (kind * SLOTS + s) + half
                    to = ((kind * 2 + t) * SLOTS + s) * HID + half * LANES
                    gain_ref[to : to + LANES, :] = jnp.broadcast_to(misc[at : at + 1, :], (LANES, LANES)).T
        third = jnp.broadcast_to(misc[12:13, :], (LANES, LANES)).T
        third_ref[t * TOWER2 : (t + 1) * TOWER2, :] = third[:TOWER2]
        lab_ref[t * 16 : (t + 1) * 16, :] = packs[t][LABEL_AT : LABEL_AT + 16, :].astype(F32)

    for m in range(BIG):
        pc_ref[part(m), :] = tn(wc_ref[:, part(m)], x_ref[...])
    lg_ref[...] = nn(gates, x_ref[...])

    def first_gelu(j, here):
        for m in range(BIG):
            act, slope = gelu_both(pc_ref[part(m), here])
            pc_ref[part(m), here] = slope
            h_ref[part(m), here] = act.astype(BF)

    lane_tiles(events, first_gelu)
    for m in range(BIG):
        pb_ref[part(m), :] = tn(w2_ref[m], h_ref[part(m), :])

    def second_gelu(j, here):
        for m in range(BIG):
            act, slope = gelu_both(pb_ref[part(m), here])
            centred = act - col_sum(act) * (1.0 / HID)
            scale = lax.rsqrt(col_sum(centred * centred) * (1.0 / HID) + EPSILON)
            normed = centred * scale
            pb_ref[part(m), here] = normed
            s2_ref[part(m), here] = slope * scale
            out = normed * gain_ref[part(m), :] + gain_ref[part(BIG + m), :]
            if m % SLOTS == SLOTS - 1:
                out = out.astype(BF).astype(F32)
            y_ref[part(m), here] = out

    lane_tiles(events, second_gelu)
    orders = [(t * SLOTS, t * SLOTS + 1, t * SLOTS + 2, (1 - t) * SLOTS + 2) for t in range(2)]

    def mix(j, here):
        for t in range(2):
            logits = [lg_ref[8 * t + k : 8 * t + k + 1, here] for k in range(GATES)]
            top = jnp.maximum(jnp.maximum(logits[0], logits[1]), jnp.maximum(logits[2], logits[3]))
            raised = [jnp.exp(logit - top) for logit in logits]
            scale = 1.0 / (raised[0] + raised[1] + raised[2] + raised[3])
            mixture = None
            for k in range(GATES):
                prob = raised[k] * scale
                prob_ref[8 * t + k : 8 * t + k + 1, here] = prob
                term = prob * y_ref[part(orders[t][k]), here]
                mixture = term if mixture is None else mixture + term
            q_ref[part(t), here] = mixture.astype(BF)

    lane_tiles(events, mix)
    for t in range(2):
        pt_ref[t * TOWER1 : (t + 1) * TOWER1, :] = tn(packs[t][T1_AT : T1_AT + HID, :], q_ref[part(t), :])

    def tower_gelu(j, here):
        act, slope = gelu_both(pt_ref[:, here])
        pt_ref[:, here] = slope
        u1_ref[:, here] = act.astype(BF)

    lane_tiles(events, tower_gelu)
    for t in range(2):
        p4_ref[t * TOWER2 : (t + 1) * TOWER2, :] = nn(
            packs[t][T2_AT : T2_AT + TOWER2, :], u1_ref[t * TOWER1 : (t + 1) * TOWER1, :]
        )

    def head(j, here):
        act, slope = gelu_both(p4_ref[:, here])
        u2 = act.astype(BF).astype(F32)
        product = u2 * third_ref[...]
        deltas = []
        for t in range(2):
            logit = col_sum(product[t * TOWER2 : (t + 1) * TOWER2])
            prediction = 1.0 / (1.0 + jnp.exp(-logit))
            preds[t][pl.ds(j, 1), :] = prediction
            label = lab_ref[pl.ds(t * 16 + position * (events // LANES) + j, 1), :]
            deltas.append(jnp.broadcast_to(prediction - label, (TOWER2, LANES)))
        delta = jnp.concatenate(deltas, axis=0)
        acc3_ref[...] += delta * u2
        e2_ref[:, here] = (slope * (delta * third_ref[...])).astype(BF)

    lane_tiles(events, head)
    for t in range(2):
        du_ref[t * TOWER1 : (t + 1) * TOWER1, :] = tn(
            packs[t][T2_AT : T2_AT + TOWER2, :], e2_ref[t * TOWER2 : (t + 1) * TOWER2, :]
        )

    def tower_back(j, here):
        e1_ref[:, here] = (pt_ref[:, here] * du_ref[:, here]).astype(BF)

    lane_tiles(events, tower_back)
    for t in range(2):
        dm_ref[part(t), :] = nn(packs[t][T1_AT : T1_AT + HID, :], e1_ref[t * TOWER1 : (t + 1) * TOWER1, :])

    def mix_back(j, here):
        codes = []
        probs = [[prob_ref[8 * t + k : 8 * t + k + 1, here] for k in range(GATES)] for t in range(2)]
        for t in range(2):
            mixed = dm_ref[part(t), here]
            dmb_ref[part(t), here] = mixed.astype(BF)
            d_prob = [col_sum(mixed * y_ref[part(orders[t][k]), here]) for k in range(GATES)]
            weighted = probs[t][0] * d_prob[0]
            for k in range(1, GATES):
                weighted = weighted + probs[t][k] * d_prob[k]
            codes += [probs[t][k] * (d_prob[k] - weighted) for k in range(GATES)]
            codes.append(jnp.zeros((8 - GATES, LANES), F32))
        fc_ref[WIDE : WIDE + 16, here] = jnp.concatenate(codes, axis=0).astype(BF)
        for m in range(BIG):
            t, s = divmod(m, SLOTS)
            up = probs[t][s] * dm_ref[part(t), here]
            if s == SLOTS - 1:
                up = up + probs[1 - t][SLOTS] * dm_ref[part(1 - t), here]
            normed = pb_ref[part(m), here]
            up_normed = up * normed
            acc_ref[part(m), :] += up_normed
            gain = gain_ref[part(m), :]
            d_normed = up * gain
            mean_one = col_sum(d_normed) * (1.0 / HID)
            mean_two = col_sum(d_normed * normed) * (1.0 / HID)
            e_ref[part(m), here] = (s2_ref[part(m), here] * (d_normed - mean_one - normed * mean_two)).astype(BF)

    lane_tiles(events, mix_back)
    for m in range(BIG):
        s2_ref[part(m), :] = nn(w2_ref[m], e_ref[part(m), :])

    def first_back(j, here):
        for m in range(BIG):
            fc_ref[part(m), here] = (pc_ref[part(m), here] * s2_ref[part(m), here]).astype(BF)

    lane_tiles(events, first_back)
    dx_ref[...] = nn(wc_ref[...], fc_ref[...]).astype(BF).T
    targets[0].start()

    gate_grad = nt(fc_ref[WIDE : WIDE + 16, :], x_ref[...])
    weights = prob_ref[...].astype(BF)
    shifts = [nt(weights, dmb_ref[part(t), :]) for t in range(2)]
    third_grad = col_sum(acc3_ref[...].T)
    for t, results, sent in ((1, oth_outs, oth_sent), (0, own_outs, own_sent)):
        for s in range(SLOTS):
            m = t * SLOTS + s
            g1_ref[...] = nt(x_ref[...], fc_ref[part(m), :])
            g2_ref[...] = nt(h_ref[part(m), :], e_ref[part(m), :])
            p = 0
            for out, (pieces, small_first) in zip(results, plan):
                for g in range(pieces):
                    one, two = rows_of(t, p)
                    p += 1
                    at = g * SLOTS * (rows1 + rows2) + (SMALL_ROWS if small_first else 0)
                    out[at + s * rows1 : at + (s + 1) * rows1, :] = g1_ref[one, :].astype(BF)
                    at = at + SLOTS * rows1 + s * rows2
                    out[at : at + rows2, :] = g2_ref[two, :].astype(BF)
        tower = slice(t * TOWER1, (t + 1) * TOWER1)
        half = slice(t * TOWER2, (t + 1) * TOWER2)
        lines = []
        for g in range(GATES):
            row = gate_grad[8 * t + g : 8 * t + g + 1, :]
            lines += [row[:, p * LANES : (p + 1) * LANES] for p in range(D // LANES)]
        for s in range(SLOTS):
            for k in range(2):
                at = (t * SLOTS + s) * HID + k * LANES
                lines.append(col_sum(acc_ref[at : at + LANES, :].T))
        for s in range(SLOTS):
            row = shifts[t][8 * t + s : 8 * t + s + 1, :]
            if s == SLOTS - 1:
                row = row + shifts[1 - t][8 * (1 - t) + SLOTS : 8 * (1 - t) + SLOTS + 1, :]
            lines += [row[:, :LANES], row[:, LANES:]]
        lines.append(third_grad if t == 0 else pltpu.roll(third_grad, TOWER2, 1))
        lines.append(jnp.zeros((3, LANES), F32))
        small = jnp.concatenate(
            [
                nt(q_ref[part(t), :], e1_ref[tower, :]),
                nt(e2_ref[half, :], u1_ref[tower, :]),
                jnp.concatenate(lines, axis=0),
            ],
            axis=0,
        )
        small = jnp.concatenate([small[:SMALL_ROWS], small[SMALL_ROWS:]], axis=1).astype(BF)
        for out, copy, (_, small_first) in list(zip(results, sent, plan))[::-1]:
            if small_first:
                out[:SMALL_ROWS, :] = small
            copy.start()
    for copy in targets:
        copy.wait()


def layer(ids, x_parts, own_groups, oth_groups, own_pack, oth_pack, plan, rows1, rows2):
    events = sum(part.shape[0] for part in x_parts)
    rows = SLOTS * (rows1 + rows2)
    grads = tuple(shape((pieces * rows + small * SMALL_ROWS, HID)) for pieces, small in plan)
    pred = shape((events // LANES, LANES), F32)
    results = (shape((events, D)),) + grads + grads
    scratch = [
        ((D, events), BF),
        ((D, WIDE + LANES), BF),
        ((BIG, HID, HID), BF),
        ((2 * WIDE, LANES), F32),
        ((2 * TOWER2, LANES), F32),
        ((32, LANES), F32),
        ((WIDE, events), F32),
        ((WIDE, events), F32),
        ((WIDE, events), F32),
        ((WIDE, events), F32),
        ((WIDE, events), BF),
        ((WIDE, events), BF),
        ((WIDE + LANES, events), BF),
        ((16, events), F32),
        ((16, events), F32),
        ((2 * HID, events), BF),
        ((2 * TOWER1, events), F32),
        ((2 * TOWER1, events), BF),
        ((2 * TOWER2, events), F32),
        ((2 * TOWER2, events), BF),
        ((2 * TOWER1, events), BF),
        ((2 * TOWER1, events), F32),
        ((2 * HID, events), F32),
        ((2 * HID, events), BF),
        ((WIDE, LANES), F32),
        ((2 * TOWER2, LANES), F32),
        ((D, HID), F32),
        ((HID, HID), F32),
    ]
    arrays = [*x_parts, *own_groups, *oth_groups, own_pack, oth_pack]
    staging = [(array.shape, array.dtype) for array in arrays] + [(r.shape, r.dtype) for r in results]
    mine, theirs, dx, *grads = pl.pallas_call(
        functools.partial(main_kernel, len(x_parts), len(own_groups), plan, len(arrays), rows1, rows2),
        out_shape=(pred, pred) + results,
        in_specs=[SSPEC] + [ASPEC] * len(arrays),
        out_specs=(VSPEC, VSPEC) + (ASPEC,) * len(results),
        scratch_shapes=[pltpu.VMEM(dims, kind) for dims, kind in staging + scratch]
        + [pltpu.SemaphoreType.DMA((len(results),)), pltpu.SemaphoreType.DMA((len(arrays),))],
        compiler_params=params(50),
        cost_estimate=cost(events * BIG * 196608 * 6, 10e6),
    )(ids, *arrays)
    return (mine, theirs), dx, grads[: len(plan)], grads[len(plan) :]


def sibling(value):
    return lax.ppermute(value, "task", [(0, 1), (1, 0)])


def flipped(value, mask):
    pairs = [(i, i ^ mask) for i in range(lax.axis_size("dp"))]
    return lax.ppermute(value, "dp", pairs)


def crossed(value, masks):
    n = lax.axis_size("dp")
    pairs = [(t * n + i, t * n + (i ^ masks[t])) for t in range(2) for i in range(n)]
    return lax.ppermute(value, ("task", "dp"), pairs)


def stack_kernel(count, *refs):
    out, sems = refs[count], refs[count + 1]
    copies = [pltpu.make_async_copy(refs[k], out.at[k], sems.at[k]) for k in range(count)]
    for copy in copies:
        copy.start()
    for copy in copies:
        copy.wait()


def stacked(pieces):
    return pl.pallas_call(
        functools.partial(stack_kernel, len(pieces)),
        out_shape=shape((len(pieces),) + pieces[0].shape, pieces[0].dtype),
        in_specs=[ASPEC] * len(pieces),
        out_specs=VSPEC,
        scratch_shapes=[pltpu.SemaphoreType.DMA((len(pieces),))],
        compiler_params=params(4),
        cost_estimate=cost(0, 1e6),
    )(*pieces)


def summed(*terms):
    total = terms[0].astype(F32)
    for term in terms[1:]:
        total = total + term.astype(F32)
    return total.astype(BF)


def small_kernel(one_ref, two_ref, out_ref):
    out_ref[...] = (one_ref[...].astype(F32) + two_ref[...].astype(F32)).astype(BF)


def small_sum(one, two):
    lead = pl.BlockSpec((SMALL_ROWS, HID), lambda i: (0, 0))
    return pl.pallas_call(
        small_kernel,
        grid=(1,),
        out_shape=shape((SMALL_ROWS, HID)),
        in_specs=[lead, lead],
        out_specs=lead,
        compiler_params=params(4),
        cost_estimate=cost(8e9, 1e6),
    )(one, two)


def tie_kernel(*refs):
    pass


def tied(value, after):
    return pl.pallas_call(
        tie_kernel,
        out_shape=shape(value.shape, value.dtype),
        in_specs=[ASPEC, ASPEC],
        out_specs=ASPEC,
        input_output_aliases={0: 0},
        compiler_params=params(1),
        cost_estimate=cost(0, 1),
    )(value, after)


def far_kernel(quarter, rows, keep_ref, got_ref, mid_ref, near_ref, *outs):
    for k, out in enumerate(outs):
        here = slice(k * rows, (k + 1) * rows)
        total = keep_ref[here, :].astype(F32) + got_ref[here, :].astype(F32)
        at = SMALL_ROWS + k * rows
        total = total + mid_ref[at : at + rows, :].astype(F32)
        out[...] = (total + near_ref[here, :].astype(F32)).astype(BF)


def far_messages(quarter, rows, keep, got, mid, near):
    def lead(size):
        return pl.BlockSpec((size, HID), lambda i: (0, 0))

    size = quarter * rows
    return pl.pallas_call(
        functools.partial(far_kernel, quarter, rows),
        grid=(1,),
        out_shape=(shape((rows, HID)),) * quarter,
        in_specs=[lead(size), lead(size), lead(size + SMALL_ROWS), lead(size)],
        out_specs=(lead(rows),) * quarter,
        compiler_params=params(12),
        cost_estimate=cost(0, 4e6),
    )(keep, got, mid, near)


def last_kernel(count, rows1, rows2, ids_ref, *refs):
    total = refs[0][...].astype(F32)
    for k in range(1, count):
        total = total + refs[k][...].astype(F32)
    small = refs[count][...].astype(F32)
    refs = refs[count + 1 :]
    if len(refs) > 12:
        small = small + refs[0][...].astype(F32)
        refs = refs[1:]
    w1_ref, w2_ref, o1_ref, o2_ref, sg_ref, ss_ref, og_ref, os_ref, gate_ref, t1_ref, t2_ref, t3_ref = refs
    tiny = jnp.concatenate([small[:, :LANES], small[:, LANES:]], axis=0)
    cut = SLOTS * rows1
    for s in range(EXPERTS):
        w1_ref[s] = total[s * rows1 : (s + 1) * rows1]
        w2_ref[s] = total[cut + s * rows2 : cut + (s + 1) * rows2]
    o1_ref[...] = total[EXPERTS * rows1 : cut]
    o2_ref[...] = total[cut + EXPERTS * rows2 :]
    t1_ref[...] = tiny[T1_AT : T1_AT + HID]
    t2_ref[...] = tiny[T2_AT : T2_AT + TOWER2]
    gates = []
    for g in range(GATES):
        at = GATE_AT + 4 * g
        gates.append(jnp.concatenate([tiny[at + p : at + p + 1] for p in range(D // LANES)], axis=1))
    turned = ids_ref[0] != 0
    gate_ref[0:1, :] = gates[0]
    gate_ref[1:2, :] = gates[1]
    gate_ref[2:3, :] = jnp.where(turned, gates[3], gates[2])
    gate_ref[3:4, :] = jnp.where(turned, gates[2], gates[3])
    for kind, (spec, own) in enumerate(((sg_ref, og_ref), (ss_ref, os_ref))):
        for s in range(SLOTS):
            at = MISC_AT + 2 * (kind * SLOTS + s)
            row = jnp.concatenate([tiny[at : at + 1], tiny[at + 1 : at + 2]], axis=1)
            if s < EXPERTS:
                spec[s : s + 1, :] = row
            else:
                own[...] = row
    t3_ref[...] = tiny[MISC_AT + 12 : MISC_AT + 13, :TOWER2]


def finish(ids, parts, smalls, rows1, rows2):
    outs = (
        shape((EXPERTS, rows1, HID), F32),
        shape((EXPERTS, rows2, HID), F32),
        shape((rows1, HID), F32),
        shape((rows2, HID), F32),
        shape((EXPERTS, HID), F32),
        shape((EXPERTS, HID), F32),
        shape((1, HID), F32),
        shape((1, HID), F32),
        shape((GATES, D), F32),
        shape((HID, TOWER1), F32),
        shape((TOWER2, TOWER1), F32),
        shape((1, TOWER2), F32),
    )
    return pl.pallas_call(
        functools.partial(last_kernel, len(parts), rows1, rows2),
        out_shape=outs,
        in_specs=[SSPEC] + [VSPEC] * (len(parts) + len(smalls)),
        out_specs=(VSPEC,) * len(outs),
        compiler_params=params(8),
        cost_estimate=cost(0, 4e6),
    )(ids, *parts, *smalls)


def per_device(
    entries,
    lengths,
    labels,
    spec_w1,
    spec_w2,
    spec_gain,
    spec_shift,
    shared_w1,
    shared_w2,
    shared_gain,
    shared_shift,
    gate_w,
    tower_w1,
    tower_w2,
    tower_w3,
):
    position = lax.axis_index("task")
    n = lax.axis_size("dp")
    ids = jnp.stack([position, lax.axis_index("dp")]).astype(jnp.int32)
    rows1, rows2 = spec_w1.shape[2], spec_w2.shape[2]
    direct = rows2 % 16 == 0 and n % 4 == 0 and n & (n - 1) == 0
    pack = jnp.concatenate(
        [part.reshape(-1, HID) for part in (spec_w1, shared_w1, spec_w2, shared_w2)], axis=0
    )
    if direct:
        quarter = n // 4
        far = [pack] + [flipped(pack, 4 * k) for k in range(1, quarter)]

    rows = entries.shape[0]
    starts, ends, meta, small = prepare(
        ids,
        lengths,
        labels,
        spec_gain[0],
        spec_shift[0],
        shared_gain,
        shared_shift,
        gate_w[0].T,
        tower_w1[0],
        tower_w2[0].T,
        tower_w3,
        rows // ROWS,
    )
    other_small = sibling(small)
    turned = entries.T
    x_first = pool(0, 2, ids, meta, starts, ends, turned)

    if direct:
        zc = stacked(far)
        r1 = tied(crossed(zc, (1, 2)), x_first)
        r2 = crossed(zc, (2, 1))
        x_second = pool(1, 2, ids, meta, starts, ends, turned, r2)
        r3 = tied(crossed(r1, (2, 1)), x_second)
        own = [zc, r2, r1, r3]
        plan, used1, used2 = ((2 * quarter, 0), (2 * quarter, 1)), rows1, rows2
    else:
        x_second = pool(1, 2, ids, meta, starts, ends, turned)
        every = lax.all_gather(pack, "dp", axis=0)
        cut = SLOTS * rows1
        w1 = every[:, :cut].reshape(n, SLOTS, rows1, HID).swapaxes(0, 1).reshape(-1, HID)
        w2 = every[:, cut:].reshape(n, SLOTS, rows2, HID).swapaxes(0, 1).reshape(-1, HID)
        own = [jnp.concatenate([w1, w2], axis=0)[None]]
        plan, used1, used2 = ((1, 1),), D, HID
    other = [sibling(group) for group in own]
    pred, dx, own_grads, oth_grads = layer(
        ids, [x_first, x_second], own, other, small, other_small, plan, used1, used2
    )

    got = [sibling(grad) for grad in oth_grads[::-1]][::-1]
    other_dx = sibling(dx)
    turned = expand(ids, meta, starts, ends, dx, other_dx, rows)
    piece = SLOTS * (rows1 + rows2)
    if direct:
        keep, send = own_grads
        send = summed(send, got[1])
        mid = tied(crossed(send, (1, 2)), turned)
        cut = quarter * piece
        small = small_sum(send, mid)
        send = summed(keep[cut:], got[0][cut:], mid[SMALL_ROWS + cut :])
        near = crossed(send, (2, 1))
        parts = far_messages(quarter, piece, keep, got[0], mid, near)
        smalls = [small] + [tied(flipped(small, 4 * k), parts[0]) for k in range(1, quarter)]
        parts = [parts[0]] + [flipped(parts[k], 4 * k) for k in range(1, quarter)]
        small = summed(*smalls)
        grads = finish(ids, parts, [small, crossed(small, (2, 1))], rows1, rows2)
    else:
        whole = own_grads[0].astype(F32) + got[0].astype(F32)
        small = lax.psum(whole[:SMALL_ROWS], "dp")
        whole = whole[SMALL_ROWS:]
        cut = SLOTS * D
        g1 = lax.psum_scatter(whole[:cut].reshape(SLOTS, D, HID), "dp", scatter_dimension=1, tiled=True)
        g2 = lax.psum_scatter(whole[cut:].reshape(SLOTS, HID, HID), "dp", scatter_dimension=1, tiled=True)
        part = jnp.concatenate([g1.reshape(-1, HID), g2.reshape(-1, HID)], axis=0)
        grads = finish(ids, [part], [small], rows1, rows2)
    w1, w2, o1, o2, sg, ss, og, os, gate, t1, t2, t3 = grads
    entry_grads = turned.T

    mine = pred[0].reshape(-1)
    theirs = sibling(pred[1]).reshape(-1)
    predictions = jnp.where(
        position == 0, jnp.concatenate([mine, theirs]), jnp.concatenate([theirs, mine])
    )[None]
    return (
        predictions,
        entry_grads,
        w1[None],
        w2[None],
        sg[None],
        ss[None],
        o1[None],
        o2[None],
        og,
        os,
        gate.T[None],
        t1[None],
        t2.T[None],
        t3,
    )


def solution(mesh):
    placed = (
        P("dp", None),
        P("dp", None),
        P("task", "dp"),
        P("task", None, "dp", None),
        P("task", None, "dp", None),
        P("task", None, None),
        P("task", None, None),
        P("task", "dp", None),
        P("task", "dp", None),
        P("task", None),
        P("task", None),
        P("task", None, None),
        P("task", None, None),
        P("task", None, None),
        P("task", None),
    )
    return jax.shard_map(
        per_device,
        mesh=mesh,
        in_specs=placed,
        out_specs=(
            P("task", "dp"),
            P("dp", None),
            P("task", None, "dp", None),
            P("task", None, "dp", None),
            P("task", None, None),
            P("task", None, None),
            P("task", "dp", None),
            P("task", "dp", None),
            P("task", None),
            P("task", None),
            P("task", None, None),
            P("task", None, None),
            P("task", None, None),
            P("task", None),
        ),
        check_vma=False,
    )
```

```python
import functools

import jax
import jax.numpy as jnp
from jax import lax
from jax.experimental import pallas as pl
from jax.experimental.pallas import tpu as pltpu
from jax.sharding import PartitionSpec as P

EXPERTS = 2
GATES = 4
D = 512
HID = 256
TOWER1 = 128
TOWER2 = 64
EMB = 64
FEATS = 8
LANES = 128
BAGS = 128
EVB = BAGS // FEATS
ROWS = 128
EPSILON = 1e-05
K0 = 0.7978845608028654
K1 = K0 * 0.044715
SLOTS = 3
BIG = 2 * SLOTS
WIDE = BIG * HID
PIECE = 32
BF = jnp.bfloat16
F32 = jnp.float32

T1_AT = 0
T2_AT = T1_AT + HID
GATE_AT = T2_AT + TOWER2
MISC_AT = GATE_AT + GATES * (D // LANES)
LABEL_AT = MISC_AT + 16
G_ROWS = LABEL_AT
SMALL_ROWS = G_ROWS // 2


def nn(left, right):
    return jnp.dot(left, right, preferred_element_type=F32)


def nt(left, right):
    return lax.dot_general(left, right, (((1,), (1,)), ((), ())), preferred_element_type=F32)


def tn(left, right):
    return lax.dot_general(left, right, (((0,), (0,)), ((), ())), preferred_element_type=F32)


def params(mib, **kwargs):
    return pltpu.CompilerParams(vmem_limit_bytes=mib * 1024 * 1024, **kwargs)


def cost(flops, moved):
    return pl.CostEstimate(flops=int(flops), bytes_accessed=int(moved), transcendentals=0)


def shape(dims, kind=BF):
    return jax.ShapeDtypeStruct(dims, kind)


VSPEC = pl.BlockSpec(memory_space=pltpu.VMEM)
SSPEC = pl.BlockSpec(memory_space=pltpu.SMEM)
ASPEC = pl.BlockSpec(memory_space=pl.ANY)


def line(ref, row):
    both = ref[row : row + 1, :].astype(F32)
    return [both[:, :LANES], both[:, LANES:]]


def bags_kernel(blocks, chunks, len_ref, st_ref, en_ref, meta_ref):
    k = lax.broadcasted_iota(jnp.int32, (BAGS, BAGS), 0)
    j = lax.broadcasted_iota(jnp.int32, (BAGS, BAGS), 1)
    natural = (j % EVB) * FEATS + j // EVB
    before = jnp.where(k < natural, 1.0, 0.0).astype(BF)
    same = jnp.where(k == natural, 1.0, 0.0).astype(BF)
    lens_f = jnp.concatenate(
        [len_ref[:, b * BAGS : (b + 1) * BAGS] for b in range(blocks)], axis=0
    ).astype(F32)
    lens = lens_f.astype(BF)
    in_block = nn(lens, before)
    own = nn(lens, same)
    sums = jnp.sum(lens_f, axis=1, keepdims=True)
    high = jnp.floor(sums * (1.0 / 128.0))
    low = sums - high * 128.0
    bi = lax.broadcasted_iota(jnp.int32, (blocks, blocks), 0)
    bj = lax.broadcasted_iota(jnp.int32, (blocks, blocks), 1)
    lower = jnp.where(bj < bi, 1.0, 0.0).astype(BF)
    offset = 128.0 * nn(lower, jnp.broadcast_to(high, (blocks, BAGS)).astype(BF)) + nn(
        lower, jnp.broadcast_to(low, (blocks, BAGS)).astype(BF)
    )
    starts = offset + in_block
    st_ref[pl.ds(0, blocks), :] = starts.astype(jnp.int32)
    en_ref[pl.ds(0, blocks), :] = (starts + own).astype(jnp.int32)
    past = jnp.full((8, BAGS), chunks * ROWS, jnp.int32)
    st_ref[pl.ds(blocks, 8), :] = past
    en_ref[pl.ds(blocks, 8), :] = past
    lanes = meta_ref.shape[1]
    begins = jnp.concatenate([offset] * (lanes // BAGS), axis=1)
    row = lax.broadcasted_iota(jnp.int32, (blocks, lanes), 0)
    col = lax.broadcasted_iota(jnp.int32, (blocks, lanes), 1)
    begin = jnp.sum(jnp.where(row == col, begins, 0.0), axis=0, keepdims=True)
    spot = lax.broadcasted_iota(jnp.int32, (1, lanes), 1)
    begin = jnp.where(spot >= blocks, float(chunks * ROWS), begin)
    reached = jnp.where(begins <= (col * ROWS).astype(F32), 1.0, 0.0)
    first = jnp.sum(reached, axis=0, keepdims=True) - 1.0
    meta_ref[0:1, :] = begin.astype(jnp.int32)
    meta_ref[1:2, :] = first.astype(jnp.int32)


def small_kernel(
    ids_ref,
    label_ref,
    sgain_ref,
    sshift_ref,
    ogain_ref,
    oshift_ref,
    gate_ref,
    t1_ref,
    t2_ref,
    t3_ref,
    small_ref,
):
    small_ref[T1_AT : T1_AT + HID, :] = t1_ref[...]
    small_ref[T2_AT : T2_AT + TOWER2, :] = t2_ref[...]
    gate = gate_ref[...].astype(F32)
    turned = jnp.concatenate([gate[0:2], gate[3:4], gate[2:3]], axis=0)
    gate = jnp.where(ids_ref[0] == 0, gate, turned)
    lines = [gate[g : g + 1, p * LANES : (p + 1) * LANES] for g in range(GATES) for p in range(D // LANES)]
    lines += line(sgain_ref, 0) + line(sgain_ref, 1) + line(ogain_ref, 0)
    lines += line(sshift_ref, 0) + line(sshift_ref, 1) + line(oshift_ref, 0)
    lines += [jnp.concatenate([t3_ref[...].astype(F32)] * 2, axis=1), jnp.zeros((3, LANES), F32)]
    events = label_ref.shape[1]
    lines += [label_ref[:, p * LANES : (p + 1) * LANES].astype(F32) for p in range(events // LANES)]
    lines += [jnp.zeros((16 - events // LANES, LANES), F32)]
    small_ref[pl.ds(GATE_AT, 48), :] = jnp.concatenate(lines, axis=0).astype(BF)


def bags(lengths, chunks):
    blocks = lengths.shape[1] // BAGS
    lanes = -(-max(blocks + 1, chunks) // LANES) * LANES
    bounds = shape((blocks + 8, BAGS), jnp.int32)
    return pl.pallas_call(
        functools.partial(bags_kernel, blocks, chunks),
        out_shape=(bounds, bounds, shape((2, lanes), jnp.int32)),
        in_specs=[VSPEC],
        out_specs=(VSPEC,) * 3,
        compiler_params=params(4),
        cost_estimate=cost(1e9, 1e6),
    )(lengths)


def pack_small(ids, *arrays):
    return pl.pallas_call(
        small_kernel,
        out_shape=shape((LABEL_AT + 16, LANES)),
        in_specs=[SSPEC] + [VSPEC] * len(arrays),
        out_specs=VSPEC,
        compiler_params=params(56),
        cost_estimate=cost(1e9, 1e6),
    )(ids, *arrays)


def one_hot(starts, ends, base):
    row = lax.broadcasted_iota(jnp.int32, (ROWS, 2 * BAGS), 0).astype(F32).astype(BF)
    low = jnp.clip(starts - base, 0, ROWS).astype(F32).astype(BF)
    high = jnp.clip(ends - base, 0, ROWS).astype(F32).astype(BF)
    return jnp.where((row >= low) & (row < high), jnp.ones((), BF), jnp.zeros((), BF))


def window(ref, block):
    first = ref[pl.ds(block, 1), :]
    second = ref[pl.ds(block + 1, 1), :]
    return jnp.concatenate([first, second], axis=1)


def pool_kernel(skip, count, half_blocks, chunks, ids_ref, meta_ref, st_ref, en_ref, ent_ref, *refs):
    x_ref, acc_ref = refs[-2:]
    base_block = ids_ref[0] * half_blocks + skip

    def clear(i, carry):
        at = pl.multiple_of((base_block + i) * BAGS, BAGS)
        acc_ref[:, pl.ds(at, BAGS)] = jnp.zeros((EMB, BAGS), F32)
        return carry

    lax.fori_loop(0, count, clear, 0, unroll=True)

    low_chunk = meta_ref[0, base_block] // ROWS
    high_chunk = (meta_ref[0, base_block + count] + ROWS - 1) // ROWS
    step = 9

    def chunk(i, carry):
        for u in range(step):
            c = low_chunk + i * step + u
            inside = jnp.minimum(c, chunks - 1)
            block = meta_ref[1, inside]
            at = pl.multiple_of(inside * ROWS, ROWS)
            picked = one_hot(window(st_ref, block), window(en_ref, block), c * ROWS)
            part = nn(ent_ref[:, pl.ds(at, ROWS)], picked)
            to = pl.multiple_of(block * BAGS, BAGS)
            acc_ref[:, pl.ds(to, 2 * BAGS)] += part
        return carry

    lax.fori_loop(0, (high_chunk - low_chunk + step - 1) // step, chunk, 0)

    def place(i, carry):
        at = pl.multiple_of((base_block + i) * BAGS, BAGS)
        to = pl.multiple_of(i * EVB, EVB)
        block = acc_ref[:, pl.ds(at, BAGS)].T
        for pair in range(FEATS // 2):
            left = block[2 * pair * EVB : (2 * pair + 1) * EVB]
            right = block[(2 * pair + 1) * EVB : (2 * pair + 2) * EVB]
            x_ref[pl.ds(to, EVB), pair * 2 * EMB : (pair + 1) * 2 * EMB] = jnp.concatenate(
                [left, right], axis=1
            ).astype(BF)
        return carry

    lax.fori_loop(0, count, place, 0, unroll=12)


def pool(part, parts, ids, meta, starts, ends, entries, *after):
    blocks = starts.shape[0] - 8
    half_blocks = blocks // 2
    count = half_blocks // parts
    chunks = entries.shape[1] // ROWS
    return pl.pallas_call(
        functools.partial(pool_kernel, part * count, count, half_blocks, chunks),
        out_shape=shape((count * EVB, D)),
        in_specs=[SSPEC, SSPEC, VSPEC, VSPEC, VSPEC] + [ASPEC] * len(after),
        out_specs=VSPEC,
        scratch_shapes=[pltpu.VMEM((EMB, (blocks + 1) * BAGS), F32)],
        compiler_params=params(16),
        cost_estimate=cost(10e9, 5e6),
    )(ids, meta, starts, ends, entries, *after)


def expand_kernel(half_blocks, group, ids_ref, meta_ref, st_ref, en_ref, own_ref, other_ref, out_ref, pred_ref, token_ref, rows_ref):
    position = ids_ref[0]
    step = pl.program_id(0)
    events = half_blocks * EVB

    @pl.when(step == 0)
    def _():
        for source, half in ((own_ref, position), (other_ref, 1 - position)):

            def place(i, carry):
                at = pl.multiple_of(i * EVB, EVB)
                to = pl.multiple_of((half * half_blocks + i) * BAGS, BAGS)
                for pair in range(FEATS // 2):
                    tile = source[pl.ds(at, EVB), pair * 2 * EMB : (pair + 1) * 2 * EMB]
                    rows_ref[pl.ds(to + 2 * pair * EVB, EVB), :] = tile[:, :EMB]
                    rows_ref[pl.ds(to + (2 * pair + 1) * EVB, EVB), :] = tile[:, EMB:]
                return carry

            lax.fori_loop(0, half_blocks, place, 0, unroll=12)
        rows_ref[pl.ds(2 * half_blocks * BAGS, BAGS), :] = jnp.zeros((BAGS, EMB), BF)
        own = own_ref[events : events + 16, : 2 * LANES].astype(F32)
        other = other_ref[events : events + 16, : 2 * LANES].astype(F32)
        mine = (own[:, :LANES] + own[:, LANES:])[:8]
        theirs = (other[:, :LANES] + other[:, LANES:])[8:]
        halves = (jnp.where(position == 0, mine, theirs), jnp.where(position == 0, theirs, mine))
        tiles = events // LANES
        token_ref[...] = mine
        pred_ref[...] = jnp.concatenate([half[k : k + 1] for half in halves for k in range(tiles)], axis=1)

    for u in range(group):
        c = step * group + u
        block = meta_ref[1, c]
        picked = one_hot(window(st_ref, block), window(en_ref, block), c * ROWS)
        at = pl.multiple_of(block * BAGS, BAGS)
        out_ref[:, u * ROWS : (u + 1) * ROWS] = nn(picked, rows_ref[pl.ds(at, 2 * BAGS), :]).astype(BF).T


def expand(ids, meta, starts, ends, own, other, rows):
    blocks = starts.shape[0] - 8
    chunks = rows // ROWS
    group = 36
    while chunks % group:
        group -= 1
    return pl.pallas_call(
        functools.partial(expand_kernel, blocks // 2, group),
        grid=(chunks // group,),
        out_shape=(shape((EMB, rows)), shape((1, blocks * EVB), F32), shape((8, LANES), F32)),
        in_specs=[SSPEC, SSPEC, VSPEC, VSPEC, VSPEC, VSPEC],
        out_specs=(
            pl.BlockSpec((EMB, group * ROWS), lambda i: (0, i)),
            pl.BlockSpec((1, blocks * EVB), lambda i: (0, 0)),
            pl.BlockSpec((8, LANES), lambda i: (0, 0)),
        ),
        scratch_shapes=[pltpu.VMEM(((blocks + 1) * BAGS, EMB), BF)],
        compiler_params=params(24, dimension_semantics=("arbitrary",)),
        cost_estimate=cost(12e9, 6e6),
    )(ids, meta, starts, ends, own, other)


def gelu_twice(v):
    cube = K1 * (v * v)
    bend = jnp.tanh(v * (cube + K0))
    rise = 1.0 + bend
    act = v * rise
    slope = rise + act * (1.0 - bend) * (3.0 * cube + K0)
    return act, slope


def gelu_both(v):
    act, slope = gelu_twice(v)
    return 0.5 * act, 0.5 * slope


def wide(block, row):
    return jnp.concatenate([block[row : row + 1, :], block[row + 1 : row + 2, :]], axis=1)


def by_eight(value):
    return jnp.sum(value.reshape(-1, 8, value.shape[-1]), axis=0)


def plus(total, term):
    return term if total is None else total + term


def pieces_of(m):
    return [slice(at, at + PIECE) for at in range(m * HID, (m + 1) * HID, PIECE)]


def col_sum(value):
    return jnp.sum(value, axis=0, keepdims=True)


def lane_tiles(events, body):
    def step(j, carry):
        body(j, pl.ds(pl.multiple_of(j * LANES, LANES), LANES))
        return carry

    lax.fori_loop(0, events // LANES, step, 0)


def main_kernel(xs, groups, plan, rows1, rows2, ids_ref, *refs):
    refs = list(refs)
    take = lambda n: [refs.pop(0) for _ in range(n)]
    x_parts = take(xs)
    own_groups, oth_groups = take(groups), take(groups)
    packs = take(2)
    (dx_ref,) = take(1)
    own_outs, oth_outs = take(len(plan)), take(len(plan))
    x_ref, wc_ref, w2_ref, gain_ref, third_ref, lab_ref, pc_ref, pb_ref, s2_ref, y_ref, h_ref, e_ref, fc_ref = take(13)
    scale_ref, lg_ref, prob_ref, q_ref, pt_ref, u1_ref, p4_ref, e2_ref, e1_ref, du_ref, dm_ref, dmb_ref, ds_ref, dn_ref, acc3_ref, pred_ref, g1_ref, g2_ref = take(18)
    position = ids_ref[0]
    events = x_ref.shape[1]
    quarter = D // rows1 // 4

    def part(m):
        return slice(m * HID, (m + 1) * HID)

    def rows_of(t, p):
        if not quarter:
            return pl.ds(0, rows1), pl.ds(0, rows2)
        where = position if t == 0 else 1 - position
        d = ids_ref[1] ^ (4 * (p % quarter))
        if (p // quarter) & 1:
            d = d ^ (2 - where)
        if p // quarter >= 2:
            d = d ^ (1 + where)
        return (
            pl.ds(pl.multiple_of(d * rows1, rows1), rows1),
            pl.ds(pl.multiple_of(d * rows2, rows2), rows2),
        )

    size = events // xs
    for k, piece in enumerate(x_parts):
        x_ref[:, k * size : (k + 1) * size] = piece[...].T
    for t, whole in enumerate((own_groups, oth_groups)):
        p = 0
        for group in whole:
            for g in range(group.shape[0]):
                one, two = rows_of(t, p)
                p += 1
                for s in range(SLOTS):
                    wc_ref[one, part(t * SLOTS + s)] = group[g, s * rows1 : (s + 1) * rows1, :]
                    low = SLOTS * rows1 + s * rows2
                    w2_ref[t * SLOTS + s, two, :] = (0.5 * group[g, low : low + rows2, :].astype(F32)).astype(BF)
    lines = []
    for t in range(2):
        block = packs[t][GATE_AT : GATE_AT + 16, :].astype(F32)
        for g in range(GATES):
            lines.append(
                jnp.concatenate([block[4 * g + p : 4 * g + p + 1, :] for p in range(D // LANES)], axis=1)
            )
        lines.append(jnp.zeros((8 - GATES, D), F32))
    gates = jnp.concatenate(lines, axis=0).astype(BF)
    wc_ref[:, WIDE:] = jnp.concatenate([gates, jnp.zeros((LANES - 16, D), BF)], axis=0).T
    fc_ref[WIDE:, :] = jnp.zeros((LANES, events), BF)
    acc3_ref[...] = jnp.zeros_like(acc3_ref)
    miscs = [packs[t][MISC_AT : MISC_AT + 16, :].astype(F32) for t in range(2)]
    for t in range(2):
        misc = miscs[t]
        for s in range(SLOTS):
            for kind in range(2):
                for half in range(2):
                    at = 2 * (kind * SLOTS + s) + half
                    to = ((kind * 2 + t) * SLOTS + s) * HID + half * LANES
                    gain_ref[to : to + LANES, :] = jnp.broadcast_to(misc[at : at + 1, :], (LANES, LANES)).T
        third = jnp.broadcast_to(misc[12:13, :], (LANES, LANES)).T
        third_ref[t * TOWER2 : (t + 1) * TOWER2, :] = third[:TOWER2]
        lab_ref[t * 16 : (t + 1) * 16, :] = packs[t][LABEL_AT : LABEL_AT + 16, :].astype(F32)

    for m in range(BIG):
        pc_ref[part(m), :] = tn(wc_ref[:, part(m)], x_ref[...])
    lg_ref[...] = nn(gates, x_ref[...])

    def first_gelu(j, here):
        for m in range(BIG):
            for rows in pieces_of(m):
                act, slope = gelu_twice(pc_ref[rows, here])
                pc_ref[rows, here] = slope
                h_ref[rows, here] = act.astype(BF)

    lane_tiles(events, first_gelu)
    for m in range(BIG):
        pb_ref[part(m), :] = tn(w2_ref[m], h_ref[part(m), :])

    def second_gelu(j, here):
        def front(m):
            total = None
            for rows in pieces_of(m):
                act, slope = gelu_twice(pb_ref[rows, here])
                pb_ref[rows, here] = act
                s2_ref[rows, here] = slope
                total = plus(total, by_eight(act))
            return col_sum(total) * (1.0 / HID)

        def back(m, mean):
            total = None
            for rows in pieces_of(m):
                centred = pb_ref[rows, here] - mean
                pb_ref[rows, here] = centred
                total = plus(total, by_eight(centred * centred))
            scale = lax.rsqrt(col_sum(total) * (1.0 / HID) + 4.0 * EPSILON)
            scale_ref[m : m + 1, here] = scale
            for rows in pieces_of(m):
                normed = pb_ref[rows, here] * scale
                pb_ref[rows, here] = normed
                out = normed * gain_ref[rows, :] + gain_ref[slice(WIDE + rows.start, WIDE + rows.stop), :]
                if m % SLOTS == SLOTS - 1:
                    out = out.astype(BF).astype(F32)
                y_ref[rows, here] = out

        means = front(0)
        for m in range(BIG):
            ahead = front(m + 1) if m + 1 < BIG else None
            back(m, means)
            means = ahead

    lane_tiles(events, second_gelu)
    orders = [(t * SLOTS, t * SLOTS + 1, t * SLOTS + 2, (1 - t) * SLOTS + 2) for t in range(2)]

    prob_ref[...] = jnp.ones_like(prob_ref)

    def mix(j, here):
        for t in range(2):
            logits = [lg_ref[8 * t + k : 8 * t + k + 1, here] for k in range(GATES)]
            top = jnp.maximum(jnp.maximum(logits[0], logits[1]), jnp.maximum(logits[2], logits[3]))
            raised = [jnp.exp(logit - top) for logit in logits]
            scale = 1.0 / (raised[0] + raised[1] + raised[2] + raised[3])
            mixture = None
            for k in range(GATES):
                prob = raised[k] * scale
                prob_ref[8 * t + k : 8 * t + k + 1, here] = prob
                term = prob * y_ref[part(orders[t][k]), here]
                mixture = term if mixture is None else mixture + term
            q_ref[part(t), here] = mixture.astype(BF)

    lane_tiles(events, mix)
    for t in range(2):
        pt_ref[t * TOWER1 : (t + 1) * TOWER1, :] = tn(packs[t][T1_AT : T1_AT + HID, :], q_ref[part(t), :])

    def tower_gelu(j, here):
        act, slope = gelu_both(pt_ref[:, here])
        pt_ref[:, here] = slope
        u1_ref[:, here] = act.astype(BF)

    lane_tiles(events, tower_gelu)
    for t in range(2):
        p4_ref[t * TOWER2 : (t + 1) * TOWER2, :] = nn(
            packs[t][T2_AT : T2_AT + TOWER2, :], u1_ref[t * TOWER1 : (t + 1) * TOWER1, :]
        )

    def head(j, here):
        act, slope = gelu_both(p4_ref[:, here])
        u2 = act.astype(BF).astype(F32)
        product = u2 * third_ref[...]
        deltas = []
        for t in range(2):
            logit = col_sum(product[t * TOWER2 : (t + 1) * TOWER2])
            prediction = 1.0 / (1.0 + jnp.exp(-logit))
            pred_ref[pl.ds(8 * t + j, 1), :] = prediction
            label = lab_ref[pl.ds(t * 16 + position * (events // LANES) + j, 1), :]
            deltas.append(jnp.broadcast_to(prediction - label, (TOWER2, LANES)))
        delta = jnp.concatenate(deltas, axis=0)
        acc3_ref[...] += delta * u2
        e2_ref[:, here] = (slope * (delta * third_ref[...])).astype(BF)

    lane_tiles(events, head)
    for t in range(2):
        du_ref[t * TOWER1 : (t + 1) * TOWER1, :] = tn(
            packs[t][T2_AT : T2_AT + TOWER2, :], e2_ref[t * TOWER2 : (t + 1) * TOWER2, :]
        )

    def tower_back(j, here):
        e1_ref[:, here] = (pt_ref[:, here] * du_ref[:, here]).astype(BF)

    lane_tiles(events, tower_back)
    for t in range(2):
        mixed = nn(packs[t][T1_AT : T1_AT + HID, :], e1_ref[t * TOWER1 : (t + 1) * TOWER1, :])
        dm_ref[part(t), :] = mixed
        dmb_ref[part(t), :] = mixed.astype(BF)
        rows = [wide(miscs[t], 2 * (SLOTS + s)) for s in range(EXPERTS)] + [jnp.zeros((8 - EXPERTS, HID), F32)]
        ds_ref[8 * t : 8 * t + 8, :] = nn(jnp.concatenate(rows, axis=0).astype(BF), dmb_ref[part(t), :])

    def mix_back(j, here):
        probs = [[prob_ref[8 * t + k : 8 * t + k + 1, here] for k in range(GATES)] for t in range(2)]
        d_probs = [[None] * GATES for _ in range(2)]
        for t in range(2):
            for k in range(EXPERTS, GATES):
                total = None
                for mine, rows in zip(pieces_of(t), pieces_of(orders[t][k])):
                    total = plus(total, by_eight(dm_ref[mine, here] * y_ref[rows, here]))
                d_probs[t][k] = col_sum(total)

        def turned_gain(m, rows):
            t, s = divmod(m, SLOTS)
            mine = slice(rows.start - m * HID + t * HID, rows.stop - m * HID + t * HID)
            up = dm_ref[mine, here]
            if s == SLOTS - 1:
                theirs = slice(mine.start + (1 - 2 * t) * HID, mine.stop + (1 - 2 * t) * HID)
                up = probs[t][s] * up + probs[1 - t][SLOTS] * dm_ref[theirs, here]
            return up * gain_ref[rows, :]

        def front(m):
            one, two = None, None
            for rows in pieces_of(m):
                d_normed = turned_gain(m, rows)
                y_ref[rows, here] = d_normed
                product = d_normed * pb_ref[rows, here]
                dn_ref[rows, here] = product.astype(BF)
                one = plus(one, by_eight(d_normed))
                two = plus(two, by_eight(product))
            return col_sum(one), col_sum(two)

        def back(m, one, two):
            t, s = divmod(m, SLOTS)
            one, two = one * (1.0 / HID), two * (1.0 / HID)
            outer = scale_ref[m : m + 1, here]
            if s < EXPERTS:
                outer = outer * probs[t][s]
            for rows in pieces_of(m):
                inner = y_ref[rows, here] - one - pb_ref[rows, here] * two
                e_ref[rows, here] = (s2_ref[rows, here] * outer * inner).astype(BF)

        sums = front(0)
        for m in range(BIG):
            ahead = front(m + 1) if m + 1 < BIG else None
            t, s = divmod(m, SLOTS)
            if s < EXPERTS:
                d_probs[t][s] = sums[1] + ds_ref[8 * t + s : 8 * t + s + 1, here]
            back(m, *sums)
            sums = ahead
        codes = []
        for t in range(2):
            weighted = probs[t][0] * d_probs[t][0]
            for k in range(1, GATES):
                weighted = weighted + probs[t][k] * d_probs[t][k]
            codes += [probs[t][k] * (d_probs[t][k] - weighted) for k in range(GATES)]
            codes.append(jnp.zeros((8 - GATES, LANES), F32))
        fc_ref[WIDE : WIDE + 16, here] = jnp.concatenate(codes, axis=0).astype(BF)

    lane_tiles(events, mix_back)
    for m in range(BIG):
        s2_ref[part(m), :] = nn(w2_ref[m], e_ref[part(m), :])

    def first_back(j, here):
        for m in range(BIG):
            fc_ref[part(m), here] = (pc_ref[part(m), here] * s2_ref[part(m), here]).astype(BF)

    lane_tiles(events, first_back)
    dx_ref[:events, :] = nn(wc_ref[...], fc_ref[...]).astype(BF).T
    pred = pred_ref[...]
    high = pred.astype(BF)
    low = (pred - high.astype(F32)).astype(BF)
    dx_ref[events:, :] = jnp.concatenate([high, low, high, low], axis=1)

    gate_grad = nt(fc_ref[WIDE : WIDE + 16, :], x_ref[...])
    weights = prob_ref[...].astype(BF)
    shifts = [nt(weights, dmb_ref[part(t), :]) for t in range(2)]
    third_grad = col_sum(acc3_ref[...].T)
    for t, results in enumerate((own_outs, oth_outs)):
        for s in range(SLOTS):
            m = t * SLOTS + s
            g1_ref[...] = nt(x_ref[...], fc_ref[part(m), :])
            g2_ref[...] = nt(h_ref[part(m), :], e_ref[part(m), :])
            p = 0
            for out, (pieces, small_first) in zip(results, plan):
                for g in range(pieces):
                    one, two = rows_of(t, p)
                    p += 1
                    at = g * SLOTS * (rows1 + rows2) + (SMALL_ROWS if small_first else 0)
                    out[at + s * rows1 : at + (s + 1) * rows1, :] = g1_ref[one, :].astype(BF)
                    at = at + SLOTS * rows1 + s * rows2
                    out[at : at + rows2, :] = (0.5 * g2_ref[two, :]).astype(BF)
        tower = slice(t * TOWER1, (t + 1) * TOWER1)
        half = slice(t * TOWER2, (t + 1) * TOWER2)
        lines = []
        for g in range(GATES):
            row = gate_grad[8 * t + g : 8 * t + g + 1, :]
            lines += [row[:, p * LANES : (p + 1) * LANES] for p in range(D // LANES)]
        for s in range(SLOTS):
            at = 8 * t + (s if s < EXPERTS else GATES)
            row = nt(weights, dn_ref[part(t * SLOTS + s), :])[at : at + 1, :] / wide(miscs[t], 2 * s)
            lines += [row[:, :LANES], row[:, LANES:]]
        for s in range(SLOTS):
            row = shifts[t][8 * t + s : 8 * t + s + 1, :]
            if s == SLOTS - 1:
                row = row + shifts[1 - t][8 * (1 - t) + SLOTS : 8 * (1 - t) + SLOTS + 1, :]
            lines += [row[:, :LANES], row[:, LANES:]]
        lines.append(third_grad if t == 0 else pltpu.roll(third_grad, TOWER2, 1))
        lines.append(jnp.zeros((3, LANES), F32))
        small = jnp.concatenate(
            [
                nt(q_ref[part(t), :], e1_ref[tower, :]),
                nt(e2_ref[half, :], u1_ref[tower, :]),
                jnp.concatenate(lines, axis=0),
            ],
            axis=0,
        )
        small = jnp.concatenate([small[:SMALL_ROWS], small[SMALL_ROWS:]], axis=1).astype(BF)
        for out, (_, small_first) in zip(results, plan):
            if small_first:
                out[:SMALL_ROWS, :] = small


def layer(ids, x_parts, own_groups, oth_groups, own_pack, oth_pack, plan, rows1, rows2):
    events = sum(part.shape[0] for part in x_parts)
    rows = SLOTS * (rows1 + rows2)
    grads = tuple(shape((pieces * rows + small * SMALL_ROWS, HID)) for pieces, small in plan)
    results = (shape((events + 16, D)),) + grads + grads
    scratch = [
        ((D, events), BF),
        ((D, WIDE + LANES), BF),
        ((BIG, HID, HID), BF),
        ((2 * WIDE, LANES), F32),
        ((2 * TOWER2, LANES), F32),
        ((32, LANES), F32),
        ((WIDE, events), F32),
        ((WIDE, events), F32),
        ((WIDE, events), F32),
        ((WIDE, events), F32),
        ((WIDE, events), BF),
        ((WIDE, events), BF),
        ((WIDE + LANES, events), BF),
        ((8, events), F32),
        ((16, events), F32),
        ((16, events), F32),
        ((2 * HID, events), BF),
        ((2 * TOWER1, events), F32),
        ((2 * TOWER1, events), BF),
        ((2 * TOWER2, events), F32),
        ((2 * TOWER2, events), BF),
        ((2 * TOWER1, events), BF),
        ((2 * TOWER1, events), F32),
        ((2 * HID, events), F32),
        ((2 * HID, events), BF),
        ((16, events), F32),
        ((WIDE, events), BF),
        ((2 * TOWER2, LANES), F32),
        ((16, LANES), F32),
        ((D, HID), F32),
        ((HID, HID), F32),
    ]
    arrays = [*x_parts, *own_groups, *oth_groups, own_pack, oth_pack]
    dx, *grads = pl.pallas_call(
        functools.partial(main_kernel, len(x_parts), len(own_groups), plan, rows1, rows2),
        out_shape=results,
        in_specs=[SSPEC] + [VSPEC] * len(arrays),
        out_specs=(VSPEC,) * len(results),
        scratch_shapes=[pltpu.VMEM(dims, kind) for dims, kind in scratch],
        compiler_params=params(46),
        cost_estimate=cost(events * BIG * 196608 * 6, 10e6),
    )(ids, *arrays)
    return dx, grads[: len(plan)], grads[len(plan) :]


def sibling(value):
    return lax.ppermute(value, "task", [(0, 1), (1, 0)])


def flipped(value, mask):
    pairs = [(i, i ^ mask) for i in range(lax.axis_size("dp"))]
    return lax.ppermute(value, "dp", pairs)


def crossed(value, masks):
    n = lax.axis_size("dp")
    pairs = [(t * n + i, t * n + (i ^ masks[t])) for t in range(2) for i in range(n)]
    return lax.ppermute(value, ("task", "dp"), pairs)


def stack_kernel(count, *refs):
    out, sems = refs[-2:]
    copies = [pltpu.make_async_copy(refs[k], out.at[k], sems.at[k]) for k in range(count)]
    for copy in copies:
        copy.start()
    for copy in copies:
        copy.wait()


def stacked(pieces):
    return pl.pallas_call(
        functools.partial(stack_kernel, len(pieces)),
        out_shape=shape((len(pieces),) + pieces[0].shape, pieces[0].dtype),
        in_specs=[ASPEC] * len(pieces),
        out_specs=VSPEC,
        scratch_shapes=[pltpu.SemaphoreType.DMA((len(pieces),))],
        compiler_params=params(4),
        cost_estimate=cost(0, 1e6),
    )(*pieces)


def summed(*terms):
    total = terms[0].astype(F32)
    for term in terms[1:]:
        total = total + term.astype(F32)
    return total.astype(BF)


def small_sum_kernel(one_ref, two_ref, out_ref):
    out_ref[...] = (one_ref[...].astype(F32) + two_ref[...].astype(F32)).astype(BF)


def small_sum(one, two):
    lead = pl.BlockSpec((SMALL_ROWS, HID), lambda i: (0, 0))
    return pl.pallas_call(
        small_sum_kernel,
        grid=(1,),
        out_shape=shape((SMALL_ROWS, HID)),
        in_specs=[lead, lead],
        out_specs=lead,
        compiler_params=params(4),
        cost_estimate=cost(8e9, 1e6),
    )(one, two)


def tie_kernel(*refs):
    pass


def tied(value, after):
    return pl.pallas_call(
        tie_kernel,
        out_shape=shape(value.shape, value.dtype),
        in_specs=[ASPEC, ASPEC],
        out_specs=ASPEC,
        input_output_aliases={0: 0},
        compiler_params=params(1),
        cost_estimate=cost(0, 1),
    )(value, after)


def far_kernel(quarter, rows, keep_ref, got_ref, mid_ref, near_ref, *outs):
    for k, out in enumerate(outs):
        here = slice(k * rows, (k + 1) * rows)
        total = keep_ref[here, :].astype(F32) + got_ref[here, :].astype(F32)
        at = SMALL_ROWS + k * rows
        total = total + mid_ref[at : at + rows, :].astype(F32)
        out[...] = (total + near_ref[here, :].astype(F32)).astype(BF)


def far_messages(quarter, rows, keep, got, mid, near):
    def lead(size):
        return pl.BlockSpec((size, HID), lambda i: (0, 0))

    size = quarter * rows
    return pl.pallas_call(
        functools.partial(far_kernel, quarter, rows),
        grid=(1,),
        out_shape=(shape((rows, HID)),) * quarter,
        in_specs=[lead(size), lead(size), lead(size + SMALL_ROWS), lead(size)],
        out_specs=(lead(rows),) * quarter,
        compiler_params=params(12),
        cost_estimate=cost(0, 4e6),
    )(keep, got, mid, near)


def last_kernel(count, rows1, rows2, *refs):
    total = refs[0][...].astype(F32)
    for k in range(1, count):
        total = total + refs[k][...].astype(F32)
    w1_ref, w2_ref, o1_ref, o2_ref, token_ref = refs[count:]
    token_ref[...] = total[:8, :LANES]
    cut = SLOTS * rows1
    for s in range(EXPERTS):
        w1_ref[s] = total[s * rows1 : (s + 1) * rows1]
        w2_ref[s] = total[cut + s * rows2 : cut + (s + 1) * rows2]
    o1_ref[...] = total[EXPERTS * rows1 : cut]
    o2_ref[...] = total[cut + EXPERTS * rows2 :]


def finish(parts, rows1, rows2):
    outs = (
        shape((EXPERTS, rows1, HID), F32),
        shape((EXPERTS, rows2, HID), F32),
        shape((rows1, HID), F32),
        shape((rows2, HID), F32),
        shape((8, LANES), F32),
    )
    return pl.pallas_call(
        functools.partial(last_kernel, len(parts), rows1, rows2),
        out_shape=outs,
        in_specs=[VSPEC] * len(parts),
        out_specs=(VSPEC,) * len(outs),
        compiler_params=params(8),
        cost_estimate=cost(10e9, 2e6),
    )(*parts)


def last_small_kernel(count, ids_ref, *refs):
    small = refs[0][...].astype(F32)
    for k in range(1, count):
        small = small + refs[k][...].astype(F32)
    sg_ref, ss_ref, og_ref, os_ref, gate_ref, t1_ref, t2_ref, t3_ref = refs[-8:]
    tiny = jnp.concatenate([small[:, :LANES], small[:, LANES:]], axis=0)
    t1_ref[...] = tiny[T1_AT : T1_AT + HID]
    t2_ref[...] = tiny[T2_AT : T2_AT + TOWER2]
    gates = []
    for g in range(GATES):
        at = GATE_AT + 4 * g
        gates.append(jnp.concatenate([tiny[at + p : at + p + 1] for p in range(D // LANES)], axis=1))
    turned = ids_ref[0] != 0
    gate_ref[0:1, :] = gates[0]
    gate_ref[1:2, :] = gates[1]
    gate_ref[2:3, :] = jnp.where(turned, gates[3], gates[2])
    gate_ref[3:4, :] = jnp.where(turned, gates[2], gates[3])
    for kind, (spec, own) in enumerate(((sg_ref, og_ref), (ss_ref, os_ref))):
        for s in range(SLOTS):
            at = MISC_AT + 2 * (kind * SLOTS + s)
            row = jnp.concatenate([tiny[at : at + 1], tiny[at + 1 : at + 2]], axis=1)
            if s < EXPERTS:
                spec[s : s + 1, :] = row
            else:
                own[...] = row
    t3_ref[...] = tiny[MISC_AT + 12 : MISC_AT + 13, :TOWER2]


def finish_small(ids, parts, after):
    outs = (
        shape((EXPERTS, HID), F32),
        shape((EXPERTS, HID), F32),
        shape((1, HID), F32),
        shape((1, HID), F32),
        shape((GATES, D), F32),
        shape((HID, TOWER1), F32),
        shape((TOWER2, TOWER1), F32),
        shape((1, TOWER2), F32),
    )
    return pl.pallas_call(
        functools.partial(last_small_kernel, len(parts)),
        out_shape=outs,
        in_specs=[SSPEC] + [VSPEC] * len(parts) + [ASPEC],
        out_specs=(VSPEC,) * len(outs),
        compiler_params=params(8),
        cost_estimate=cost(0, 2e6),
    )(ids, *parts, after)


def per_device(
    entries,
    lengths,
    labels,
    spec_w1,
    spec_w2,
    spec_gain,
    spec_shift,
    shared_w1,
    shared_w2,
    shared_gain,
    shared_shift,
    gate_w,
    tower_w1,
    tower_w2,
    tower_w3,
):
    position = lax.axis_index("task")
    n = lax.axis_size("dp")
    ids = jnp.stack([position, lax.axis_index("dp")]).astype(jnp.int32)
    rows1, rows2 = spec_w1.shape[2], spec_w2.shape[2]
    direct = rows2 % 16 == 0 and n % 4 == 0 and n & (n - 1) == 0
    pack = jnp.concatenate(
        [part.reshape(-1, HID) for part in (spec_w1, shared_w1, spec_w2, shared_w2)], axis=0
    )
    if direct:
        quarter = n // 4
        far = [pack] + [flipped(pack, 4 * k) for k in range(1, quarter)]

    rows = entries.shape[0]
    starts, ends, meta = bags(lengths, rows // ROWS)
    small = pack_small(
        ids,
        labels,
        spec_gain[0],
        spec_shift[0],
        shared_gain,
        shared_shift,
        gate_w[0].T,
        tower_w1[0],
        tower_w2[0].T,
        tower_w3,
    )
    other_small = sibling(small)
    turned = entries.T
    x_first = pool(0, 2, ids, meta, starts, ends, turned, small)

    if direct:
        zc = stacked(far)
        r1 = tied(crossed(zc, (1, 2)), x_first)
        r2 = crossed(zc, (2, 1))
        x_second = pool(1, 2, ids, meta, starts, ends, turned, r2)
        r3 = tied(crossed(r1, (2, 1)), x_second)
        own = [zc, r2, r1, r3]
        plan, used1, used2 = ((2 * quarter, 0), (2 * quarter, 1)), rows1, rows2
    else:
        x_second = pool(1, 2, ids, meta, starts, ends, turned)
        every = lax.all_gather(pack, "dp", axis=0)
        cut = SLOTS * rows1
        w1 = every[:, :cut].reshape(n, SLOTS, rows1, HID).swapaxes(0, 1).reshape(-1, HID)
        w2 = every[:, cut:].reshape(n, SLOTS, rows2, HID).swapaxes(0, 1).reshape(-1, HID)
        own = [jnp.concatenate([w1, w2], axis=0)[None]]
        plan, used1, used2 = ((1, 1),), D, HID
    dx, own_grads, oth_grads = layer(
        ids, [x_first, x_second], own, [sibling(group) for group in own], small, other_small, plan, used1, used2
    )

    got = [sibling(grad) for grad in oth_grads[::-1]][::-1]
    other_dx = sibling(dx)
    turned, predictions, expanded = expand(ids, meta, starts, ends, dx, other_dx, rows)
    piece = SLOTS * (rows1 + rows2)
    if direct:
        keep, send = own_grads
        send = summed(send, got[1])
        mid = tied(crossed(send, (1, 2)), expanded)
        cut = quarter * piece
        small = small_sum(send, mid)
        send = summed(keep[cut:], got[0][cut:], mid[SMALL_ROWS + cut :])
        near = crossed(send, (2, 1))
        parts = far_messages(quarter, piece, keep, got[0], mid, near)
        smalls = [small] + [tied(flipped(small, 4 * k), parts[0]) for k in range(1, quarter)]
        parts = [parts[0]] + [flipped(parts[k], 4 * k) for k in range(1, quarter)]
        small = summed(*smalls)
        *grads, summed_up = finish(parts, rows1, rows2)
        grads += finish_small(ids, [small, crossed(small, (2, 1))], summed_up)
    else:
        whole = own_grads[0].astype(F32) + got[0].astype(F32)
        small = lax.psum(whole[:SMALL_ROWS], "dp")
        whole = whole[SMALL_ROWS:]
        cut = SLOTS * D
        g1 = lax.psum_scatter(whole[:cut].reshape(SLOTS, D, HID), "dp", scatter_dimension=1, tiled=True)
        g2 = lax.psum_scatter(whole[cut:].reshape(SLOTS, HID, HID), "dp", scatter_dimension=1, tiled=True)
        part = jnp.concatenate([g1.reshape(-1, HID), g2.reshape(-1, HID)], axis=0)
        *grads, summed_up = finish([part], rows1, rows2)
        grads += finish_small(ids, [small], summed_up)
    w1, w2, o1, o2, sg, ss, og, os, gate, t1, t2, t3 = grads
    entry_grads = turned.T
    return (
        predictions,
        entry_grads,
        w1[None],
        w2[None],
        sg[None],
        ss[None],
        o1[None],
        o2[None],
        og,
        os,
        gate.T[None],
        t1[None],
        t2.T[None],
        t3,
    )


def solution(mesh):
    placed = (
        P("dp", None),
        P("dp", None),
        P("task", "dp"),
        P("task", None, "dp", None),
        P("task", None, "dp", None),
        P("task", None, None),
        P("task", None, None),
        P("task", "dp", None),
        P("task", "dp", None),
        P("task", None),
        P("task", None),
        P("task", None, None),
        P("task", None, None),
        P("task", None, None),
        P("task", None),
    )
    return jax.shard_map(
        per_device,
        mesh=mesh,
        in_specs=placed,
        out_specs=(
            P("task", "dp"),
            P("dp", None),
            P("task", None, "dp", None),
            P("task", None, "dp", None),
            P("task", None, None),
            P("task", None, None),
            P("task", "dp", None),
            P("task", "dp", None),
            P("task", None),
            P("task", None),
            P("task", None, None),
            P("task", None, None),
            P("task", None, None),
            P("task", None),
        ),
        check_vma=False,
    )
```

```python
import functools

import jax
import jax.numpy as jnp
from jax import lax
from jax.experimental import pallas as pl
from jax.experimental.pallas import tpu as pltpu
from jax.sharding import PartitionSpec as P

EXPERTS = 2
GATES = 4
D = 512
HID = 256
TOWER1 = 128
TOWER2 = 64
EMB = 64
FEATS = 8
LANES = 128
BAGS = 128
EVB = BAGS // FEATS
ROWS = 128
EPSILON = 1e-05
K0 = 0.7978845608028654
K1 = K0 * 0.044715
SLOTS = 3
BIG = 2 * SLOTS
WIDE = BIG * HID
PIECE = 32
SPAN = 256
BF = jnp.bfloat16
F32 = jnp.float32

T1_AT = 0
T2_AT = T1_AT + HID
GATE_AT = T2_AT + TOWER2
MISC_AT = GATE_AT + GATES * (D // LANES)
LABEL_AT = MISC_AT + 16
G_ROWS = LABEL_AT
SMALL_ROWS = G_ROWS // 2


def nn(left, right):
    return jnp.dot(left, right, preferred_element_type=F32)


def nt(left, right):
    return lax.dot_general(left, right, (((1,), (1,)), ((), ())), preferred_element_type=F32)


def tn(left, right):
    return lax.dot_general(left, right, (((0,), (0,)), ((), ())), preferred_element_type=F32)


def params(mib, **kwargs):
    return pltpu.CompilerParams(vmem_limit_bytes=mib * 1024 * 1024, **kwargs)


def cost(flops, moved):
    return pl.CostEstimate(flops=int(flops), bytes_accessed=int(moved), transcendentals=0)


def shape(dims, kind=BF):
    return jax.ShapeDtypeStruct(dims, kind)


VSPEC = pl.BlockSpec(memory_space=pltpu.VMEM)
SSPEC = pl.BlockSpec(memory_space=pltpu.SMEM)
ASPEC = pl.BlockSpec(memory_space=pl.ANY)


def line(ref, row):
    both = ref[row : row + 1, :].astype(F32)
    return [both[:, :LANES], both[:, LANES:]]


def bags_kernel(blocks, chunks, len_ref, st_ref, en_ref, meta_ref):
    k = lax.broadcasted_iota(jnp.int32, (BAGS, BAGS), 0)
    j = lax.broadcasted_iota(jnp.int32, (BAGS, BAGS), 1)
    natural = (j % EVB) * FEATS + j // EVB
    before = jnp.where(k < natural, 1.0, 0.0).astype(BF)
    same = jnp.where(k == natural, 1.0, 0.0).astype(BF)
    lens_f = jnp.concatenate(
        [len_ref[:, b * BAGS : (b + 1) * BAGS] for b in range(blocks)], axis=0
    ).astype(F32)
    lens = lens_f.astype(BF)
    in_block = nn(lens, before)
    own = nn(lens, same)
    sums = jnp.sum(lens_f, axis=1, keepdims=True)
    high = jnp.floor(sums * (1.0 / 128.0))
    low = sums - high * 128.0
    bi = lax.broadcasted_iota(jnp.int32, (blocks, blocks), 0)
    bj = lax.broadcasted_iota(jnp.int32, (blocks, blocks), 1)
    lower = jnp.where(bj < bi, 1.0, 0.0).astype(BF)
    offset = 128.0 * nn(lower, jnp.broadcast_to(high, (blocks, BAGS)).astype(BF)) + nn(
        lower, jnp.broadcast_to(low, (blocks, BAGS)).astype(BF)
    )
    starts = offset + in_block
    st_ref[pl.ds(0, blocks), :] = starts.astype(jnp.int32)
    en_ref[pl.ds(0, blocks), :] = (starts + own).astype(jnp.int32)
    past = jnp.full((8, BAGS), chunks * ROWS, jnp.int32)
    st_ref[pl.ds(blocks, 8), :] = past
    en_ref[pl.ds(blocks, 8), :] = past
    lanes = meta_ref.shape[1]
    begins = jnp.concatenate([offset] * (lanes // BAGS), axis=1)
    row = lax.broadcasted_iota(jnp.int32, (blocks, lanes), 0)
    col = lax.broadcasted_iota(jnp.int32, (blocks, lanes), 1)
    begin = jnp.sum(jnp.where(row == col, begins, 0.0), axis=0, keepdims=True)
    spot = lax.broadcasted_iota(jnp.int32, (1, lanes), 1)
    begin = jnp.where(spot >= blocks, float(chunks * ROWS), begin)
    reached = jnp.where(begins <= (col * ROWS).astype(F32), 1.0, 0.0)
    first = jnp.sum(reached, axis=0, keepdims=True) - 1.0
    meta_ref[0:1, :] = begin.astype(jnp.int32)
    meta_ref[1:2, :] = first.astype(jnp.int32)


def small_kernel(
    ids_ref,
    label_ref,
    sgain_ref,
    sshift_ref,
    ogain_ref,
    oshift_ref,
    gate_ref,
    t1_ref,
    t2_ref,
    t3_ref,
    small_ref,
):
    small_ref[T1_AT : T1_AT + HID, :] = t1_ref[...]
    small_ref[T2_AT : T2_AT + TOWER2, :] = t2_ref[...]
    gate = gate_ref[...].astype(F32)
    turned = jnp.concatenate([gate[0:2], gate[3:4], gate[2:3]], axis=0)
    gate = jnp.where(ids_ref[0] == 0, gate, turned)
    lines = [gate[g : g + 1, p * LANES : (p + 1) * LANES] for g in range(GATES) for p in range(D // LANES)]
    lines += line(sgain_ref, 0) + line(sgain_ref, 1) + line(ogain_ref, 0)
    lines += line(sshift_ref, 0) + line(sshift_ref, 1) + line(oshift_ref, 0)
    lines += [jnp.concatenate([t3_ref[...].astype(F32)] * 2, axis=1), jnp.zeros((3, LANES), F32)]
    events = label_ref.shape[1]
    lines += [label_ref[:, p * LANES : (p + 1) * LANES].astype(F32) for p in range(events // LANES)]
    lines += [jnp.zeros((16 - events // LANES, LANES), F32)]
    small_ref[pl.ds(GATE_AT, 48), :] = jnp.concatenate(lines, axis=0).astype(BF)


def bags(lengths, chunks):
    blocks = lengths.shape[1] // BAGS
    lanes = -(-max(blocks + 1, chunks) // LANES) * LANES
    bounds = shape((blocks + 8, BAGS), jnp.int32)
    return pl.pallas_call(
        functools.partial(bags_kernel, blocks, chunks),
        out_shape=(bounds, bounds, shape((2, lanes), jnp.int32)),
        in_specs=[VSPEC],
        out_specs=(VSPEC,) * 3,
        compiler_params=params(4),
        cost_estimate=cost(1e9, 1e6),
    )(lengths)


def pack_small(ids, *arrays):
    return pl.pallas_call(
        small_kernel,
        out_shape=shape((LABEL_AT + 16, LANES)),
        in_specs=[SSPEC] + [VSPEC] * len(arrays),
        out_specs=VSPEC,
        compiler_params=params(56),
        cost_estimate=cost(1e9, 1e6),
    )(ids, *arrays)


def one_hot(starts, ends, base):
    row = lax.broadcasted_iota(jnp.int32, (ROWS, 2 * BAGS), 0).astype(F32).astype(BF)
    low = jnp.clip(starts - base, 0, ROWS).astype(F32).astype(BF)
    high = jnp.clip(ends - base, 0, ROWS).astype(F32).astype(BF)
    return jnp.where((row >= low) & (row < high), jnp.ones((), BF), jnp.zeros((), BF))


def window(ref, block):
    first = ref[pl.ds(block, 1), :]
    second = ref[pl.ds(block + 1, 1), :]
    return jnp.concatenate([first, second], axis=1)


def pool_kernel(skip, count, half_blocks, chunks, ids_ref, meta_ref, st_ref, en_ref, ent_ref, *refs):
    x_ref, acc_ref = refs[-2:]
    base_block = ids_ref[0] * half_blocks + skip

    def clear(i, carry):
        at = pl.multiple_of((base_block + i) * BAGS, BAGS)
        acc_ref[:, pl.ds(at, BAGS)] = jnp.zeros((EMB, BAGS), F32)
        return carry

    lax.fori_loop(0, count, clear, 0, unroll=True)

    low_chunk = meta_ref[0, base_block] // ROWS
    high_chunk = (meta_ref[0, base_block + count] + ROWS - 1) // ROWS
    step = 9

    def chunk(i, carry):
        for u in range(step):
            c = low_chunk + i * step + u
            inside = jnp.minimum(c, chunks - 1)
            block = meta_ref[1, inside]
            at = pl.multiple_of(inside * ROWS, ROWS)
            picked = one_hot(window(st_ref, block), window(en_ref, block), c * ROWS)
            part = nn(ent_ref[:, pl.ds(at, ROWS)], picked)
            to = pl.multiple_of(block * BAGS, BAGS)
            acc_ref[:, pl.ds(to, 2 * BAGS)] += part
        return carry

    lax.fori_loop(0, (high_chunk - low_chunk + step - 1) // step, chunk, 0)

    def place(i, carry):
        at = pl.multiple_of((base_block + i) * BAGS, BAGS)
        to = pl.multiple_of(i * EVB, EVB)
        block = acc_ref[:, pl.ds(at, BAGS)].T
        for pair in range(FEATS // 2):
            left = block[2 * pair * EVB : (2 * pair + 1) * EVB]
            right = block[(2 * pair + 1) * EVB : (2 * pair + 2) * EVB]
            x_ref[pl.ds(to, EVB), pair * 2 * EMB : (pair + 1) * 2 * EMB] = jnp.concatenate(
                [left, right], axis=1
            ).astype(BF)
        return carry

    lax.fori_loop(0, count, place, 0, unroll=12)


def pool(part, parts, ids, meta, starts, ends, entries, *after):
    blocks = starts.shape[0] - 8
    half_blocks = blocks // 2
    count = half_blocks // parts
    chunks = entries.shape[1] // ROWS
    return pl.pallas_call(
        functools.partial(pool_kernel, part * count, count, half_blocks, chunks),
        out_shape=shape((count * EVB, D)),
        in_specs=[SSPEC, SSPEC, VSPEC, VSPEC, VSPEC] + [ASPEC] * len(after),
        out_specs=VSPEC,
        scratch_shapes=[pltpu.VMEM((EMB, (blocks + 1) * BAGS), F32)],
        compiler_params=params(16),
        cost_estimate=cost(10e9, 5e6),
    )(ids, meta, starts, ends, entries, *after)


def expand_kernel(half_blocks, group, ids_ref, meta_ref, st_ref, en_ref, own_ref, other_ref, out_ref, pred_ref, token_ref, rows_ref):
    position = ids_ref[0]
    step = pl.program_id(0)
    events = half_blocks * EVB

    @pl.when(step == 0)
    def _():
        for source, half in ((own_ref, position), (other_ref, 1 - position)):

            def place(i, carry):
                at = pl.multiple_of(i * EVB, EVB)
                to = pl.multiple_of((half * half_blocks + i) * BAGS, BAGS)
                for pair in range(FEATS // 2):
                    tile = source[pl.ds(at, EVB), pair * 2 * EMB : (pair + 1) * 2 * EMB]
                    rows_ref[pl.ds(to + 2 * pair * EVB, EVB), :] = tile[:, :EMB]
                    rows_ref[pl.ds(to + (2 * pair + 1) * EVB, EVB), :] = tile[:, EMB:]
                return carry

            lax.fori_loop(0, half_blocks, place, 0, unroll=12)
        rows_ref[pl.ds(2 * half_blocks * BAGS, BAGS), :] = jnp.zeros((BAGS, EMB), BF)
        own = own_ref[events : events + 16, : 2 * LANES].astype(F32)
        other = other_ref[events : events + 16, : 2 * LANES].astype(F32)
        mine = (own[:, :LANES] + own[:, LANES:])[:8]
        theirs = (other[:, :LANES] + other[:, LANES:])[8:]
        halves = (jnp.where(position == 0, mine, theirs), jnp.where(position == 0, theirs, mine))
        tiles = events // LANES
        token_ref[...] = mine
        pred_ref[...] = jnp.concatenate([half[k : k + 1] for half in halves for k in range(tiles)], axis=1)

    for u in range(group):
        c = step * group + u
        block = meta_ref[1, c]
        picked = one_hot(window(st_ref, block), window(en_ref, block), c * ROWS)
        at = pl.multiple_of(block * BAGS, BAGS)
        out_ref[:, u * ROWS : (u + 1) * ROWS] = nn(picked, rows_ref[pl.ds(at, 2 * BAGS), :]).astype(BF).T


def expand(ids, meta, starts, ends, own, other, rows):
    blocks = starts.shape[0] - 8
    chunks = rows // ROWS
    group = 36
    while chunks % group:
        group -= 1
    return pl.pallas_call(
        functools.partial(expand_kernel, blocks // 2, group),
        grid=(chunks // group,),
        out_shape=(shape((EMB, rows)), shape((1, blocks * EVB), F32), shape((8, LANES), F32)),
        in_specs=[SSPEC, SSPEC, VSPEC, VSPEC, VSPEC, VSPEC],
        out_specs=(
            pl.BlockSpec((EMB, group * ROWS), lambda i: (0, i)),
            pl.BlockSpec((1, blocks * EVB), lambda i: (0, 0)),
            pl.BlockSpec((8, LANES), lambda i: (0, 0)),
        ),
        scratch_shapes=[pltpu.VMEM(((blocks + 1) * BAGS, EMB), BF)],
        compiler_params=params(24, dimension_semantics=("arbitrary",)),
        cost_estimate=cost(12e9, 6e6),
    )(ids, meta, starts, ends, own, other)


def gelu_twice(v):
    cube = K1 * (v * v)
    bend = jnp.tanh(v * (cube + K0))
    rise = 1.0 + bend
    act = v * rise
    slope = rise + act * (1.0 - bend) * (3.0 * cube + K0)
    return act, slope


def gelu_both(v):
    act, slope = gelu_twice(v)
    return 0.5 * act, 0.5 * slope


def wide(block, row):
    return jnp.concatenate([block[row : row + 1, :], block[row + 1 : row + 2, :]], axis=1)


def by_eight(value):
    return jnp.sum(value.reshape(-1, 8, value.shape[-1]), axis=0)


def plus(total, term):
    return term if total is None else total + term


def pieces_of(m):
    return [slice(at, at + PIECE) for at in range(m * HID, (m + 1) * HID, PIECE)]


def col_sum(value):
    return jnp.sum(value, axis=0, keepdims=True)


def lane_tiles(events, body):
    def step(j, carry):
        body(j, pl.ds(pl.multiple_of(j * LANES, LANES), LANES))
        return carry

    lax.fori_loop(0, events // LANES, step, 0)


def main_kernel(xs, given, plan, rows1, rows2, ids_ref, *refs):
    refs = list(refs)
    take = lambda n: [refs.pop(0) for _ in range(n)]
    x_parts = take(xs)
    own_groups, oth_groups = take(len(given)), take(len(given))
    packs = take(2)
    (dx_ref,) = take(1)
    own_outs, oth_outs = take(len(plan)), take(len(plan))
    x_ref, wc_ref, w2_ref, gain_ref, third_ref, lab_ref, pc_ref, pb_ref, s2_ref, y_ref, h_ref, e_ref, fc_ref = take(13)
    scale_ref, lg_ref, prob_ref, q_ref, pt_ref, u1_ref, p4_ref, e2_ref, e1_ref, du_ref, dm_ref, dmb_ref, ds_ref, dn_ref, acc3_ref, pred_ref, g1_ref, g2_ref, dp_ref = take(19)
    position = ids_ref[0]
    events = x_ref.shape[1]

    def part(m):
        return slice(m * HID, (m + 1) * HID)

    def rows_of(t, piece):
        if piece is None:
            return pl.ds(0, rows1), pl.ds(0, rows2)
        where = position if t == 0 else 1 - position
        d = ids_ref[1] ^ (4 * piece[2])
        if piece[1]:
            d = d ^ (2 - where)
        if piece[0]:
            d = d ^ (1 + where)
        return (
            pl.ds(pl.multiple_of(d * rows1, rows1), rows1),
            pl.ds(pl.multiple_of(d * rows2, rows2), rows2),
        )

    size = events // xs
    for k, piece in enumerate(x_parts):
        x_ref[:, k * size : (k + 1) * size] = piece[...].T
    for t, whole in enumerate((own_groups, oth_groups)):
        for group, pieces in zip(whole, given):
            for g, piece in enumerate(pieces):
                one, two = rows_of(t, piece)
                for s in range(SLOTS):
                    wc_ref[one, part(t * SLOTS + s)] = group[g, s * rows1 : (s + 1) * rows1, :]
                    low = SLOTS * rows1 + s * rows2
                    w2_ref[t * SLOTS + s, two, :] = (0.5 * group[g, low : low + rows2, :].astype(F32)).astype(BF)
    lines = []
    for t in range(2):
        block = packs[t][GATE_AT : GATE_AT + 16, :].astype(F32)
        for g in range(GATES):
            lines.append(
                jnp.concatenate([block[4 * g + p : 4 * g + p + 1, :] for p in range(D // LANES)], axis=1)
            )
        lines.append(jnp.zeros((8 - GATES, D), F32))
    gates = jnp.concatenate(lines, axis=0).astype(BF)
    wc_ref[:, WIDE:] = jnp.concatenate([gates, jnp.zeros((LANES - 16, D), BF)], axis=0).T
    fc_ref[WIDE:, :] = jnp.zeros((LANES, events), BF)
    acc3_ref[...] = jnp.zeros_like(acc3_ref)
    miscs = [packs[t][MISC_AT : MISC_AT + 16, :].astype(F32) for t in range(2)]
    for t in range(2):
        misc = miscs[t]
        for s in range(SLOTS):
            for kind in range(2):
                for half in range(2):
                    at = 2 * (kind * SLOTS + s) + half
                    to = ((kind * 2 + t) * SLOTS + s) * HID + half * LANES
                    gain_ref[to : to + LANES, :] = jnp.broadcast_to(misc[at : at + 1, :], (LANES, LANES)).T
        third = jnp.broadcast_to(misc[12:13, :], (LANES, LANES)).T
        third_ref[t * TOWER2 : (t + 1) * TOWER2, :] = third[:TOWER2]
        lab_ref[t * 16 : (t + 1) * 16, :] = packs[t][LABEL_AT : LABEL_AT + 16, :].astype(F32)

    lg_ref[...] = nn(gates, x_ref[...])
    span = next(size for size in (SPAN, 2 * LANES, LANES) if events % size == 0)
    spans = [slice(at, at + span) for at in range(0, events, span)]

    def first_sums(m):
        pc_ref[part(m), :] = tn(wc_ref[:, part(m)], x_ref[...])

    def first_gelu(m):
        for here in spans:
            for rows in pieces_of(m):
                act, slope = gelu_twice(pc_ref[rows, here])
                pc_ref[rows, here] = slope
                h_ref[rows, here] = act.astype(BF)

    def second_gelu(m, here):
        total = None
        for rows in pieces_of(m):
            act, slope = gelu_twice(pb_ref[rows, here])
            pb_ref[rows, here] = act
            s2_ref[rows, here] = slope
            total = plus(total, by_eight(act))
        mean = col_sum(total) * (1.0 / HID)
        total = None
        for rows in pieces_of(m):
            centred = pb_ref[rows, here] - mean
            pb_ref[rows, here] = centred
            total = plus(total, by_eight(centred * centred))
        scale = lax.rsqrt(col_sum(total) * (1.0 / HID) + 4.0 * EPSILON)
        scale_ref[m : m + 1, here] = scale
        for rows in pieces_of(m):
            normed = pb_ref[rows, here] * scale
            pb_ref[rows, here] = normed
            for lanes in range(here.start, here.stop, LANES):
                block = slice(lanes, lanes + LANES)
                out = pb_ref[rows, block] * gain_ref[rows, :] + gain_ref[slice(WIDE + rows.start, WIDE + rows.stop), :]
                if m % SLOTS == SLOTS - 1:
                    out = out.astype(BF).astype(F32)
                y_ref[rows, block] = out

    first_sums(0)
    for m in range(BIG):
        if m + 1 < BIG:
            first_sums(m + 1)
        first_gelu(m)
        pb_ref[part(m), :] = tn(w2_ref[m], h_ref[part(m), :])
        if m:
            for here in spans:
                second_gelu(m - 1, here)
    for here in spans:
        second_gelu(BIG - 1, here)
    orders = [(t * SLOTS, t * SLOTS + 1, t * SLOTS + 2, (1 - t) * SLOTS + 2) for t in range(2)]

    prob_ref[...] = jnp.ones_like(prob_ref)

    def mix(j, here):
        for t in range(2):
            logits = [lg_ref[8 * t + k : 8 * t + k + 1, here] for k in range(GATES)]
            top = jnp.maximum(jnp.maximum(logits[0], logits[1]), jnp.maximum(logits[2], logits[3]))
            raised = [jnp.exp(logit - top) for logit in logits]
            scale = 1.0 / (raised[0] + raised[1] + raised[2] + raised[3])
            mixture = None
            for k in range(GATES):
                prob = raised[k] * scale
                prob_ref[8 * t + k : 8 * t + k + 1, here] = prob
                term = prob * y_ref[part(orders[t][k]), here]
                mixture = term if mixture is None else mixture + term
            q_ref[part(t), here] = mixture.astype(BF)

    lane_tiles(events, mix)
    for t in range(2):
        pt_ref[t * TOWER1 : (t + 1) * TOWER1, :] = tn(packs[t][T1_AT : T1_AT + HID, :], q_ref[part(t), :])

    def tower_gelu(j, here):
        act, slope = gelu_both(pt_ref[:, here])
        pt_ref[:, here] = slope
        u1_ref[:, here] = act.astype(BF)

    lane_tiles(events, tower_gelu)
    for t in range(2):
        p4_ref[t * TOWER2 : (t + 1) * TOWER2, :] = nn(
            packs[t][T2_AT : T2_AT + TOWER2, :], u1_ref[t * TOWER1 : (t + 1) * TOWER1, :]
        )

    def head(j, here):
        act, slope = gelu_both(p4_ref[:, here])
        u2 = act.astype(BF).astype(F32)
        product = u2 * third_ref[...]
        deltas = []
        for t in range(2):
            logit = col_sum(product[t * TOWER2 : (t + 1) * TOWER2])
            prediction = 1.0 / (1.0 + jnp.exp(-logit))
            pred_ref[pl.ds(8 * t + j, 1), :] = prediction
            label = lab_ref[pl.ds(t * 16 + position * (events // LANES) + j, 1), :]
            deltas.append(jnp.broadcast_to(prediction - label, (TOWER2, LANES)))
        delta = jnp.concatenate(deltas, axis=0)
        acc3_ref[...] += delta * u2
        e2_ref[:, here] = (slope * (delta * third_ref[...])).astype(BF)

    lane_tiles(events, head)
    for t in range(2):
        du_ref[t * TOWER1 : (t + 1) * TOWER1, :] = tn(
            packs[t][T2_AT : T2_AT + TOWER2, :], e2_ref[t * TOWER2 : (t + 1) * TOWER2, :]
        )

    def tower_back(j, here):
        e1_ref[:, here] = (pt_ref[:, here] * du_ref[:, here]).astype(BF)

    lane_tiles(events, tower_back)
    for t in range(2):
        mixed = nn(packs[t][T1_AT : T1_AT + HID, :], e1_ref[t * TOWER1 : (t + 1) * TOWER1, :])
        dm_ref[part(t), :] = mixed
        dmb_ref[part(t), :] = mixed.astype(BF)
        rows = [wide(miscs[t], 2 * (SLOTS + s)) for s in range(EXPERTS)] + [jnp.zeros((8 - EXPERTS, HID), F32)]
        ds_ref[8 * t : 8 * t + 8, :] = nn(jnp.concatenate(rows, axis=0).astype(BF), dmb_ref[part(t), :])

    def probs_of(t, k, here):
        return prob_ref[8 * t + k : 8 * t + k + 1, here]

    def shared_probs(here):
        for t in range(2):
            for k in range(EXPERTS, GATES):
                total = None
                for mine, rows in zip(pieces_of(t), pieces_of(orders[t][k])):
                    total = plus(total, by_eight(dm_ref[mine, here] * y_ref[rows, here]))
                dp_ref[8 * t + k : 8 * t + k + 1, here] = col_sum(total)

    def norm_back(m, here):
        t, s = divmod(m, SLOTS)
        one, two = None, None
        for rows in pieces_of(m):
            mine = slice(rows.start - m * HID + t * HID, rows.stop - m * HID + t * HID)
            for lanes in range(here.start, here.stop, LANES):
                block = slice(lanes, lanes + LANES)
                up = dm_ref[mine, block]
                if s == SLOTS - 1:
                    theirs = slice(mine.start + (1 - 2 * t) * HID, mine.stop + (1 - 2 * t) * HID)
                    up = probs_of(t, s, block) * up + probs_of(1 - t, SLOTS, block) * dm_ref[theirs, block]
                y_ref[rows, block] = up * gain_ref[rows, :]
            d_normed = y_ref[rows, here]
            product = d_normed * pb_ref[rows, here]
            dn_ref[rows, here] = product.astype(BF)
            one = plus(one, by_eight(d_normed))
            two = plus(two, by_eight(product))
        one, two = col_sum(one), col_sum(two)
        outer = scale_ref[m : m + 1, here]
        if s < EXPERTS:
            outer = outer * probs_of(t, s, here)
            dp_ref[8 * t + s : 8 * t + s + 1, here] = two + ds_ref[8 * t + s : 8 * t + s + 1, here]
        one, two = one * (1.0 / HID), two * (1.0 / HID)
        for rows in pieces_of(m):
            inner = y_ref[rows, here] - one - pb_ref[rows, here] * two
            e_ref[rows, here] = (s2_ref[rows, here] * outer * inner).astype(BF)

    def put(m, first, value, scale):
        t, s = divmod(m, SLOTS)
        held = (g1_ref if first else g2_ref).at[m % 2]
        held[...] = value
        for out, (small_first, pieces) in zip((own_outs, oth_outs)[t], plan):
            for g, piece in enumerate(pieces):
                mine = rows_of(t, piece)[0 if first else 1]
                at = g * SLOTS * (rows1 + rows2) + (SMALL_ROWS if small_first else 0)
                at, size = (at + s * rows1, rows1) if first else (at + SLOTS * rows1 + s * rows2, rows2)
                out[at : at + size, :] = (scale * held[mine, :]).astype(BF)

    for here in spans:
        shared_probs(here)
    for here in spans:
        norm_back(0, here)
    for m in range(BIG):
        y_ref[part(m), :] = nn(w2_ref[m], e_ref[part(m), :])
        put(m, False, nt(h_ref[part(m), :], e_ref[part(m), :]), 0.5)
        if m + 1 < BIG:
            for here in spans:
                norm_back(m + 1, here)
        for here in spans:
            for rows in pieces_of(m):
                fc_ref[rows, here] = (pc_ref[rows, here] * y_ref[rows, here]).astype(BF)
        put(m, True, nt(x_ref[...], fc_ref[part(m), :]), 1.0)
    codes = []
    for t in range(2):
        probs = [probs_of(t, k, slice(None)) for k in range(GATES)]
        d_probs = [dp_ref[8 * t + k : 8 * t + k + 1, :] for k in range(GATES)]
        weighted = probs[0] * d_probs[0]
        for k in range(1, GATES):
            weighted = weighted + probs[k] * d_probs[k]
        codes += [probs[k] * (d_probs[k] - weighted) for k in range(GATES)]
        codes.append(jnp.zeros((8 - GATES, events), F32))
    fc_ref[WIDE : WIDE + 16, :] = jnp.concatenate(codes, axis=0).astype(BF)
    dx_ref[:events, :] = nn(wc_ref[...], fc_ref[...]).astype(BF).T
    pred = pred_ref[...]
    high = pred.astype(BF)
    low = (pred - high.astype(F32)).astype(BF)
    dx_ref[events:, :] = jnp.concatenate([high, low, high, low], axis=1)

    gate_grad = nt(fc_ref[WIDE : WIDE + 16, :], x_ref[...])
    weights = prob_ref[...].astype(BF)
    shifts = [nt(weights, dmb_ref[part(t), :]) for t in range(2)]
    third_grad = col_sum(acc3_ref[...].T)
    for t, results in enumerate((own_outs, oth_outs)):
        tower = slice(t * TOWER1, (t + 1) * TOWER1)
        half = slice(t * TOWER2, (t + 1) * TOWER2)
        lines = []
        for g in range(GATES):
            row = gate_grad[8 * t + g : 8 * t + g + 1, :]
            lines += [row[:, p * LANES : (p + 1) * LANES] for p in range(D // LANES)]
        for s in range(SLOTS):
            at = 8 * t + (s if s < EXPERTS else GATES)
            row = nt(weights, dn_ref[part(t * SLOTS + s), :])[at : at + 1, :] / wide(miscs[t], 2 * s)
            lines += [row[:, :LANES], row[:, LANES:]]
        for s in range(SLOTS):
            row = shifts[t][8 * t + s : 8 * t + s + 1, :]
            if s == SLOTS - 1:
                row = row + shifts[1 - t][8 * (1 - t) + SLOTS : 8 * (1 - t) + SLOTS + 1, :]
            lines += [row[:, :LANES], row[:, LANES:]]
        lines.append(third_grad if t == 0 else pltpu.roll(third_grad, TOWER2, 1))
        lines.append(jnp.zeros((3, LANES), F32))
        small = jnp.concatenate(
            [
                nt(q_ref[part(t), :], e1_ref[tower, :]),
                nt(e2_ref[half, :], u1_ref[tower, :]),
                jnp.concatenate(lines, axis=0),
            ],
            axis=0,
        )
        small = jnp.concatenate([small[:SMALL_ROWS], small[SMALL_ROWS:]], axis=1).astype(BF)
        for out, (small_first, _) in zip(results, plan):
            if small_first:
                out[:SMALL_ROWS, :] = small


def layer(ids, x_parts, own_groups, oth_groups, own_pack, oth_pack, given, plan, rows1, rows2):
    events = sum(part.shape[0] for part in x_parts)
    rows = SLOTS * (rows1 + rows2)
    grads = tuple(shape((len(pieces) * rows + small * SMALL_ROWS, HID)) for small, pieces in plan)
    results = (shape((events + 16, D)),) + grads + grads
    scratch = [
        ((D, events), BF),
        ((D, WIDE + LANES), BF),
        ((BIG, HID, HID), BF),
        ((2 * WIDE, LANES), F32),
        ((2 * TOWER2, LANES), F32),
        ((32, LANES), F32),
        ((WIDE, events), F32),
        ((WIDE, events), F32),
        ((WIDE, events), F32),
        ((WIDE, events), F32),
        ((WIDE, events), BF),
        ((WIDE, events), BF),
        ((WIDE + LANES, events), BF),
        ((8, events), F32),
        ((16, events), F32),
        ((16, events), F32),
        ((2 * HID, events), BF),
        ((2 * TOWER1, events), F32),
        ((2 * TOWER1, events), BF),
        ((2 * TOWER2, events), F32),
        ((2 * TOWER2, events), BF),
        ((2 * TOWER1, events), BF),
        ((2 * TOWER1, events), F32),
        ((2 * HID, events), F32),
        ((2 * HID, events), BF),
        ((16, events), F32),
        ((WIDE, events), BF),
        ((2 * TOWER2, LANES), F32),
        ((16, LANES), F32),
        ((2, D, HID), F32),
        ((2, HID, HID), F32),
        ((16, events), F32),
    ]
    arrays = [*x_parts, *own_groups, *oth_groups, own_pack, oth_pack]
    dx, *grads = pl.pallas_call(
        functools.partial(main_kernel, len(x_parts), given, plan, rows1, rows2),
        out_shape=results,
        in_specs=[SSPEC] + [VSPEC] * len(arrays),
        out_specs=(VSPEC,) * len(results),
        scratch_shapes=[pltpu.VMEM(dims, kind) for dims, kind in scratch],
        compiler_params=params(46),
        cost_estimate=cost(events * BIG * 196608 * 6, 10e6),
    )(ids, *arrays)
    return dx, grads[: len(plan)], grads[len(plan) :]


def sibling(value):
    return lax.ppermute(value, "task", [(0, 1), (1, 0)])


def flipped(value, mask):
    pairs = [(i, i ^ mask) for i in range(lax.axis_size("dp"))]
    return lax.ppermute(value, "dp", pairs)


def crossed(value, masks):
    n = lax.axis_size("dp")
    pairs = [(t * n + i, t * n + (i ^ masks[t])) for t in range(2) for i in range(n)]
    return lax.ppermute(value, ("task", "dp"), pairs)


def stack_kernel(count, *refs):
    out, sems = refs[-2:]
    copies = [pltpu.make_async_copy(refs[k], out.at[k], sems.at[k]) for k in range(count)]
    for copy in copies:
        copy.start()
    for copy in copies:
        copy.wait()


def stacked(pieces):
    return pl.pallas_call(
        functools.partial(stack_kernel, len(pieces)),
        out_shape=shape((len(pieces),) + pieces[0].shape, pieces[0].dtype),
        in_specs=[ASPEC] * len(pieces),
        out_specs=VSPEC,
        scratch_shapes=[pltpu.SemaphoreType.DMA((len(pieces),))],
        compiler_params=params(4),
        cost_estimate=cost(0, 1e6),
    )(*pieces)


def summed(*terms):
    total = terms[0].astype(F32)
    for term in terms[1:]:
        total = total + term.astype(F32)
    return total.astype(BF)


def small_sum_kernel(one_ref, two_ref, *refs):
    out_ref = refs[-1]
    out_ref[...] = (one_ref[...].astype(F32) + two_ref[...].astype(F32)).astype(BF)


def small_sum(one, two, *after):
    lead = pl.BlockSpec((SMALL_ROWS, HID), lambda i: (0, 0))
    return pl.pallas_call(
        small_sum_kernel,
        grid=(1,),
        out_shape=shape((SMALL_ROWS, HID)),
        in_specs=[lead, lead] + [ASPEC] * len(after),
        out_specs=lead,
        compiler_params=params(4),
        cost_estimate=cost(8e9, 1e6),
    )(one, two, *after)


def tie_kernel(*refs):
    pass


def tied(value, after):
    return pl.pallas_call(
        tie_kernel,
        out_shape=shape(value.shape, value.dtype),
        in_specs=[ASPEC, ASPEC],
        out_specs=ASPEC,
        input_output_aliases={0: 0},
        compiler_params=params(1),
        cost_estimate=cost(0, 1),
    )(value, after)


def far_kernel(rows, keep_ref, got_ref, mid_ref, near_ref, *outs):
    for k, out in enumerate(outs):
        here = slice(k * rows, (k + 1) * rows)
        total = keep_ref[here, :].astype(F32) + got_ref[here, :].astype(F32)
        at = SMALL_ROWS + k * rows
        total = total + mid_ref[at : at + rows, :].astype(F32)
        out[...] = (total + near_ref[here, :].astype(F32)).astype(BF)


def block(rows, at=0):
    return pl.BlockSpec((rows, HID), lambda i: (at, 0))


def far_messages(far, rows, keep, got, mid, near):
    size = far * rows
    return pl.pallas_call(
        functools.partial(far_kernel, rows),
        grid=(1,),
        out_shape=(shape((rows, HID)),) * far,
        in_specs=[block(size), block(size), block(size + SMALL_ROWS), block(size)],
        out_specs=(block(rows),) * far,
        compiler_params=params(12),
        cost_estimate=cost(0, 4e6),
    )(keep, got, mid, near)


def home_kernel(rows, keep_ref, got_ref, mid_ref, *refs):
    smalls, (message_ref, base_ref) = refs[:-2], refs[-2:]
    total = keep_ref[...].astype(F32) + got_ref[...].astype(F32) + mid_ref[...].astype(F32)
    base_ref[...] = total[:rows]
    message_ref[SMALL_ROWS:, :] = total[rows:].astype(BF)
    small = smalls[0][...].astype(F32)
    for term in smalls[1:]:
        small = small + term[...].astype(F32)
    message_ref[:SMALL_ROWS, :] = small.astype(BF)


def home_message(far, rows, keep, got, mid, smalls):
    at = block(2 * rows, far)
    return pl.pallas_call(
        functools.partial(home_kernel, rows),
        grid=(1,),
        out_shape=(shape((SMALL_ROWS + rows, HID)), shape((rows, HID), F32)),
        in_specs=[at, at, block(2 * rows)] + [block(SMALL_ROWS)] * len(smalls),
        out_specs=(block(SMALL_ROWS + rows), block(rows)),
        compiler_params=params(8),
        cost_estimate=cost(0, 2e6),
    )(keep, got, mid, *smalls)


def total_kernel(*refs):
    total = refs[0][...].astype(F32)
    for term in refs[1:-1]:
        total = total + term[...].astype(F32)
    refs[-1][...] = total


def totalled(*terms):
    return pl.pallas_call(
        total_kernel,
        out_shape=shape(terms[0].shape, F32),
        in_specs=[VSPEC] * len(terms),
        out_specs=VSPEC,
        compiler_params=params(4),
        cost_estimate=cost(10e9, 1e6),
    )(*terms)


def last_kernel(rows1, rows2, paired, ids_ref, *refs):
    if paired:
        part_ref, sent_ref, near_ref = refs[:3]
        total = part_ref[...] + near_ref[SMALL_ROWS:, :].astype(F32)
        small = sent_ref[:SMALL_ROWS, :].astype(F32) + near_ref[:SMALL_ROWS, :].astype(F32)
    else:
        total, small = refs[0][...], refs[1][...]
    w1_ref, w2_ref, o1_ref, o2_ref, sg_ref, ss_ref, og_ref, os_ref, gate_ref, t1_ref, t2_ref, t3_ref = refs[-12:]
    cut = SLOTS * rows1
    for s in range(EXPERTS):
        w1_ref[s] = total[s * rows1 : (s + 1) * rows1]
        w2_ref[s] = total[cut + s * rows2 : cut + (s + 1) * rows2]
    o1_ref[...] = total[EXPERTS * rows1 : cut]
    o2_ref[...] = total[cut + EXPERTS * rows2 :]
    tiny = jnp.concatenate([small[:, :LANES], small[:, LANES:]], axis=0)
    t1_ref[...] = tiny[T1_AT : T1_AT + HID]
    t2_ref[...] = tiny[T2_AT : T2_AT + TOWER2]
    gates = []
    for g in range(GATES):
        at = GATE_AT + 4 * g
        gates.append(jnp.concatenate([tiny[at + p : at + p + 1] for p in range(D // LANES)], axis=1))
    turned = ids_ref[0] != 0
    gate_ref[0:1, :] = gates[0]
    gate_ref[1:2, :] = gates[1]
    gate_ref[2:3, :] = jnp.where(turned, gates[3], gates[2])
    gate_ref[3:4, :] = jnp.where(turned, gates[2], gates[3])
    for kind, (spec, own) in enumerate(((sg_ref, og_ref), (ss_ref, os_ref))):
        for s in range(SLOTS):
            at = MISC_AT + 2 * (kind * SLOTS + s)
            row = jnp.concatenate([tiny[at : at + 1], tiny[at + 1 : at + 2]], axis=1)
            if s < EXPERTS:
                spec[s : s + 1, :] = row
            else:
                own[...] = row
    t3_ref[...] = tiny[MISC_AT + 12 : MISC_AT + 13, :TOWER2]


def finish(ids, terms, rows1, rows2):
    outs = (
        shape((EXPERTS, rows1, HID), F32),
        shape((EXPERTS, rows2, HID), F32),
        shape((rows1, HID), F32),
        shape((rows2, HID), F32),
        shape((EXPERTS, HID), F32),
        shape((EXPERTS, HID), F32),
        shape((1, HID), F32),
        shape((1, HID), F32),
        shape((GATES, D), F32),
        shape((HID, TOWER1), F32),
        shape((TOWER2, TOWER1), F32),
        shape((1, TOWER2), F32),
    )
    return pl.pallas_call(
        functools.partial(last_kernel, rows1, rows2, len(terms) == 3),
        out_shape=outs,
        in_specs=[SSPEC] + [VSPEC] * len(terms),
        out_specs=(VSPEC,) * len(outs),
        compiler_params=params(8),
        cost_estimate=cost(0, 2e6),
    )(ids, *terms)


def per_device(
    entries,
    lengths,
    labels,
    spec_w1,
    spec_w2,
    spec_gain,
    spec_shift,
    shared_w1,
    shared_w2,
    shared_gain,
    shared_shift,
    gate_w,
    tower_w1,
    tower_w2,
    tower_w3,
):
    position = lax.axis_index("task")
    n = lax.axis_size("dp")
    ids = jnp.stack([position, lax.axis_index("dp")]).astype(jnp.int32)
    rows1, rows2 = spec_w1.shape[2], spec_w2.shape[2]
    direct = rows2 % 16 == 0 and n % 4 == 0 and n & (n - 1) == 0
    pack = jnp.concatenate(
        [part.reshape(-1, HID) for part in (spec_w1, shared_w1, spec_w2, shared_w2)], axis=0
    )
    if direct:
        quarter = n // 4
        far = [pack] + [flipped(pack, 4 * k) for k in range(1, quarter)]

    rows = entries.shape[0]
    starts, ends, meta = bags(lengths, rows // ROWS)
    small = pack_small(
        ids,
        labels,
        spec_gain[0],
        spec_shift[0],
        shared_gain,
        shared_shift,
        gate_w[0].T,
        tower_w1[0],
        tower_w2[0].T,
        tower_w3,
    )
    other_small = sibling(small)
    turned = entries.T
    x_first = pool(0, 2, ids, meta, starts, ends, turned)

    if direct:
        zc = stacked(far)
        r1 = tied(crossed(zc, (1, 2)), x_first)
        r2 = crossed(tied(zc, x_first), (2, 1))
        x_second = pool(1, 2, ids, meta, starts, ends, turned, other_small)
        r3 = tied(crossed(r1, (2, 1)), x_second)
        own = [zc, r2, r1, r3]
        given = tuple(tuple((one, two, k) for k in range(quarter)) for one, two in ((0, 0), (0, 1), (1, 0), (1, 1)))
        far_ones = [(two, k) for two in range(2) for k in range(1, quarter)]
        home_ones = [(0, 0), (1, 0)]
        send = [(1, *piece) for piece in far_ones]
        keep = [(0, *piece) for piece in far_ones + home_ones] + [(1, *piece) for piece in home_ones]
        plan, used1, used2 = ((0, tuple(keep)), (1, tuple(send))), rows1, rows2
    else:
        x_second = pool(1, 2, ids, meta, starts, ends, turned)
        every = lax.all_gather(pack, "dp", axis=0)
        cut = SLOTS * rows1
        w1 = every[:, :cut].reshape(n, SLOTS, rows1, HID).swapaxes(0, 1).reshape(-1, HID)
        w2 = every[:, cut:].reshape(n, SLOTS, rows2, HID).swapaxes(0, 1).reshape(-1, HID)
        own = [jnp.concatenate([w1, w2], axis=0)[None]]
        given, plan, used1, used2 = ((None,),), ((1, (None,)),), D, HID
    dx, own_grads, oth_grads = layer(
        ids, [x_first, x_second], own, [sibling(group) for group in own], small, other_small, given, plan, used1, used2
    )

    got = [sibling(grad) for grad in oth_grads[::-1]][::-1]
    other_dx = sibling(dx)
    turned, predictions, expanded = expand(ids, meta, starts, ends, dx, other_dx, rows)
    piece = SLOTS * (rows1 + rows2)
    if direct:
        keep, send = own_grads
        far, cut = quarter - 1, (quarter - 1) * piece
        send = summed(send, got[1])
        mid = tied(crossed(send, (1, 2)), expanded)
        home = slice(2 * cut + 2 * piece, 2 * cut + 4 * piece)
        home = summed(keep[home], got[0][home])
        late = slice(cut, 2 * cut)
        near = crossed(summed(keep[late], got[0][late], mid[SMALL_ROWS + cut :]), (2, 1))
        small = small_sum(send, mid)
        home_mid = crossed(tied(home, mid), (1, 2))
        smalls = [flipped(small, 4 * k) for k in range(1, quarter)]
        parts = far_messages(far, piece, keep, got[0], mid, near)
        smalls = [small] + [tied(term, parts[0]) for term in smalls]
        message, base = home_message(far, piece, keep, got[0], home_mid, smalls)
        parts = [flipped(part, 4 * (k + 1)) for k, part in enumerate(parts)]
        grads = finish(ids, [totalled(base, *parts), message, crossed(message, (2, 1))], rows1, rows2)
    else:
        whole = own_grads[0].astype(F32) + got[0].astype(F32)
        small = lax.psum(whole[:SMALL_ROWS], "dp")
        whole = whole[SMALL_ROWS:]
        cut = SLOTS * D
        g1 = lax.psum_scatter(whole[:cut].reshape(SLOTS, D, HID), "dp", scatter_dimension=1, tiled=True)
        g2 = lax.psum_scatter(whole[cut:].reshape(SLOTS, HID, HID), "dp", scatter_dimension=1, tiled=True)
        part = jnp.concatenate([g1.reshape(-1, HID), g2.reshape(-1, HID)], axis=0)
        grads = finish(ids, [part, small], rows1, rows2)
    w1, w2, o1, o2, sg, ss, og, os, gate, t1, t2, t3 = grads
    entry_grads = turned.T
    return (
        predictions,
        entry_grads,
        w1[None],
        w2[None],
        sg[None],
        ss[None],
        o1[None],
        o2[None],
        og,
        os,
        gate.T[None],
        t1[None],
        t2.T[None],
        t3,
    )


def solution(mesh):
    placed = (
        P("dp", None),
        P("dp", None),
        P("task", "dp"),
        P("task", None, "dp", None),
        P("task", None, "dp", None),
        P("task", None, None),
        P("task", None, None),
        P("task", "dp", None),
        P("task", "dp", None),
        P("task", None),
        P("task", None),
        P("task", None, None),
        P("task", None, None),
        P("task", None, None),
        P("task", None),
    )
    return jax.shard_map(
        per_device,
        mesh=mesh,
        in_specs=placed,
        out_specs=(
            P("task", "dp"),
            P("dp", None),
            P("task", None, "dp", None),
            P("task", None, "dp", None),
            P("task", None, None),
            P("task", None, None),
            P("task", "dp", None),
            P("task", "dp", None),
            P("task", None),
            P("task", None),
            P("task", None, None),
            P("task", None, None),
            P("task", None, None),
            P("task", None),
        ),
        check_vma=False,
    )
```

```python
import functools

import jax
import jax.numpy as jnp
from jax import lax
from jax.experimental import pallas as pl
from jax.experimental.pallas import tpu as pltpu
from jax.sharding import PartitionSpec as P

EXPERTS = 2
GATES = 4
D = 512
HID = 256
TOWER1 = 128
TOWER2 = 64
EMB = 64
FEATS = 8
LANES = 128
BAGS = 128
EVB = BAGS // FEATS
ROWS = 128
EPSILON = 1e-05
K0 = 0.7978845608028654
K1 = K0 * 0.044715
SLOTS = 3
BIG = 2 * SLOTS
WIDE = BIG * HID
HALF = SLOTS * HID
PIECE = 32
SPAN = 256
BF = jnp.bfloat16
F32 = jnp.float32

T1_AT = 0
T2_AT = T1_AT + HID
GATE_AT = T2_AT + TOWER2
MISC_AT = GATE_AT + GATES * (D // LANES)
LABEL_AT = MISC_AT + 16
G_ROWS = LABEL_AT
SMALL_ROWS = G_ROWS // 2


def nn(left, right):
    return jnp.dot(left, right, preferred_element_type=F32)


def nt(left, right):
    return lax.dot_general(left, right, (((1,), (1,)), ((), ())), preferred_element_type=F32)


def tn(left, right):
    return lax.dot_general(left, right, (((0,), (0,)), ((), ())), preferred_element_type=F32)


def params(mib, **kwargs):
    return pltpu.CompilerParams(vmem_limit_bytes=mib * 1024 * 1024, **kwargs)


def cost(flops, moved):
    return pl.CostEstimate(flops=int(flops), bytes_accessed=int(moved), transcendentals=0)


def shape(dims, kind=BF):
    return jax.ShapeDtypeStruct(dims, kind)


VSPEC = pl.BlockSpec(memory_space=pltpu.VMEM)
SSPEC = pl.BlockSpec(memory_space=pltpu.SMEM)
ASPEC = pl.BlockSpec(memory_space=pl.ANY)


def line(ref, row):
    both = ref[row : row + 1, :].astype(F32)
    return [both[:, :LANES], both[:, LANES:]]


def bags_kernel(blocks, chunks, len_ref, st_ref, en_ref, meta_ref):
    k = lax.broadcasted_iota(jnp.int32, (BAGS, BAGS), 0)
    j = lax.broadcasted_iota(jnp.int32, (BAGS, BAGS), 1)
    natural = (j % EVB) * FEATS + j // EVB
    before = jnp.where(k < natural, 1.0, 0.0).astype(BF)
    same = jnp.where(k == natural, 1.0, 0.0).astype(BF)
    lens_f = jnp.concatenate(
        [len_ref[:, b * BAGS : (b + 1) * BAGS] for b in range(blocks)], axis=0
    ).astype(F32)
    lens = lens_f.astype(BF)
    in_block = nn(lens, before)
    own = nn(lens, same)
    sums = jnp.sum(lens_f, axis=1, keepdims=True)
    high = jnp.floor(sums * (1.0 / 128.0))
    low = sums - high * 128.0
    bi = lax.broadcasted_iota(jnp.int32, (blocks, blocks), 0)
    bj = lax.broadcasted_iota(jnp.int32, (blocks, blocks), 1)
    lower = jnp.where(bj < bi, 1.0, 0.0).astype(BF)
    offset = 128.0 * nn(lower, jnp.broadcast_to(high, (blocks, BAGS)).astype(BF)) + nn(
        lower, jnp.broadcast_to(low, (blocks, BAGS)).astype(BF)
    )
    starts = offset + in_block
    st_ref[pl.ds(0, blocks), :] = starts.astype(jnp.int32)
    en_ref[pl.ds(0, blocks), :] = (starts + own).astype(jnp.int32)
    past = jnp.full((8, BAGS), chunks * ROWS, jnp.int32)
    st_ref[pl.ds(blocks, 8), :] = past
    en_ref[pl.ds(blocks, 8), :] = past
    lanes = meta_ref.shape[1]
    begins = jnp.concatenate([offset] * (lanes // BAGS), axis=1)
    row = lax.broadcasted_iota(jnp.int32, (blocks, lanes), 0)
    col = lax.broadcasted_iota(jnp.int32, (blocks, lanes), 1)
    begin = jnp.sum(jnp.where(row == col, begins, 0.0), axis=0, keepdims=True)
    spot = lax.broadcasted_iota(jnp.int32, (1, lanes), 1)
    begin = jnp.where(spot >= blocks, float(chunks * ROWS), begin)
    reached = jnp.where(begins <= (col * ROWS).astype(F32), 1.0, 0.0)
    first = jnp.sum(reached, axis=0, keepdims=True) - 1.0
    meta_ref[0:1, :] = begin.astype(jnp.int32)
    meta_ref[1:2, :] = first.astype(jnp.int32)


def small_kernel(
    ids_ref,
    label_ref,
    sgain_ref,
    sshift_ref,
    ogain_ref,
    oshift_ref,
    gate_ref,
    t1_ref,
    t2_ref,
    t3_ref,
    small_ref,
):
    small_ref[T1_AT : T1_AT + HID, :] = t1_ref[...]
    small_ref[T2_AT : T2_AT + TOWER2, :] = t2_ref[...]
    gate = gate_ref[...].astype(F32)
    turned = jnp.concatenate([gate[0:2], gate[3:4], gate[2:3]], axis=0)
    gate = jnp.where(ids_ref[0] == 0, gate, turned)
    lines = [gate[g : g + 1, p * LANES : (p + 1) * LANES] for g in range(GATES) for p in range(D // LANES)]
    lines += line(sgain_ref, 0) + line(sgain_ref, 1) + line(ogain_ref, 0)
    lines += line(sshift_ref, 0) + line(sshift_ref, 1) + line(oshift_ref, 0)
    lines += [jnp.concatenate([t3_ref[...].astype(F32)] * 2, axis=1), jnp.zeros((3, LANES), F32)]
    events = label_ref.shape[1]
    lines += [label_ref[:, p * LANES : (p + 1) * LANES].astype(F32) for p in range(events // LANES)]
    lines += [jnp.zeros((16 - events // LANES, LANES), F32)]
    small_ref[pl.ds(GATE_AT, 48), :] = jnp.concatenate(lines, axis=0).astype(BF)


def bags(lengths, chunks):
    blocks = lengths.shape[1] // BAGS
    lanes = -(-max(blocks + 1, chunks) // LANES) * LANES
    bounds = shape((blocks + 8, BAGS), jnp.int32)
    return pl.pallas_call(
        functools.partial(bags_kernel, blocks, chunks),
        out_shape=(bounds, bounds, shape((2, lanes), jnp.int32)),
        in_specs=[VSPEC],
        out_specs=(VSPEC,) * 3,
        compiler_params=params(4),
        cost_estimate=cost(1e9, 1e6),
    )(lengths)


def pack_small(ids, *arrays):
    return pl.pallas_call(
        small_kernel,
        out_shape=shape((LABEL_AT + 16, LANES)),
        in_specs=[SSPEC] + [VSPEC] * len(arrays),
        out_specs=VSPEC,
        compiler_params=params(56),
        cost_estimate=cost(1e9, 1e6),
    )(ids, *arrays)


def one_hot(starts, ends, base):
    row = lax.broadcasted_iota(jnp.int32, (ROWS, 2 * BAGS), 0).astype(F32).astype(BF)
    low = jnp.clip(starts - base, 0, ROWS).astype(F32).astype(BF)
    high = jnp.clip(ends - base, 0, ROWS).astype(F32).astype(BF)
    return jnp.where((row >= low) & (row < high), jnp.ones((), BF), jnp.zeros((), BF))


def window(ref, block):
    first = ref[pl.ds(block, 1), :]
    second = ref[pl.ds(block + 1, 1), :]
    return jnp.concatenate([first, second], axis=1)


def pool_kernel(skip, count, half_blocks, chunks, ids_ref, meta_ref, st_ref, en_ref, ent_ref, *refs):
    x_ref, acc_ref = refs[-2:]
    base_block = ids_ref[0] * half_blocks + skip

    def clear(i, carry):
        at = pl.multiple_of((base_block + i) * BAGS, BAGS)
        acc_ref[:, pl.ds(at, BAGS)] = jnp.zeros((EMB, BAGS), F32)
        return carry

    lax.fori_loop(0, count, clear, 0, unroll=True)

    low_chunk = meta_ref[0, base_block] // ROWS
    high_chunk = (meta_ref[0, base_block + count] + ROWS - 1) // ROWS
    step = 9

    def chunk(i, carry):
        for u in range(step):
            c = low_chunk + i * step + u
            inside = jnp.minimum(c, chunks - 1)
            block = meta_ref[1, inside]
            at = pl.multiple_of(inside * ROWS, ROWS)
            picked = one_hot(window(st_ref, block), window(en_ref, block), c * ROWS)
            part = nn(ent_ref[:, pl.ds(at, ROWS)], picked)
            to = pl.multiple_of(block * BAGS, BAGS)
            acc_ref[:, pl.ds(to, 2 * BAGS)] += part
        return carry

    lax.fori_loop(0, (high_chunk - low_chunk + step - 1) // step, chunk, 0)

    def place(i, carry):
        at = pl.multiple_of((base_block + i) * BAGS, BAGS)
        to = pl.multiple_of(i * EVB, EVB)
        block = acc_ref[:, pl.ds(at, BAGS)].T
        for pair in range(FEATS // 2):
            left = block[2 * pair * EVB : (2 * pair + 1) * EVB]
            right = block[(2 * pair + 1) * EVB : (2 * pair + 2) * EVB]
            x_ref[pl.ds(to, EVB), pair * 2 * EMB : (pair + 1) * 2 * EMB] = jnp.concatenate(
                [left, right], axis=1
            ).astype(BF)
        return carry

    lax.fori_loop(0, count, place, 0, unroll=12)


def pool(part, parts, ids, meta, starts, ends, entries, *after):
    blocks = starts.shape[0] - 8
    half_blocks = blocks // 2
    count = half_blocks // parts
    chunks = entries.shape[1] // ROWS
    return pl.pallas_call(
        functools.partial(pool_kernel, part * count, count, half_blocks, chunks),
        out_shape=shape((count * EVB, D)),
        in_specs=[SSPEC, SSPEC, VSPEC, VSPEC, VSPEC] + [ASPEC] * len(after),
        out_specs=VSPEC,
        scratch_shapes=[pltpu.VMEM((EMB, (blocks + 1) * BAGS), F32)],
        compiler_params=params(16),
        cost_estimate=cost(10e9, 5e6),
    )(ids, meta, starts, ends, entries, *after)


def expand_kernel(half_blocks, group, ids_ref, meta_ref, st_ref, en_ref, own_ref, other_ref, out_ref, pred_ref, token_ref, rows_ref):
    position = ids_ref[0]
    step = pl.program_id(0)
    events = half_blocks * EVB

    @pl.when(step == 0)
    def _():
        for source, half in ((own_ref, position), (other_ref, 1 - position)):

            def place(i, carry):
                at = pl.multiple_of(i * EVB, EVB)
                to = pl.multiple_of((half * half_blocks + i) * BAGS, BAGS)
                for pair in range(FEATS // 2):
                    tile = source[pl.ds(at, EVB), pair * 2 * EMB : (pair + 1) * 2 * EMB]
                    rows_ref[pl.ds(to + 2 * pair * EVB, EVB), :] = tile[:, :EMB]
                    rows_ref[pl.ds(to + (2 * pair + 1) * EVB, EVB), :] = tile[:, EMB:]
                return carry

            lax.fori_loop(0, half_blocks, place, 0, unroll=12)
        rows_ref[pl.ds(2 * half_blocks * BAGS, BAGS), :] = jnp.zeros((BAGS, EMB), BF)
        own = own_ref[events : events + 16, : 2 * LANES].astype(F32)
        other = other_ref[events : events + 16, : 2 * LANES].astype(F32)
        mine = (own[:, :LANES] + own[:, LANES:])[:8]
        theirs = (other[:, :LANES] + other[:, LANES:])[8:]
        halves = (jnp.where(position == 0, mine, theirs), jnp.where(position == 0, theirs, mine))
        tiles = events // LANES
        token_ref[...] = mine
        pred_ref[...] = jnp.concatenate([half[k : k + 1] for half in halves for k in range(tiles)], axis=1)

    for u in range(group):
        c = step * group + u
        block = meta_ref[1, c]
        picked = one_hot(window(st_ref, block), window(en_ref, block), c * ROWS)
        at = pl.multiple_of(block * BAGS, BAGS)
        out_ref[:, u * ROWS : (u + 1) * ROWS] = nn(picked, rows_ref[pl.ds(at, 2 * BAGS), :]).astype(BF).T


def expand(ids, meta, starts, ends, own, other, rows):
    blocks = starts.shape[0] - 8
    chunks = rows // ROWS
    group = 36
    while chunks % group:
        group -= 1
    return pl.pallas_call(
        functools.partial(expand_kernel, blocks // 2, group),
        grid=(chunks // group,),
        out_shape=(shape((EMB, rows)), shape((1, blocks * EVB), F32), shape((8, LANES), F32)),
        in_specs=[SSPEC, SSPEC, VSPEC, VSPEC, VSPEC, VSPEC],
        out_specs=(
            pl.BlockSpec((EMB, group * ROWS), lambda i: (0, i)),
            pl.BlockSpec((1, blocks * EVB), lambda i: (0, 0)),
            pl.BlockSpec((8, LANES), lambda i: (0, 0)),
        ),
        scratch_shapes=[pltpu.VMEM(((blocks + 1) * BAGS, EMB), BF)],
        compiler_params=params(24, dimension_semantics=("arbitrary",)),
        cost_estimate=cost(12e9, 6e6),
    )(ids, meta, starts, ends, own, other)


def gelu_twice(v):
    cube = K1 * (v * v)
    bend = jnp.tanh(v * (cube + K0))
    rise = 1.0 + bend
    act = v * rise
    slope = rise + act * (1.0 - bend) * (3.0 * cube + K0)
    return act, slope


def gelu_both(v):
    act, slope = gelu_twice(v)
    return 0.5 * act, 0.5 * slope


def wide(block, row):
    return jnp.concatenate([block[row : row + 1, :], block[row + 1 : row + 2, :]], axis=1)


def by_eight(value):
    return jnp.sum(value.reshape(-1, 8, value.shape[-1]), axis=0)


def plus(total, term):
    return term if total is None else total + term


def pieces_of(m):
    return [slice(at, at + PIECE) for at in range(m * HID, (m + 1) * HID, PIECE)]


def col_sum(value):
    return jnp.sum(value, axis=0, keepdims=True)


def lane_tiles(events, body):
    def step(j, carry):
        body(j, pl.ds(pl.multiple_of(j * LANES, LANES), LANES))
        return carry

    lax.fori_loop(0, events // LANES, step, 0)


def part(m):
    return slice(m * HID, (m + 1) * HID)


def pick(own, other, rows):
    if rows.start < HALF:
        return own.at[rows]
    return other.at[slice(rows.start - HALF, rows.stop - HALF)]


def spans_of(events):
    span = next(size for size in (SPAN, 2 * LANES, LANES) if events % size == 0)
    return [slice(at, at + span) for at in range(0, events, span)]


def rows_of(ids_ref, t, piece, rows1, rows2):
    if piece is None:
        return pl.ds(0, rows1), pl.ds(0, rows2)
    where = ids_ref[0] if t == 0 else 1 - ids_ref[0]
    d = ids_ref[1] ^ (4 * piece[2])
    if piece[1]:
        d = d ^ (2 - where)
    if piece[0]:
        d = d ^ (1 + where)
    return (
        pl.ds(pl.multiple_of(d * rows1, rows1), rows1),
        pl.ds(pl.multiple_of(d * rows2, rows2), rows2),
    )


def assemble(ids_ref, t, groups, given, rows1, rows2, w1_ref, w2_ref):
    for group, pieces in zip(groups, given):
        for g, piece in enumerate(pieces):
            one, two = rows_of(ids_ref, t, piece, rows1, rows2)
            for s in range(SLOTS):
                w1_ref[one, part(s)] = group[g, s * rows1 : (s + 1) * rows1, :]
                low = SLOTS * rows1 + s * rows2
                w2_ref[s, two, :] = (0.5 * group[g, low : low + rows2, :].astype(F32)).astype(BF)


def put(ids_ref, t, s, outs, plan, rows1, rows2, held_ref, first, value):
    held_ref[...] = value
    for out, (small_first, pieces) in zip(outs, plan):
        for g, piece in enumerate(pieces):
            mine = rows_of(ids_ref, t, piece, rows1, rows2)[0 if first else 1]
            at = g * SLOTS * (rows1 + rows2) + (SMALL_ROWS if small_first else 0)
            at, size = (at + s * rows1, rows1) if first else (at + SLOTS * rows1 + s * rows2, rows2)
            value = held_ref[mine, :]
            out[at : at + size, :] = (value if first else 0.5 * value).astype(BF)


def first_layer(s, w1_ref, x_ref, pc_ref):
    pc_ref[part(s), :] = tn(w1_ref[:, part(s)], x_ref[...])


def first_gelu(s, pc_ref, h_ref):
    for here in spans_of(pc_ref.shape[1]):
        for rows in pieces_of(s):
            act, slope = gelu_twice(pc_ref[rows, here])
            pc_ref[rows, here] = slope
            h_ref[rows, here] = act.astype(BF)


def front_kernel(xs, given, rows1, rows2, ids_ref, *refs):
    refs = list(refs)
    take = lambda n: [refs.pop(0) for _ in range(n)]
    x_parts, groups = take(xs), take(len(given))
    x_ref, w1_ref, w2_ref, pc_ref, h_ref = refs
    size = x_ref.shape[1] // xs
    for k, piece in enumerate(x_parts):
        x_ref[:, k * size : (k + 1) * size] = piece[...].T
    assemble(ids_ref, 0, groups, given, rows1, rows2, w1_ref, w2_ref)
    first_layer(0, w1_ref, x_ref, pc_ref)
    for s in range(SLOTS):
        if s + 1 < SLOTS:
            first_layer(s + 1, w1_ref, x_ref, pc_ref)
        first_gelu(s, pc_ref, h_ref)


def front(ids, x_parts, groups, given, rows1, rows2):
    events = sum(part.shape[0] for part in x_parts)
    outs = (
        shape((D, events)),
        shape((D, HALF)),
        shape((SLOTS, HID, HID)),
        shape((HALF, events), F32),
        shape((HALF, events)),
    )
    return pl.pallas_call(
        functools.partial(front_kernel, len(x_parts), given, rows1, rows2),
        out_shape=outs,
        in_specs=[SSPEC] + [VSPEC] * (len(x_parts) + len(groups)),
        out_specs=(VSPEC,) * len(outs),
        compiler_params=params(16),
        cost_estimate=cost(6e9, 4e6),
    )(ids, *x_parts, *groups)


def back_kernel(plan, rows1, rows2, ids_ref, x_ref, h_ref, e_ref, f_ref, small_ref, *refs):
    outs, (g1_ref, g2_ref) = refs[:-2], refs[-2:]
    for s in range(SLOTS):
        g2 = nt(h_ref[part(s), :], e_ref[part(s), :])
        put(ids_ref, 0, s, outs, plan, rows1, rows2, g2_ref.at[s % 2], False, g2)
        g1 = nt(x_ref[...], f_ref[part(s), :])
        put(ids_ref, 0, s, outs, plan, rows1, rows2, g1_ref.at[s % 2], True, g1)
    for out, (small_first, _) in zip(outs, plan):
        if small_first:
            out[:SMALL_ROWS, :] = small_ref[...]


def grad_shapes(plan, rows1, rows2):
    rows = SLOTS * (rows1 + rows2)
    return tuple(shape((len(pieces) * rows + small * SMALL_ROWS, HID)) for small, pieces in plan)


def back(ids, x, h, e, f, small, plan, rows1, rows2):
    outs = grad_shapes(plan, rows1, rows2)
    return pl.pallas_call(
        functools.partial(back_kernel, plan, rows1, rows2),
        out_shape=outs,
        in_specs=[SSPEC] + [VSPEC] * 5,
        out_specs=(VSPEC,) * len(outs),
        scratch_shapes=[pltpu.VMEM((2, D, HID), F32), pltpu.VMEM((2, HID, HID), F32)],
        compiler_params=params(16),
        cost_estimate=cost(6e9, 4e6),
    )(ids, x, h, e, f, small)


def main_kernel(given, plan, rows1, rows2, ids_ref, *refs):
    refs = list(refs)
    take = lambda n: [refs.pop(0) for _ in range(n)]
    x_ref, w1own_ref, w2own_ref, pcown_ref, hown_ref = take(5)
    oth_groups = take(len(given))
    packs = take(2)
    dx_ref, eown_ref, fown_ref, small_ref = take(4)
    oth_outs = take(len(plan))
    wc_ref, w2_ref, gain_ref, third_ref, lab_ref, pc_ref, pb_ref, s2_ref, y_ref, h_ref, e_ref, fc_ref = take(12)
    scale_ref, lg_ref, prob_ref, q_ref, pt_ref, u1_ref, p4_ref, e2_ref, e1_ref, du_ref, dm_ref, dmb_ref = take(12)
    ds_ref, dn_ref, acc3_ref, pred_ref, g1_ref, g2_ref, dp_ref = take(7)
    position = ids_ref[0]
    events = x_ref.shape[1]

    def second_weights(m):
        return w2own_ref[m] if m < SLOTS else w2_ref[m - SLOTS]

    assemble(ids_ref, 1, oth_groups, given, rows1, rows2, wc_ref, w2_ref)
    lines = []
    for t in range(2):
        block = packs[t][GATE_AT : GATE_AT + 16, :].astype(F32)
        for g in range(GATES):
            lines.append(
                jnp.concatenate([block[4 * g + p : 4 * g + p + 1, :] for p in range(D // LANES)], axis=1)
            )
        lines.append(jnp.zeros((8 - GATES, D), F32))
    gates = jnp.concatenate(lines, axis=0).astype(BF)
    wc_ref[:, HALF:] = jnp.concatenate([gates, jnp.zeros((LANES - 16, D), BF)], axis=0).T
    fc_ref[HALF:, :] = jnp.zeros((LANES, events), BF)
    acc3_ref[...] = jnp.zeros_like(acc3_ref)
    miscs = [packs[t][MISC_AT : MISC_AT + 16, :].astype(F32) for t in range(2)]
    for t in range(2):
        misc = miscs[t]
        for s in range(SLOTS):
            for kind in range(2):
                for half in range(2):
                    at = 2 * (kind * SLOTS + s) + half
                    to = ((kind * 2 + t) * SLOTS + s) * HID + half * LANES
                    gain_ref[to : to + LANES, :] = jnp.broadcast_to(misc[at : at + 1, :], (LANES, LANES)).T
        third = jnp.broadcast_to(misc[12:13, :], (LANES, LANES)).T
        third_ref[t * TOWER2 : (t + 1) * TOWER2, :] = third[:TOWER2]
        lab_ref[t * 16 : (t + 1) * 16, :] = packs[t][LABEL_AT : LABEL_AT + 16, :].astype(F32)

    lg_ref[...] = nn(gates, x_ref[...])
    spans = spans_of(events)

    def second_gelu(m, here):
        total = None
        for rows in pieces_of(m):
            act, slope = gelu_twice(pb_ref[rows, here])
            pb_ref[rows, here] = act
            s2_ref[rows, here] = slope
            total = plus(total, by_eight(act))
        mean = col_sum(total) * (1.0 / HID)
        total = None
        for rows in pieces_of(m):
            centred = pb_ref[rows, here] - mean
            pb_ref[rows, here] = centred
            total = plus(total, by_eight(centred * centred))
        scale = lax.rsqrt(col_sum(total) * (1.0 / HID) + 4.0 * EPSILON)
        scale_ref[m : m + 1, here] = scale
        for rows in pieces_of(m):
            normed = pb_ref[rows, here] * scale
            pb_ref[rows, here] = normed
            for lanes in range(here.start, here.stop, LANES):
                block = slice(lanes, lanes + LANES)
                out = pb_ref[rows, block] * gain_ref[rows, :] + gain_ref[slice(WIDE + rows.start, WIDE + rows.stop), :]
                if m % SLOTS == SLOTS - 1:
                    out = out.astype(BF).astype(F32)
                y_ref[rows, block] = out

    turn = [m for s in range(SLOTS) for m in (s, SLOTS + s)]
    first_layer(0, wc_ref, x_ref, pc_ref)
    for i, m in enumerate(turn):
        s = m - SLOTS
        if s >= 0:
            if s + 1 < SLOTS:
                first_layer(s + 1, wc_ref, x_ref, pc_ref)
            first_gelu(s, pc_ref, h_ref)
        pb_ref[part(m), :] = tn(second_weights(m), pick(hown_ref, h_ref, part(m))[...])
        if i:
            for here in spans:
                second_gelu(turn[i - 1], here)
    for here in spans:
        second_gelu(turn[-1], here)
    orders = [(t * SLOTS, t * SLOTS + 1, t * SLOTS + 2, (1 - t) * SLOTS + 2) for t in range(2)]

    prob_ref[...] = jnp.ones_like(prob_ref)

    def mix(j, here):
        for t in range(2):
            logits = [lg_ref[8 * t + k : 8 * t + k + 1, here] for k in range(GATES)]
            top = jnp.maximum(jnp.maximum(logits[0], logits[1]), jnp.maximum(logits[2], logits[3]))
            raised = [jnp.exp(logit - top) for logit in logits]
            scale = 1.0 / (raised[0] + raised[1] + raised[2] + raised[3])
            mixture = None
            for k in range(GATES):
                prob = raised[k] * scale
                prob_ref[8 * t + k : 8 * t + k + 1, here] = prob
                term = prob * y_ref[part(orders[t][k]), here]
                mixture = term if mixture is None else mixture + term
            q_ref[part(t), here] = mixture.astype(BF)

    lane_tiles(events, mix)
    for t in range(2):
        pt_ref[t * TOWER1 : (t + 1) * TOWER1, :] = tn(packs[t][T1_AT : T1_AT + HID, :], q_ref[part(t), :])

    def tower_gelu(j, here):
        act, slope = gelu_both(pt_ref[:, here])
        pt_ref[:, here] = slope
        u1_ref[:, here] = act.astype(BF)

    lane_tiles(events, tower_gelu)
    for t in range(2):
        p4_ref[t * TOWER2 : (t + 1) * TOWER2, :] = nn(
            packs[t][T2_AT : T2_AT + TOWER2, :], u1_ref[t * TOWER1 : (t + 1) * TOWER1, :]
        )

    def head(j, here):
        act, slope = gelu_both(p4_ref[:, here])
        u2 = act.astype(BF).astype(F32)
        product = u2 * third_ref[...]
        deltas = []
        for t in range(2):
            logit = col_sum(product[t * TOWER2 : (t + 1) * TOWER2])
            prediction = 1.0 / (1.0 + jnp.exp(-logit))
            pred_ref[pl.ds(8 * t + j, 1), :] = prediction
            label = lab_ref[pl.ds(t * 16 + position * (events // LANES) + j, 1), :]
            deltas.append(jnp.broadcast_to(prediction - label, (TOWER2, LANES)))
        delta = jnp.concatenate(deltas, axis=0)
        acc3_ref[...] += delta * u2
        e2_ref[:, here] = (slope * (delta * third_ref[...])).astype(BF)

    lane_tiles(events, head)
    for t in range(2):
        du_ref[t * TOWER1 : (t + 1) * TOWER1, :] = tn(
            packs[t][T2_AT : T2_AT + TOWER2, :], e2_ref[t * TOWER2 : (t + 1) * TOWER2, :]
        )

    def tower_back(j, here):
        e1_ref[:, here] = (pt_ref[:, here] * du_ref[:, here]).astype(BF)

    lane_tiles(events, tower_back)
    for t in range(2):
        mixed = nn(packs[t][T1_AT : T1_AT + HID, :], e1_ref[t * TOWER1 : (t + 1) * TOWER1, :])
        dm_ref[part(t), :] = mixed
        dmb_ref[part(t), :] = mixed.astype(BF)
        rows = [wide(miscs[t], 2 * (SLOTS + s)) for s in range(EXPERTS)] + [jnp.zeros((8 - EXPERTS, HID), F32)]
        ds_ref[8 * t : 8 * t + 8, :] = nn(jnp.concatenate(rows, axis=0).astype(BF), dmb_ref[part(t), :])

    def probs_of(t, k, here):
        return prob_ref[8 * t + k : 8 * t + k + 1, here]

    def shared_probs(here):
        for t in range(2):
            for k in range(EXPERTS, GATES):
                total = None
                for mine, rows in zip(pieces_of(t), pieces_of(orders[t][k])):
                    total = plus(total, by_eight(dm_ref[mine, here] * y_ref[rows, here]))
                dp_ref[8 * t + k : 8 * t + k + 1, here] = col_sum(total)

    def norm_back(m, here):
        t, s = divmod(m, SLOTS)
        one, two = None, None
        for rows in pieces_of(m):
            mine = slice(rows.start - m * HID + t * HID, rows.stop - m * HID + t * HID)
            for lanes in range(here.start, here.stop, LANES):
                block = slice(lanes, lanes + LANES)
                up = dm_ref[mine, block]
                if s == SLOTS - 1:
                    theirs = slice(mine.start + (1 - 2 * t) * HID, mine.stop + (1 - 2 * t) * HID)
                    up = probs_of(t, s, block) * up + probs_of(1 - t, SLOTS, block) * dm_ref[theirs, block]
                y_ref[rows, block] = up * gain_ref[rows, :]
            d_normed = y_ref[rows, here]
            product = d_normed * pb_ref[rows, here]
            dn_ref[rows, here] = product.astype(BF)
            one = plus(one, by_eight(d_normed))
            two = plus(two, by_eight(product))
        one, two = col_sum(one), col_sum(two)
        outer = scale_ref[m : m + 1, here]
        if s < EXPERTS:
            outer = outer * probs_of(t, s, here)
            dp_ref[8 * t + s : 8 * t + s + 1, here] = two + ds_ref[8 * t + s : 8 * t + s + 1, here]
        one, two = one * (1.0 / HID), two * (1.0 / HID)
        for rows in pieces_of(m):
            inner = y_ref[rows, here] - one - pb_ref[rows, here] * two
            pick(eown_ref, e_ref, rows)[:, here] = (s2_ref[rows, here] * outer * inner).astype(BF)

    for here in spans:
        shared_probs(here)
    turn = [m for s in range(SLOTS) for m in (SLOTS + s, s)]
    for here in spans:
        norm_back(turn[0], here)
    for i, m in enumerate(turn):
        y_ref[part(m), :] = nn(second_weights(m), pick(eown_ref, e_ref, part(m))[...])
        s = m - SLOTS
        if s >= 0:
            g2 = nt(h_ref[part(s), :], e_ref[part(s), :])
            put(ids_ref, 1, s, oth_outs, plan, rows1, rows2, g2_ref.at[s % 2], False, g2)
        if i + 1 < BIG:
            for here in spans:
                norm_back(turn[i + 1], here)
        for here in spans:
            for rows in pieces_of(m):
                value = pick(pcown_ref, pc_ref, rows)[:, here] * y_ref[rows, here]
                pick(fown_ref, fc_ref, rows)[:, here] = value.astype(BF)
        if s >= 0:
            g1 = nt(x_ref[...], fc_ref[part(s), :])
            put(ids_ref, 1, s, oth_outs, plan, rows1, rows2, g1_ref.at[s % 2], True, g1)
    codes = []
    for t in range(2):
        probs = [probs_of(t, k, slice(None)) for k in range(GATES)]
        d_probs = [dp_ref[8 * t + k : 8 * t + k + 1, :] for k in range(GATES)]
        weighted = probs[0] * d_probs[0]
        for k in range(1, GATES):
            weighted = weighted + probs[k] * d_probs[k]
        codes += [probs[k] * (d_probs[k] - weighted) for k in range(GATES)]
        codes.append(jnp.zeros((8 - GATES, events), F32))
    fc_ref[HALF : HALF + 16, :] = jnp.concatenate(codes, axis=0).astype(BF)
    dx = nn(w1own_ref[...], fown_ref[...]) + nn(wc_ref[...], fc_ref[...])
    dx_ref[:events, :] = dx.astype(BF).T
    pred = pred_ref[...]
    high = pred.astype(BF)
    low = (pred - high.astype(F32)).astype(BF)
    dx_ref[events:, :] = jnp.concatenate([high, low, high, low], axis=1)

    gate_grad = nt(fc_ref[HALF : HALF + 16, :], x_ref[...])
    weights = prob_ref[...].astype(BF)
    shifts = [nt(weights, dmb_ref[part(t), :]) for t in range(2)]
    third_grad = col_sum(acc3_ref[...].T)
    for t in range(2):
        tower = slice(t * TOWER1, (t + 1) * TOWER1)
        half = slice(t * TOWER2, (t + 1) * TOWER2)
        lines = []
        for g in range(GATES):
            row = gate_grad[8 * t + g : 8 * t + g + 1, :]
            lines += [row[:, p * LANES : (p + 1) * LANES] for p in range(D // LANES)]
        for s in range(SLOTS):
            at = 8 * t + (s if s < EXPERTS else GATES)
            row = nt(weights, dn_ref[part(t * SLOTS + s), :])[at : at + 1, :] / wide(miscs[t], 2 * s)
            lines += [row[:, :LANES], row[:, LANES:]]
        for s in range(SLOTS):
            row = shifts[t][8 * t + s : 8 * t + s + 1, :]
            if s == SLOTS - 1:
                row = row + shifts[1 - t][8 * (1 - t) + SLOTS : 8 * (1 - t) + SLOTS + 1, :]
            lines += [row[:, :LANES], row[:, LANES:]]
        lines.append(third_grad if t == 0 else pltpu.roll(third_grad, TOWER2, 1))
        lines.append(jnp.zeros((3, LANES), F32))
        small = jnp.concatenate(
            [
                nt(q_ref[part(t), :], e1_ref[tower, :]),
                nt(e2_ref[half, :], u1_ref[tower, :]),
                jnp.concatenate(lines, axis=0),
            ],
            axis=0,
        )
        small = jnp.concatenate([small[:SMALL_ROWS], small[SMALL_ROWS:]], axis=1).astype(BF)
        if t == 0:
            small_ref[...] = small
            continue
        for out, (small_first, _) in zip(oth_outs, plan):
            if small_first:
                out[:SMALL_ROWS, :] = small


def layer(ids, started, oth_groups, own_pack, oth_pack, given, plan, rows1, rows2):
    events = started[0].shape[1]
    half = shape((HALF, events))
    results = (shape((events + 16, D)), half, half, shape((SMALL_ROWS, HID))) + grad_shapes(plan, rows1, rows2)
    scratch = [
        ((D, HALF + LANES), BF),
        ((SLOTS, HID, HID), BF),
        ((2 * WIDE, LANES), F32),
        ((2 * TOWER2, LANES), F32),
        ((32, LANES), F32),
        ((HALF, events), F32),
        ((WIDE, events), F32),
        ((WIDE, events), F32),
        ((WIDE, events), F32),
        ((HALF, events), BF),
        ((HALF, events), BF),
        ((HALF + LANES, events), BF),
        ((8, events), F32),
        ((16, events), F32),
        ((16, events), F32),
        ((2 * HID, events), BF),
        ((2 * TOWER1, events), F32),
        ((2 * TOWER1, events), BF),
        ((2 * TOWER2, events), F32),
        ((2 * TOWER2, events), BF),
        ((2 * TOWER1, events), BF),
        ((2 * TOWER1, events), F32),
        ((2 * HID, events), F32),
        ((2 * HID, events), BF),
        ((16, events), F32),
        ((WIDE, events), BF),
        ((2 * TOWER2, LANES), F32),
        ((16, LANES), F32),
        ((2, D, HID), F32),
        ((2, HID, HID), F32),
        ((16, events), F32),
    ]
    arrays = [*started, *oth_groups, own_pack, oth_pack]
    return pl.pallas_call(
        functools.partial(main_kernel, given, plan, rows1, rows2),
        out_shape=results,
        in_specs=[SSPEC] + [VSPEC] * len(arrays),
        out_specs=(VSPEC,) * len(results),
        scratch_shapes=[pltpu.VMEM(dims, kind) for dims, kind in scratch],
        compiler_params=params(42),
        cost_estimate=cost(events * BIG * 196608 * 6, 10e6),
    )(ids, *arrays)


def sibling(value):
    return lax.ppermute(value, "task", [(0, 1), (1, 0)])


def flipped(value, mask):
    pairs = [(i, i ^ mask) for i in range(lax.axis_size("dp"))]
    return lax.ppermute(value, "dp", pairs)


def crossed(value, masks):
    n = lax.axis_size("dp")
    pairs = [(t * n + i, t * n + (i ^ masks[t])) for t in range(2) for i in range(n)]
    return lax.ppermute(value, ("task", "dp"), pairs)


def stack_kernel(count, *refs):
    out, sems = refs[-2:]
    copies = [pltpu.make_async_copy(refs[k], out.at[k], sems.at[k]) for k in range(count)]
    for copy in copies:
        copy.start()
    for copy in copies:
        copy.wait()


def stacked(pieces):
    return pl.pallas_call(
        functools.partial(stack_kernel, len(pieces)),
        out_shape=shape((len(pieces),) + pieces[0].shape, pieces[0].dtype),
        in_specs=[ASPEC] * len(pieces),
        out_specs=VSPEC,
        scratch_shapes=[pltpu.SemaphoreType.DMA((len(pieces),))],
        compiler_params=params(4),
        cost_estimate=cost(0, 1e6),
    )(*pieces)


def summed(*terms):
    total = terms[0].astype(F32)
    for term in terms[1:]:
        total = total + term.astype(F32)
    return total.astype(BF)


def small_sum_kernel(one_ref, two_ref, *refs):
    out_ref = refs[-1]
    out_ref[...] = (one_ref[...].astype(F32) + two_ref[...].astype(F32)).astype(BF)


def small_sum(one, two, *after):
    lead = pl.BlockSpec((SMALL_ROWS, HID), lambda i: (0, 0))
    return pl.pallas_call(
        small_sum_kernel,
        grid=(1,),
        out_shape=shape((SMALL_ROWS, HID)),
        in_specs=[lead, lead] + [ASPEC] * len(after),
        out_specs=lead,
        compiler_params=params(4),
        cost_estimate=cost(8e9, 1e6),
    )(one, two, *after)


def tie_kernel(*refs):
    pass


def tied(value, after):
    return pl.pallas_call(
        tie_kernel,
        out_shape=shape(value.shape, value.dtype),
        in_specs=[ASPEC, ASPEC],
        out_specs=ASPEC,
        input_output_aliases={0: 0},
        compiler_params=params(1),
        cost_estimate=cost(0, 1),
    )(value, after)


def far_kernel(rows, keep_ref, got_ref, mid_ref, near_ref, *outs):
    for k, out in enumerate(outs):
        here = slice(k * rows, (k + 1) * rows)
        total = keep_ref[here, :].astype(F32) + got_ref[here, :].astype(F32)
        at = SMALL_ROWS + k * rows
        total = total + mid_ref[at : at + rows, :].astype(F32)
        out[...] = (total + near_ref[here, :].astype(F32)).astype(BF)


def block(rows, at=0):
    return pl.BlockSpec((rows, HID), lambda i: (at, 0))


def far_messages(far, rows, keep, got, mid, near):
    size = far * rows
    return pl.pallas_call(
        functools.partial(far_kernel, rows),
        grid=(1,),
        out_shape=(shape((rows, HID)),) * far,
        in_specs=[block(size), block(size), block(size + SMALL_ROWS), block(size)],
        out_specs=(block(rows),) * far,
        compiler_params=params(12),
        cost_estimate=cost(0, 4e6),
    )(keep, got, mid, near)


def home_kernel(rows, keep_ref, got_ref, mid_ref, *refs):
    smalls, (message_ref, base_ref) = refs[:-2], refs[-2:]
    total = keep_ref[...].astype(F32) + got_ref[...].astype(F32) + mid_ref[...].astype(F32)
    base_ref[...] = total[:rows]
    message_ref[SMALL_ROWS:, :] = total[rows:].astype(BF)
    small = smalls[0][...].astype(F32)
    for term in smalls[1:]:
        small = small + term[...].astype(F32)
    message_ref[:SMALL_ROWS, :] = small.astype(BF)


def home_message(far, rows, keep, got, mid, smalls):
    at = block(2 * rows, far)
    return pl.pallas_call(
        functools.partial(home_kernel, rows),
        grid=(1,),
        out_shape=(shape((SMALL_ROWS + rows, HID)), shape((rows, HID), F32)),
        in_specs=[at, at, block(2 * rows)] + [block(SMALL_ROWS)] * len(smalls),
        out_specs=(block(SMALL_ROWS + rows), block(rows)),
        compiler_params=params(8),
        cost_estimate=cost(0, 2e6),
    )(keep, got, mid, *smalls)


def total_kernel(*refs):
    total = refs[0][...].astype(F32)
    for term in refs[1:-1]:
        total = total + term[...].astype(F32)
    refs[-1][...] = total


def totalled(*terms):
    return pl.pallas_call(
        total_kernel,
        out_shape=shape(terms[0].shape, F32),
        in_specs=[VSPEC] * len(terms),
        out_specs=VSPEC,
        compiler_params=params(4),
        cost_estimate=cost(10e9, 1e6),
    )(*terms)


def last_kernel(rows1, rows2, paired, ids_ref, *refs):
    if paired:
        part_ref, sent_ref, near_ref = refs[:3]
        total = part_ref[...] + near_ref[SMALL_ROWS:, :].astype(F32)
        small = sent_ref[:SMALL_ROWS, :].astype(F32) + near_ref[:SMALL_ROWS, :].astype(F32)
    else:
        total, small = refs[0][...], refs[1][...]
    w1_ref, w2_ref, o1_ref, o2_ref, sg_ref, ss_ref, og_ref, os_ref, gate_ref, t1_ref, t2_ref, t3_ref = refs[-12:]
    cut = SLOTS * rows1
    for s in range(EXPERTS):
        w1_ref[s] = total[s * rows1 : (s + 1) * rows1]
        w2_ref[s] = total[cut + s * rows2 : cut + (s + 1) * rows2]
    o1_ref[...] = total[EXPERTS * rows1 : cut]
    o2_ref[...] = total[cut + EXPERTS * rows2 :]
    tiny = jnp.concatenate([small[:, :LANES], small[:, LANES:]], axis=0)
    t1_ref[...] = tiny[T1_AT : T1_AT + HID]
    t2_ref[...] = tiny[T2_AT : T2_AT + TOWER2]
    gates = []
    for g in range(GATES):
        at = GATE_AT + 4 * g
        gates.append(jnp.concatenate([tiny[at + p : at + p + 1] for p in range(D // LANES)], axis=1))
    turned = ids_ref[0] != 0
    gate_ref[0:1, :] = gates[0]
    gate_ref[1:2, :] = gates[1]
    gate_ref[2:3, :] = jnp.where(turned, gates[3], gates[2])
    gate_ref[3:4, :] = jnp.where(turned, gates[2], gates[3])
    for kind, (spec, own) in enumerate(((sg_ref, og_ref), (ss_ref, os_ref))):
        for s in range(SLOTS):
            at = MISC_AT + 2 * (kind * SLOTS + s)
            row = jnp.concatenate([tiny[at : at + 1], tiny[at + 1 : at + 2]], axis=1)
            if s < EXPERTS:
                spec[s : s + 1, :] = row
            else:
                own[...] = row
    t3_ref[...] = tiny[MISC_AT + 12 : MISC_AT + 13, :TOWER2]


def finish(ids, terms, rows1, rows2):
    outs = (
        shape((EXPERTS, rows1, HID), F32),
        shape((EXPERTS, rows2, HID), F32),
        shape((rows1, HID), F32),
        shape((rows2, HID), F32),
        shape((EXPERTS, HID), F32),
        shape((EXPERTS, HID), F32),
        shape((1, HID), F32),
        shape((1, HID), F32),
        shape((GATES, D), F32),
        shape((HID, TOWER1), F32),
        shape((TOWER2, TOWER1), F32),
        shape((1, TOWER2), F32),
    )
    return pl.pallas_call(
        functools.partial(last_kernel, rows1, rows2, len(terms) == 3),
        out_shape=outs,
        in_specs=[SSPEC] + [VSPEC] * len(terms),
        out_specs=(VSPEC,) * len(outs),
        compiler_params=params(8),
        cost_estimate=cost(0, 2e6),
    )(ids, *terms)


def per_device(
    entries,
    lengths,
    labels,
    spec_w1,
    spec_w2,
    spec_gain,
    spec_shift,
    shared_w1,
    shared_w2,
    shared_gain,
    shared_shift,
    gate_w,
    tower_w1,
    tower_w2,
    tower_w3,
):
    position = lax.axis_index("task")
    n = lax.axis_size("dp")
    ids = jnp.stack([position, lax.axis_index("dp")]).astype(jnp.int32)
    rows1, rows2 = spec_w1.shape[2], spec_w2.shape[2]
    direct = rows2 % 16 == 0 and n % 4 == 0 and n & (n - 1) == 0
    pack = jnp.concatenate(
        [part.reshape(-1, HID) for part in (spec_w1, shared_w1, spec_w2, shared_w2)], axis=0
    )
    if direct:
        quarter = n // 4
        far = [pack] + [flipped(pack, 4 * k) for k in range(1, quarter)]

    rows = entries.shape[0]
    starts, ends, meta = bags(lengths, rows // ROWS)
    small = pack_small(
        ids,
        labels,
        spec_gain[0],
        spec_shift[0],
        shared_gain,
        shared_shift,
        gate_w[0].T,
        tower_w1[0],
        tower_w2[0].T,
        tower_w3,
    )
    other_small = sibling(small)
    turned = entries.T
    x_first = pool(0, 2, ids, meta, starts, ends, turned)

    if direct:
        zc = stacked(far)
        r1 = tied(crossed(zc, (1, 2)), x_first)
        r2 = crossed(tied(zc, x_first), (2, 1))
        x_second = pool(1, 2, ids, meta, starts, ends, turned, other_small)
        r3 = tied(crossed(r1, (2, 1)), x_second)
        own = [zc, r2, r1, r3]
        given = tuple(tuple((one, two, k) for k in range(quarter)) for one, two in ((0, 0), (0, 1), (1, 0), (1, 1)))
        far_ones = [(two, k) for two in range(2) for k in range(1, quarter)]
        home_ones = [(0, 0), (1, 0)]
        send = [(1, *piece) for piece in far_ones]
        keep = [(0, *piece) for piece in far_ones + home_ones] + [(1, *piece) for piece in home_ones]
        plan, used1, used2 = ((0, tuple(keep)), (1, tuple(send))), rows1, rows2
    else:
        x_second = pool(1, 2, ids, meta, starts, ends, turned)
        every = lax.all_gather(pack, "dp", axis=0)
        cut = SLOTS * rows1
        w1 = every[:, :cut].reshape(n, SLOTS, rows1, HID).swapaxes(0, 1).reshape(-1, HID)
        w2 = every[:, cut:].reshape(n, SLOTS, rows2, HID).swapaxes(0, 1).reshape(-1, HID)
        own = [jnp.concatenate([w1, w2], axis=0)[None]]
        given, plan, used1, used2 = ((None,),), ((1, (None,)),), D, HID
    other = [sibling(group) for group in own]
    started = front(ids, [x_first, x_second], own, given, used1, used2)
    dx, e, f, own_small, *oth_grads = layer(ids, started, other, small, other_small, given, plan, used1, used2)
    got = [sibling(grad) for grad in oth_grads[::-1]][::-1]
    own_grads = back(ids, started[0], started[4], e, f, own_small, plan, used1, used2)
    other_dx = sibling(dx)
    turned, predictions, expanded = expand(ids, meta, starts, ends, dx, other_dx, rows)
    piece = SLOTS * (rows1 + rows2)
    if direct:
        keep, send = own_grads
        far, cut = quarter - 1, (quarter - 1) * piece
        send = summed(send, got[1])
        mid = tied(crossed(send, (1, 2)), expanded)
        home = slice(2 * cut + 2 * piece, 2 * cut + 4 * piece)
        home = summed(keep[home], got[0][home])
        late = slice(cut, 2 * cut)
        near = crossed(summed(keep[late], got[0][late], mid[SMALL_ROWS + cut :]), (2, 1))
        small = small_sum(send, mid)
        home_mid = crossed(tied(home, mid), (1, 2))
        mask = 4
        while 2 * mask < n:
            small = summed(small, flipped(small, mask))
            mask *= 2
        smalls = [flipped(small, mask)]
        parts = far_messages(far, piece, keep, got[0], mid, near)
        smalls = [small] + [tied(term, parts[0]) for term in smalls]
        message, base = home_message(far, piece, keep, got[0], home_mid, smalls)
        parts = [flipped(part, 4 * (k + 1)) for k, part in enumerate(parts)]
        grads = finish(ids, [totalled(base, *parts), message, crossed(message, (2, 1))], rows1, rows2)
    else:
        whole = own_grads[0].astype(F32) + got[0].astype(F32)
        small = lax.psum(whole[:SMALL_ROWS], "dp")
        whole = whole[SMALL_ROWS:]
        cut = SLOTS * D
        g1 = lax.psum_scatter(whole[:cut].reshape(SLOTS, D, HID), "dp", scatter_dimension=1, tiled=True)
        g2 = lax.psum_scatter(whole[cut:].reshape(SLOTS, HID, HID), "dp", scatter_dimension=1, tiled=True)
        part = jnp.concatenate([g1.reshape(-1, HID), g2.reshape(-1, HID)], axis=0)
        grads = finish(ids, [part, small], rows1, rows2)
    w1, w2, o1, o2, sg, ss, og, os, gate, t1, t2, t3 = grads
    entry_grads = turned.T
    return (
        predictions,
        entry_grads,
        w1[None],
        w2[None],
        sg[None],
        ss[None],
        o1[None],
        o2[None],
        og,
        os,
        gate.T[None],
        t1[None],
        t2.T[None],
        t3,
    )


def solution(mesh):
    placed = (
        P("dp", None),
        P("dp", None),
        P("task", "dp"),
        P("task", None, "dp", None),
        P("task", None, "dp", None),
        P("task", None, None),
        P("task", None, None),
        P("task", "dp", None),
        P("task", "dp", None),
        P("task", None),
        P("task", None),
        P("task", None, None),
        P("task", None, None),
        P("task", None, None),
        P("task", None),
    )
    return jax.shard_map(
        per_device,
        mesh=mesh,
        in_specs=placed,
        out_specs=(
            P("task", "dp"),
            P("dp", None),
            P("task", None, "dp", None),
            P("task", None, "dp", None),
            P("task", None, None),
            P("task", None, None),
            P("task", "dp", None),
            P("task", "dp", None),
            P("task", None),
            P("task", None),
            P("task", None, None),
            P("task", None, None),
            P("task", None, None),
            P("task", None),
        ),
        check_vma=False,
    )
```

```python
import functools

import jax
import jax.numpy as jnp
from jax import lax
from jax.experimental import pallas as pl
from jax.experimental.pallas import tpu as pltpu
from jax.sharding import PartitionSpec as P

EXPERTS = 2
GATES = 4
D = 512
HID = 256
TOWER1 = 128
TOWER2 = 64
EMB = 64
FEATS = 8
LANES = 128
BAGS = 128
EVB = BAGS // FEATS
ROWS = 128
EPSILON = 1e-05
K0 = 0.7978845608028654
K1 = K0 * 0.044715
SLOTS = 3
BIG = 2 * SLOTS
WIDE = BIG * HID
HALF = SLOTS * HID
PIECE = 32
SPAN = 256
BF = jnp.bfloat16
F32 = jnp.float32

T1_AT = 0
T2_AT = T1_AT + HID
GATE_AT = T2_AT + TOWER2
MISC_AT = GATE_AT + GATES * (D // LANES)
LABEL_AT = MISC_AT + 16
G_ROWS = LABEL_AT
SMALL_ROWS = G_ROWS // 2


def nn(left, right):
    return jnp.dot(left, right, preferred_element_type=F32)


def nt(left, right):
    return lax.dot_general(left, right, (((1,), (1,)), ((), ())), preferred_element_type=F32)


def tn(left, right):
    return lax.dot_general(left, right, (((0,), (0,)), ((), ())), preferred_element_type=F32)


def params(mib, **kwargs):
    return pltpu.CompilerParams(vmem_limit_bytes=mib * 1024 * 1024, **kwargs)


def cost(flops, moved):
    return pl.CostEstimate(flops=int(flops), bytes_accessed=int(moved), transcendentals=0)


def shape(dims, kind=BF):
    return jax.ShapeDtypeStruct(dims, kind)


VSPEC = pl.BlockSpec(memory_space=pltpu.VMEM)
SSPEC = pl.BlockSpec(memory_space=pltpu.SMEM)
ASPEC = pl.BlockSpec(memory_space=pl.ANY)


def line(ref, row):
    both = ref[row : row + 1, :].astype(F32)
    return [both[:, :LANES], both[:, LANES:]]


def bags_kernel(blocks, chunks, len_ref, st_ref, en_ref, meta_ref):
    k = lax.broadcasted_iota(jnp.int32, (BAGS, BAGS), 0)
    j = lax.broadcasted_iota(jnp.int32, (BAGS, BAGS), 1)
    natural = (j % EVB) * FEATS + j // EVB
    before = jnp.where(k < natural, 1.0, 0.0).astype(BF)
    same = jnp.where(k == natural, 1.0, 0.0).astype(BF)
    lens_f = jnp.concatenate(
        [len_ref[:, b * BAGS : (b + 1) * BAGS] for b in range(blocks)], axis=0
    ).astype(F32)
    lens = lens_f.astype(BF)
    in_block = nn(lens, before)
    own = nn(lens, same)
    sums = jnp.sum(lens_f, axis=1, keepdims=True)
    high = jnp.floor(sums * (1.0 / 128.0))
    low = sums - high * 128.0
    bi = lax.broadcasted_iota(jnp.int32, (blocks, blocks), 0)
    bj = lax.broadcasted_iota(jnp.int32, (blocks, blocks), 1)
    lower = jnp.where(bj < bi, 1.0, 0.0).astype(BF)
    offset = 128.0 * nn(lower, jnp.broadcast_to(high, (blocks, BAGS)).astype(BF)) + nn(
        lower, jnp.broadcast_to(low, (blocks, BAGS)).astype(BF)
    )
    starts = offset + in_block
    st_ref[pl.ds(0, blocks), :] = starts.astype(jnp.int32)
    en_ref[pl.ds(0, blocks), :] = (starts + own).astype(jnp.int32)
    past = jnp.full((8, BAGS), chunks * ROWS, jnp.int32)
    st_ref[pl.ds(blocks, 8), :] = past
    en_ref[pl.ds(blocks, 8), :] = past
    lanes = meta_ref.shape[1]
    begins = jnp.concatenate([offset] * (lanes // BAGS), axis=1)
    row = lax.broadcasted_iota(jnp.int32, (blocks, lanes), 0)
    col = lax.broadcasted_iota(jnp.int32, (blocks, lanes), 1)
    begin = jnp.sum(jnp.where(row == col, begins, 0.0), axis=0, keepdims=True)
    spot = lax.broadcasted_iota(jnp.int32, (1, lanes), 1)
    begin = jnp.where(spot >= blocks, float(chunks * ROWS), begin)
    reached = jnp.where(begins <= (col * ROWS).astype(F32), 1.0, 0.0)
    first = jnp.sum(reached, axis=0, keepdims=True) - 1.0
    meta_ref[0:1, :] = begin.astype(jnp.int32)
    meta_ref[1:2, :] = first.astype(jnp.int32)


def small_kernel(
    ids_ref,
    label_ref,
    sgain_ref,
    sshift_ref,
    ogain_ref,
    oshift_ref,
    gate_ref,
    t1_ref,
    t2_ref,
    t3_ref,
    small_ref,
):
    small_ref[T1_AT : T1_AT + HID, :] = t1_ref[...]
    small_ref[T2_AT : T2_AT + TOWER2, :] = t2_ref[...]
    gate = gate_ref[...].astype(F32)
    turned = jnp.concatenate([gate[0:2], gate[3:4], gate[2:3]], axis=0)
    gate = jnp.where(ids_ref[0] == 0, gate, turned)
    lines = [gate[g : g + 1, p * LANES : (p + 1) * LANES] for g in range(GATES) for p in range(D // LANES)]
    lines += line(sgain_ref, 0) + line(sgain_ref, 1) + line(ogain_ref, 0)
    lines += line(sshift_ref, 0) + line(sshift_ref, 1) + line(oshift_ref, 0)
    lines += [jnp.concatenate([t3_ref[...].astype(F32)] * 2, axis=1), jnp.zeros((3, LANES), F32)]
    events = label_ref.shape[1]
    lines += [label_ref[:, p * LANES : (p + 1) * LANES].astype(F32) for p in range(events // LANES)]
    lines += [jnp.zeros((16 - events // LANES, LANES), F32)]
    small_ref[pl.ds(GATE_AT, 48), :] = jnp.concatenate(lines, axis=0).astype(BF)


def bags(lengths, chunks):
    blocks = lengths.shape[1] // BAGS
    lanes = -(-max(blocks + 1, chunks) // LANES) * LANES
    bounds = shape((blocks + 8, BAGS), jnp.int32)
    return pl.pallas_call(
        functools.partial(bags_kernel, blocks, chunks),
        out_shape=(bounds, bounds, shape((2, lanes), jnp.int32)),
        in_specs=[VSPEC],
        out_specs=(VSPEC,) * 3,
        compiler_params=params(4),
        cost_estimate=cost(1e9, 1e6),
    )(lengths)


def pack_small(ids, *arrays):
    return pl.pallas_call(
        small_kernel,
        out_shape=shape((LABEL_AT + 16, LANES)),
        in_specs=[SSPEC] + [VSPEC] * len(arrays),
        out_specs=VSPEC,
        compiler_params=params(56),
        cost_estimate=cost(1e9, 1e6),
    )(ids, *arrays)


def one_hot(starts, ends, base):
    row = lax.broadcasted_iota(jnp.int32, (ROWS, 2 * BAGS), 0).astype(F32).astype(BF)
    low = jnp.clip(starts - base, 0, ROWS).astype(F32).astype(BF)
    high = jnp.clip(ends - base, 0, ROWS).astype(F32).astype(BF)
    return jnp.where((row >= low) & (row < high), jnp.ones((), BF), jnp.zeros((), BF))


def window(ref, block):
    first = ref[pl.ds(block, 1), :]
    second = ref[pl.ds(block + 1, 1), :]
    return jnp.concatenate([first, second], axis=1)


def pool_kernel(skip, count, half_blocks, chunks, ids_ref, meta_ref, st_ref, en_ref, ent_ref, *refs):
    x_ref, acc_ref = refs[-2:]
    base_block = ids_ref[0] * half_blocks + skip

    def clear(i, carry):
        at = pl.multiple_of((base_block + i) * BAGS, BAGS)
        acc_ref[:, pl.ds(at, BAGS)] = jnp.zeros((EMB, BAGS), F32)
        return carry

    lax.fori_loop(0, count, clear, 0, unroll=True)

    low_chunk = meta_ref[0, base_block] // ROWS
    high_chunk = (meta_ref[0, base_block + count] + ROWS - 1) // ROWS
    step = 9

    def chunk(i, carry):
        for u in range(step):
            c = low_chunk + i * step + u
            inside = jnp.minimum(c, chunks - 1)
            block = meta_ref[1, inside]
            at = pl.multiple_of(inside * ROWS, ROWS)
            picked = one_hot(window(st_ref, block), window(en_ref, block), c * ROWS)
            part = nn(ent_ref[:, pl.ds(at, ROWS)], picked)
            to = pl.multiple_of(block * BAGS, BAGS)
            acc_ref[:, pl.ds(to, 2 * BAGS)] += part
        return carry

    lax.fori_loop(0, (high_chunk - low_chunk + step - 1) // step, chunk, 0)

    def place(i, carry):
        at = pl.multiple_of((base_block + i) * BAGS, BAGS)
        to = pl.multiple_of(i * EVB, EVB)
        block = acc_ref[:, pl.ds(at, BAGS)].T
        for pair in range(FEATS // 2):
            left = block[2 * pair * EVB : (2 * pair + 1) * EVB]
            right = block[(2 * pair + 1) * EVB : (2 * pair + 2) * EVB]
            x_ref[pl.ds(to, EVB), pair * 2 * EMB : (pair + 1) * 2 * EMB] = jnp.concatenate(
                [left, right], axis=1
            ).astype(BF)
        return carry

    lax.fori_loop(0, count, place, 0, unroll=12)


def pool(part, parts, ids, meta, starts, ends, entries, *after):
    blocks = starts.shape[0] - 8
    half_blocks = blocks // 2
    count = half_blocks // parts
    chunks = entries.shape[1] // ROWS
    return pl.pallas_call(
        functools.partial(pool_kernel, part * count, count, half_blocks, chunks),
        out_shape=shape((count * EVB, D)),
        in_specs=[SSPEC, SSPEC, VSPEC, VSPEC, VSPEC] + [ASPEC] * len(after),
        out_specs=VSPEC,
        scratch_shapes=[pltpu.VMEM((EMB, (blocks + 1) * BAGS), F32)],
        compiler_params=params(16),
        cost_estimate=cost(10e9, 5e6),
    )(ids, meta, starts, ends, entries, *after)


def expand_kernel(half_blocks, group, ids_ref, meta_ref, st_ref, en_ref, own_ref, other_ref, out_ref, pred_ref, token_ref, rows_ref):
    position = ids_ref[0]
    step = pl.program_id(0)
    events = half_blocks * EVB

    @pl.when(step == 0)
    def _():
        for source, half in ((own_ref, position), (other_ref, 1 - position)):

            def place(i, carry):
                at = pl.multiple_of(i * EVB, EVB)
                to = pl.multiple_of((half * half_blocks + i) * BAGS, BAGS)
                for pair in range(FEATS // 2):
                    tile = source[pl.ds(at, EVB), pair * 2 * EMB : (pair + 1) * 2 * EMB]
                    rows_ref[pl.ds(to + 2 * pair * EVB, EVB), :] = tile[:, :EMB]
                    rows_ref[pl.ds(to + (2 * pair + 1) * EVB, EVB), :] = tile[:, EMB:]
                return carry

            lax.fori_loop(0, half_blocks, place, 0, unroll=48)
        rows_ref[pl.ds(2 * half_blocks * BAGS, BAGS), :] = jnp.zeros((BAGS, EMB), BF)
        own = own_ref[events : events + 16, : 2 * LANES].astype(F32)
        other = other_ref[events : events + 16, : 2 * LANES].astype(F32)
        mine = (own[:, :LANES] + own[:, LANES:])[:8]
        theirs = (other[:, :LANES] + other[:, LANES:])[8:]
        halves = (jnp.where(position == 0, mine, theirs), jnp.where(position == 0, theirs, mine))
        tiles = events // LANES
        token_ref[...] = mine
        pred_ref[...] = jnp.concatenate([half[k : k + 1] for half in halves for k in range(tiles)], axis=1)

    for u in range(group):
        c = step * group + u
        block = meta_ref[1, c]
        picked = one_hot(window(st_ref, block), window(en_ref, block), c * ROWS)
        at = pl.multiple_of(block * BAGS, BAGS)
        out_ref[:, u * ROWS : (u + 1) * ROWS] = nn(picked, rows_ref[pl.ds(at, 2 * BAGS), :]).astype(BF).T


def expand(ids, meta, starts, ends, own, other, rows):
    blocks = starts.shape[0] - 8
    chunks = rows // ROWS
    group = 72
    while chunks % group:
        group -= 1
    return pl.pallas_call(
        functools.partial(expand_kernel, blocks // 2, group),
        grid=(chunks // group,),
        out_shape=(shape((EMB, rows)), shape((1, blocks * EVB), F32), shape((8, LANES), F32)),
        in_specs=[SSPEC, SSPEC, VSPEC, VSPEC, VSPEC, VSPEC],
        out_specs=(
            pl.BlockSpec((EMB, group * ROWS), lambda i: (0, i)),
            pl.BlockSpec((1, blocks * EVB), lambda i: (0, 0)),
            pl.BlockSpec((8, LANES), lambda i: (0, 0)),
        ),
        scratch_shapes=[pltpu.VMEM(((blocks + 1) * BAGS, EMB), BF)],
        compiler_params=params(24, dimension_semantics=("arbitrary",)),
        cost_estimate=cost(12e9, 6e6),
    )(ids, meta, starts, ends, own, other)


def gelu_twice(v):
    cube = K1 * (v * v)
    bend = jnp.tanh(v * (cube + K0))
    rise = 1.0 + bend
    act = v * rise
    slope = rise + act * (1.0 - bend) * (3.0 * cube + K0)
    return act, slope


def gelu_both(v):
    act, slope = gelu_twice(v)
    return 0.5 * act, 0.5 * slope


def wide(block, row):
    return jnp.concatenate([block[row : row + 1, :], block[row + 1 : row + 2, :]], axis=1)


def by_eight(value):
    return jnp.sum(value.reshape(-1, 8, value.shape[-1]), axis=0)


def plus(total, term):
    return term if total is None else total + term


def pieces_of(m):
    return [slice(at, at + PIECE) for at in range(m * HID, (m + 1) * HID, PIECE)]


def col_sum(value):
    return jnp.sum(value, axis=0, keepdims=True)


def lane_tiles(events, body):
    def step(j, carry):
        body(j, pl.ds(pl.multiple_of(j * LANES, LANES), LANES))
        return carry

    lax.fori_loop(0, events // LANES, step, 0)


def part(m):
    return slice(m * HID, (m + 1) * HID)


def pick(own, other, rows):
    if rows.start < HALF:
        return own.at[rows]
    return other.at[slice(rows.start - HALF, rows.stop - HALF)]


def spans_of(events):
    span = next(size for size in (SPAN, 2 * LANES, LANES) if events % size == 0)
    return [slice(at, at + span) for at in range(0, events, span)]


def rows_of(ids_ref, t, piece, rows1, rows2):
    if piece is None:
        return pl.ds(0, rows1), pl.ds(0, rows2)
    where = ids_ref[0] if t == 0 else 1 - ids_ref[0]
    d = ids_ref[1] ^ (4 * piece[2])
    if piece[1]:
        d = d ^ (2 - where)
    if piece[0]:
        d = d ^ (1 + where)
    return (
        pl.ds(pl.multiple_of(d * rows1, rows1), rows1),
        pl.ds(pl.multiple_of(d * rows2, rows2), rows2),
    )


def assemble(ids_ref, t, groups, given, rows1, rows2, w1_ref, w2_ref):
    for group, pieces in zip(groups, given):
        for g, piece in enumerate(pieces):
            one, two = rows_of(ids_ref, t, piece, rows1, rows2)
            for s in range(SLOTS):
                w1_ref[one, part(s)] = group[g, s * rows1 : (s + 1) * rows1, :]
                low = SLOTS * rows1 + s * rows2
                w2_ref[s, two, :] = (0.5 * group[g, low : low + rows2, :].astype(F32)).astype(BF)


def put(ids_ref, t, s, outs, plan, rows1, rows2, held_ref, first, value):
    held_ref[...] = value
    for out, (small_first, pieces) in zip(outs, plan):
        for g, piece in enumerate(pieces):
            mine = rows_of(ids_ref, t, piece, rows1, rows2)[0 if first else 1]
            at = g * SLOTS * (rows1 + rows2) + (SMALL_ROWS if small_first else 0)
            at, size = (at + s * rows1, rows1) if first else (at + SLOTS * rows1 + s * rows2, rows2)
            value = held_ref[mine, :]
            out[at : at + size, :] = (value if first else 0.5 * value).astype(BF)


def first_layer(s, w1_ref, x_ref, pc_ref):
    pc_ref[part(s), :] = tn(w1_ref[:, part(s)], x_ref[...])


def first_gelu(s, pc_ref, h_ref):
    for here in spans_of(pc_ref.shape[1]):
        for rows in pieces_of(s):
            act, slope = gelu_twice(pc_ref[rows, here])
            pc_ref[rows, here] = slope
            h_ref[rows, here] = act.astype(BF)


def front_kernel(xs, given, rows1, rows2, ids_ref, *refs):
    refs = list(refs)
    take = lambda n: [refs.pop(0) for _ in range(n)]
    x_parts, groups = take(xs), take(len(given))
    x_ref, w1_ref, w2_ref, pc_ref, h_ref = refs
    size = x_ref.shape[1] // xs
    for k, piece in enumerate(x_parts):
        x_ref[:, k * size : (k + 1) * size] = piece[...].T
    assemble(ids_ref, 0, groups, given, rows1, rows2, w1_ref, w2_ref)
    first_layer(0, w1_ref, x_ref, pc_ref)
    for s in range(SLOTS):
        if s + 1 < SLOTS:
            first_layer(s + 1, w1_ref, x_ref, pc_ref)
        first_gelu(s, pc_ref, h_ref)


def front(ids, x_parts, groups, given, rows1, rows2):
    events = sum(part.shape[0] for part in x_parts)
    outs = (
        shape((D, events)),
        shape((D, HALF)),
        shape((SLOTS, HID, HID)),
        shape((HALF, events), F32),
        shape((HALF, events)),
    )
    return pl.pallas_call(
        functools.partial(front_kernel, len(x_parts), given, rows1, rows2),
        out_shape=outs,
        in_specs=[SSPEC] + [VSPEC] * (len(x_parts) + len(groups)),
        out_specs=(VSPEC,) * len(outs),
        compiler_params=params(16),
        cost_estimate=cost(6e9, 4e6),
    )(ids, *x_parts, *groups)


def back_kernel(plan, rows1, rows2, ids_ref, x_ref, h_ref, e_ref, f_ref, small_ref, *refs):
    outs, (g1_ref, g2_ref) = refs[:-2], refs[-2:]
    for s in range(SLOTS):
        g2 = nt(h_ref[part(s), :], e_ref[part(s), :])
        put(ids_ref, 0, s, outs, plan, rows1, rows2, g2_ref.at[s % 2], False, g2)
        g1 = nt(x_ref[...], f_ref[part(s), :])
        put(ids_ref, 0, s, outs, plan, rows1, rows2, g1_ref.at[s % 2], True, g1)
    for out, (small_first, _) in zip(outs, plan):
        if small_first:
            out[:SMALL_ROWS, :] = small_ref[...]


def grad_shapes(plan, rows1, rows2):
    rows = SLOTS * (rows1 + rows2)
    return tuple(shape((len(pieces) * rows + small * SMALL_ROWS, HID)) for small, pieces in plan)


def back(ids, x, h, e, f, small, plan, rows1, rows2):
    outs = grad_shapes(plan, rows1, rows2)
    return pl.pallas_call(
        functools.partial(back_kernel, plan, rows1, rows2),
        out_shape=outs,
        in_specs=[SSPEC] + [VSPEC] * 5,
        out_specs=(VSPEC,) * len(outs),
        scratch_shapes=[pltpu.VMEM((2, D, HID), F32), pltpu.VMEM((2, HID, HID), F32)],
        compiler_params=params(16),
        cost_estimate=cost(6e9, 4e6),
    )(ids, x, h, e, f, small)


def main_kernel(given, plan, rows1, rows2, ids_ref, *refs):
    refs = list(refs)
    take = lambda n: [refs.pop(0) for _ in range(n)]
    x_ref, w1own_ref, w2own_ref, pcown_ref, hown_ref = take(5)
    oth_groups = take(len(given))
    packs = take(2)
    dx_ref, eown_ref, fown_ref, small_ref = take(4)
    oth_outs = take(len(plan))
    wc_ref, w2_ref, gain_ref, third_ref, lab_ref, pc_ref, pb_ref, s2_ref, y_ref, h_ref, e_ref, fc_ref = take(12)
    scale_ref, lg_ref, prob_ref, q_ref, pt_ref, u1_ref, p4_ref, e2_ref, e1_ref, du_ref, dm_ref, dmb_ref = take(12)
    ds_ref, dn_ref, acc3_ref, pred_ref, g1_ref, g2_ref, dp_ref = take(7)
    position = ids_ref[0]
    events = x_ref.shape[1]

    def second_weights(m):
        return w2own_ref[m] if m < SLOTS else w2_ref[m - SLOTS]

    assemble(ids_ref, 1, oth_groups, given, rows1, rows2, wc_ref, w2_ref)
    lines = []
    for t in range(2):
        block = packs[t][GATE_AT : GATE_AT + 16, :].astype(F32)
        for g in range(GATES):
            lines.append(
                jnp.concatenate([block[4 * g + p : 4 * g + p + 1, :] for p in range(D // LANES)], axis=1)
            )
        lines.append(jnp.zeros((8 - GATES, D), F32))
    gates = jnp.concatenate(lines, axis=0).astype(BF)
    wc_ref[:, HALF:] = jnp.concatenate([gates, jnp.zeros((LANES - 16, D), BF)], axis=0).T
    fc_ref[HALF:, :] = jnp.zeros((LANES, events), BF)
    acc3_ref[...] = jnp.zeros_like(acc3_ref)
    miscs = [packs[t][MISC_AT : MISC_AT + 16, :].astype(F32) for t in range(2)]
    for t in range(2):
        misc = miscs[t]
        for s in range(SLOTS):
            for kind in range(2):
                for half in range(2):
                    at = 2 * (kind * SLOTS + s) + half
                    to = ((kind * 2 + t) * SLOTS + s) * HID + half * LANES
                    gain_ref[to : to + LANES, :] = jnp.broadcast_to(misc[at : at + 1, :], (LANES, LANES)).T
        third = jnp.broadcast_to(misc[12:13, :], (LANES, LANES)).T
        third_ref[t * TOWER2 : (t + 1) * TOWER2, :] = third[:TOWER2]
        lab_ref[t * 16 : (t + 1) * 16, :] = packs[t][LABEL_AT : LABEL_AT + 16, :].astype(F32)

    lg_ref[...] = nn(gates, x_ref[...])
    spans = spans_of(events)

    def second_gelu(m, here):
        total = None
        for rows in pieces_of(m):
            act, slope = gelu_twice(pb_ref[rows, here])
            pb_ref[rows, here] = act
            s2_ref[rows, here] = slope
            total = plus(total, by_eight(act))
        mean = col_sum(total) * (1.0 / HID)
        total = None
        for rows in pieces_of(m):
            centred = pb_ref[rows, here] - mean
            pb_ref[rows, here] = centred
            total = plus(total, by_eight(centred * centred))
        scale = lax.rsqrt(col_sum(total) * (1.0 / HID) + 4.0 * EPSILON)
        scale_ref[m : m + 1, here] = scale
        for rows in pieces_of(m):
            normed = pb_ref[rows, here] * scale
            pb_ref[rows, here] = normed
            for lanes in range(here.start, here.stop, LANES):
                block = slice(lanes, lanes + LANES)
                out = pb_ref[rows, block] * gain_ref[rows, :] + gain_ref[slice(WIDE + rows.start, WIDE + rows.stop), :]
                if m % SLOTS == SLOTS - 1:
                    out = out.astype(BF).astype(F32)
                y_ref[rows, block] = out

    turn = [m for s in range(SLOTS) for m in (s, SLOTS + s)]
    first_layer(0, wc_ref, x_ref, pc_ref)
    for i, m in enumerate(turn):
        s = m - SLOTS
        if s >= 0:
            if s + 1 < SLOTS:
                first_layer(s + 1, wc_ref, x_ref, pc_ref)
            first_gelu(s, pc_ref, h_ref)
        pb_ref[part(m), :] = tn(second_weights(m), pick(hown_ref, h_ref, part(m))[...])
        if i:
            for here in spans:
                second_gelu(turn[i - 1], here)
    for here in spans:
        second_gelu(turn[-1], here)
    orders = [(t * SLOTS, t * SLOTS + 1, t * SLOTS + 2, (1 - t) * SLOTS + 2) for t in range(2)]

    prob_ref[...] = jnp.ones_like(prob_ref)

    def mix(j, here):
        for t in range(2):
            logits = [lg_ref[8 * t + k : 8 * t + k + 1, here] for k in range(GATES)]
            top = jnp.maximum(jnp.maximum(logits[0], logits[1]), jnp.maximum(logits[2], logits[3]))
            raised = [jnp.exp(logit - top) for logit in logits]
            scale = 1.0 / (raised[0] + raised[1] + raised[2] + raised[3])
            mixture = None
            for k in range(GATES):
                prob = raised[k] * scale
                prob_ref[8 * t + k : 8 * t + k + 1, here] = prob
                term = prob * y_ref[part(orders[t][k]), here]
                mixture = term if mixture is None else mixture + term
            q_ref[part(t), here] = mixture.astype(BF)

    lane_tiles(events, mix)
    for t in range(2):
        pt_ref[t * TOWER1 : (t + 1) * TOWER1, :] = tn(packs[t][T1_AT : T1_AT + HID, :], q_ref[part(t), :])

    def tower_gelu(j, here):
        act, slope = gelu_both(pt_ref[:, here])
        pt_ref[:, here] = slope
        u1_ref[:, here] = act.astype(BF)

    lane_tiles(events, tower_gelu)
    for t in range(2):
        p4_ref[t * TOWER2 : (t + 1) * TOWER2, :] = nn(
            packs[t][T2_AT : T2_AT + TOWER2, :], u1_ref[t * TOWER1 : (t + 1) * TOWER1, :]
        )

    def head(j, here):
        act, slope = gelu_both(p4_ref[:, here])
        u2 = act.astype(BF).astype(F32)
        product = u2 * third_ref[...]
        deltas = []
        for t in range(2):
            logit = col_sum(product[t * TOWER2 : (t + 1) * TOWER2])
            prediction = 1.0 / (1.0 + jnp.exp(-logit))
            pred_ref[pl.ds(8 * t + j, 1), :] = prediction
            label = lab_ref[pl.ds(t * 16 + position * (events // LANES) + j, 1), :]
            deltas.append(jnp.broadcast_to(prediction - label, (TOWER2, LANES)))
        delta = jnp.concatenate(deltas, axis=0)
        acc3_ref[...] += delta * u2
        e2_ref[:, here] = (slope * (delta * third_ref[...])).astype(BF)

    lane_tiles(events, head)
    for t in range(2):
        du_ref[t * TOWER1 : (t + 1) * TOWER1, :] = tn(
            packs[t][T2_AT : T2_AT + TOWER2, :], e2_ref[t * TOWER2 : (t + 1) * TOWER2, :]
        )

    def tower_back(j, here):
        e1_ref[:, here] = (pt_ref[:, here] * du_ref[:, here]).astype(BF)

    lane_tiles(events, tower_back)
    for t in range(2):
        mixed = nn(packs[t][T1_AT : T1_AT + HID, :], e1_ref[t * TOWER1 : (t + 1) * TOWER1, :])
        dm_ref[part(t), :] = mixed
        dmb_ref[part(t), :] = mixed.astype(BF)
        rows = [wide(miscs[t], 2 * (SLOTS + s)) for s in range(EXPERTS)] + [jnp.zeros((8 - EXPERTS, HID), F32)]
        ds_ref[8 * t : 8 * t + 8, :] = nn(jnp.concatenate(rows, axis=0).astype(BF), dmb_ref[part(t), :])

    def probs_of(t, k, here):
        return prob_ref[8 * t + k : 8 * t + k + 1, here]

    def shared_probs(here):
        for t in range(2):
            for k in range(EXPERTS, GATES):
                total = None
                for mine, rows in zip(pieces_of(t), pieces_of(orders[t][k])):
                    total = plus(total, by_eight(dm_ref[mine, here] * y_ref[rows, here]))
                dp_ref[8 * t + k : 8 * t + k + 1, here] = col_sum(total)

    def norm_back(m, here):
        t, s = divmod(m, SLOTS)
        one, two = None, None
        for rows in pieces_of(m):
            mine = slice(rows.start - m * HID + t * HID, rows.stop - m * HID + t * HID)
            for lanes in range(here.start, here.stop, LANES):
                block = slice(lanes, lanes + LANES)
                up = dm_ref[mine, block]
                if s == SLOTS - 1:
                    theirs = slice(mine.start + (1 - 2 * t) * HID, mine.stop + (1 - 2 * t) * HID)
                    up = probs_of(t, s, block) * up + probs_of(1 - t, SLOTS, block) * dm_ref[theirs, block]
                y_ref[rows, block] = up * gain_ref[rows, :]
            d_normed = y_ref[rows, here]
            product = d_normed * pb_ref[rows, here]
            dn_ref[rows, here] = product.astype(BF)
            one = plus(one, by_eight(d_normed))
            two = plus(two, by_eight(product))
        one, two = col_sum(one), col_sum(two)
        outer = scale_ref[m : m + 1, here]
        if s < EXPERTS:
            outer = outer * probs_of(t, s, here)
            dp_ref[8 * t + s : 8 * t + s + 1, here] = two + ds_ref[8 * t + s : 8 * t + s + 1, here]
        one, two = one * (1.0 / HID), two * (1.0 / HID)
        for rows in pieces_of(m):
            inner = y_ref[rows, here] - one - pb_ref[rows, here] * two
            pick(eown_ref, e_ref, rows)[:, here] = (s2_ref[rows, here] * outer * inner).astype(BF)

    for here in spans:
        shared_probs(here)
    turn = [m for s in range(SLOTS) for m in (SLOTS + s, s)]
    for here in spans:
        norm_back(turn[0], here)
    for i, m in enumerate(turn):
        y_ref[part(m), :] = nn(second_weights(m), pick(eown_ref, e_ref, part(m))[...])
        s = m - SLOTS
        if s >= 0:
            g2 = nt(h_ref[part(s), :], e_ref[part(s), :])
            put(ids_ref, 1, s, oth_outs, plan, rows1, rows2, g2_ref.at[s % 2], False, g2)
        if i + 1 < BIG:
            for here in spans:
                norm_back(turn[i + 1], here)
        for here in spans:
            for rows in pieces_of(m):
                value = pick(pcown_ref, pc_ref, rows)[:, here] * y_ref[rows, here]
                pick(fown_ref, fc_ref, rows)[:, here] = value.astype(BF)
        if s >= 0:
            g1 = nt(x_ref[...], fc_ref[part(s), :])
            put(ids_ref, 1, s, oth_outs, plan, rows1, rows2, g1_ref.at[s % 2], True, g1)
    codes = []
    for t in range(2):
        probs = [probs_of(t, k, slice(None)) for k in range(GATES)]
        d_probs = [dp_ref[8 * t + k : 8 * t + k + 1, :] for k in range(GATES)]
        weighted = probs[0] * d_probs[0]
        for k in range(1, GATES):
            weighted = weighted + probs[k] * d_probs[k]
        codes += [probs[k] * (d_probs[k] - weighted) for k in range(GATES)]
        codes.append(jnp.zeros((8 - GATES, events), F32))
    fc_ref[HALF : HALF + 16, :] = jnp.concatenate(codes, axis=0).astype(BF)
    dx = nn(w1own_ref[...], fown_ref[...]) + nn(wc_ref[...], fc_ref[...])
    dx_ref[:events, :] = dx.astype(BF).T
    pred = pred_ref[...]
    high = pred.astype(BF)
    low = (pred - high.astype(F32)).astype(BF)
    dx_ref[events:, :] = jnp.concatenate([high, low, high, low], axis=1)

    gate_grad = nt(fc_ref[HALF : HALF + 16, :], x_ref[...])
    weights = prob_ref[...].astype(BF)
    shifts = [nt(weights, dmb_ref[part(t), :]) for t in range(2)]
    third_grad = col_sum(acc3_ref[...].T)
    for t in range(2):
        tower = slice(t * TOWER1, (t + 1) * TOWER1)
        half = slice(t * TOWER2, (t + 1) * TOWER2)
        lines = []
        for g in range(GATES):
            row = gate_grad[8 * t + g : 8 * t + g + 1, :]
            lines += [row[:, p * LANES : (p + 1) * LANES] for p in range(D // LANES)]
        for s in range(SLOTS):
            at = 8 * t + (s if s < EXPERTS else GATES)
            row = nt(weights, dn_ref[part(t * SLOTS + s), :])[at : at + 1, :] / wide(miscs[t], 2 * s)
            lines += [row[:, :LANES], row[:, LANES:]]
        for s in range(SLOTS):
            row = shifts[t][8 * t + s : 8 * t + s + 1, :]
            if s == SLOTS - 1:
                row = row + shifts[1 - t][8 * (1 - t) + SLOTS : 8 * (1 - t) + SLOTS + 1, :]
            lines += [row[:, :LANES], row[:, LANES:]]
        lines.append(third_grad if t == 0 else pltpu.roll(third_grad, TOWER2, 1))
        lines.append(jnp.zeros((3, LANES), F32))
        small = jnp.concatenate(
            [
                nt(q_ref[part(t), :], e1_ref[tower, :]),
                nt(e2_ref[half, :], u1_ref[tower, :]),
                jnp.concatenate(lines, axis=0),
            ],
            axis=0,
        )
        small = jnp.concatenate([small[:SMALL_ROWS], small[SMALL_ROWS:]], axis=1).astype(BF)
        if t == 0:
            small_ref[...] = small
            continue
        for out, (small_first, _) in zip(oth_outs, plan):
            if small_first:
                out[:SMALL_ROWS, :] = small


def layer(ids, started, oth_groups, own_pack, oth_pack, given, plan, rows1, rows2):
    events = started[0].shape[1]
    half = shape((HALF, events))
    results = (shape((events + 16, D)), half, half, shape((SMALL_ROWS, HID))) + grad_shapes(plan, rows1, rows2)
    scratch = [
        ((D, HALF + LANES), BF),
        ((SLOTS, HID, HID), BF),
        ((2 * WIDE, LANES), F32),
        ((2 * TOWER2, LANES), F32),
        ((32, LANES), F32),
        ((HALF, events), F32),
        ((WIDE, events), F32),
        ((WIDE, events), F32),
        ((WIDE, events), F32),
        ((HALF, events), BF),
        ((HALF, events), BF),
        ((HALF + LANES, events), BF),
        ((8, events), F32),
        ((16, events), F32),
        ((16, events), F32),
        ((2 * HID, events), BF),
        ((2 * TOWER1, events), F32),
        ((2 * TOWER1, events), BF),
        ((2 * TOWER2, events), F32),
        ((2 * TOWER2, events), BF),
        ((2 * TOWER1, events), BF),
        ((2 * TOWER1, events), F32),
        ((2 * HID, events), F32),
        ((2 * HID, events), BF),
        ((16, events), F32),
        ((WIDE, events), BF),
        ((2 * TOWER2, LANES), F32),
        ((16, LANES), F32),
        ((2, D, HID), F32),
        ((2, HID, HID), F32),
        ((16, events), F32),
    ]
    arrays = [*started, *oth_groups, own_pack, oth_pack]
    return pl.pallas_call(
        functools.partial(main_kernel, given, plan, rows1, rows2),
        out_shape=results,
        in_specs=[SSPEC] + [VSPEC] * len(arrays),
        out_specs=(VSPEC,) * len(results),
        scratch_shapes=[pltpu.VMEM(dims, kind) for dims, kind in scratch],
        compiler_params=params(42),
        cost_estimate=cost(events * BIG * 196608 * 6, 10e6),
    )(ids, *arrays)


def sibling(value):
    return lax.ppermute(value, "task", [(0, 1), (1, 0)])


def flipped(value, mask):
    pairs = [(i, i ^ mask) for i in range(lax.axis_size("dp"))]
    return lax.ppermute(value, "dp", pairs)


def crossed(value, masks):
    n = lax.axis_size("dp")
    pairs = [(t * n + i, t * n + (i ^ masks[t])) for t in range(2) for i in range(n)]
    return lax.ppermute(value, ("task", "dp"), pairs)


def stack_kernel(count, *refs):
    out, sems = refs[-2:]
    copies = [pltpu.make_async_copy(refs[k], out.at[k], sems.at[k]) for k in range(count)]
    for copy in copies:
        copy.start()
    for copy in copies:
        copy.wait()


def stacked(pieces):
    return pl.pallas_call(
        functools.partial(stack_kernel, len(pieces)),
        out_shape=shape((len(pieces),) + pieces[0].shape, pieces[0].dtype),
        in_specs=[ASPEC] * len(pieces),
        out_specs=VSPEC,
        scratch_shapes=[pltpu.SemaphoreType.DMA((len(pieces),))],
        compiler_params=params(4),
        cost_estimate=cost(0, 1e6),
    )(*pieces)


def summed(*terms):
    total = terms[0].astype(F32)
    for term in terms[1:]:
        total = total + term.astype(F32)
    return total.astype(BF)


def small_sum_kernel(one_ref, two_ref, *refs):
    out_ref = refs[-1]
    out_ref[...] = (one_ref[...].astype(F32) + two_ref[...].astype(F32)).astype(BF)


def small_sum(one, two, *after):
    lead = pl.BlockSpec((SMALL_ROWS, HID), lambda i: (0, 0))
    return pl.pallas_call(
        small_sum_kernel,
        grid=(1,),
        out_shape=shape((SMALL_ROWS, HID)),
        in_specs=[lead, lead] + [ASPEC] * len(after),
        out_specs=lead,
        compiler_params=params(4),
        cost_estimate=cost(8e9, 1e6),
    )(one, two, *after)


def tie_kernel(*refs):
    pass


def tied(value, after):
    return pl.pallas_call(
        tie_kernel,
        out_shape=shape(value.shape, value.dtype),
        in_specs=[ASPEC, ASPEC],
        out_specs=ASPEC,
        input_output_aliases={0: 0},
        compiler_params=params(1),
        cost_estimate=cost(0, 1),
    )(value, after)


def far_kernel(rows, keep_ref, got_ref, mid_ref, near_ref, *outs):
    for k, out in enumerate(outs):
        here = slice(k * rows, (k + 1) * rows)
        total = keep_ref[here, :].astype(F32) + got_ref[here, :].astype(F32)
        at = SMALL_ROWS + k * rows
        total = total + mid_ref[at : at + rows, :].astype(F32)
        out[...] = (total + near_ref[here, :].astype(F32)).astype(BF)


def block(rows, at=0):
    return pl.BlockSpec((rows, HID), lambda i: (at, 0))


def far_messages(far, rows, keep, got, mid, near):
    size = far * rows
    return pl.pallas_call(
        functools.partial(far_kernel, rows),
        grid=(1,),
        out_shape=(shape((rows, HID)),) * far,
        in_specs=[block(size), block(size), block(size + SMALL_ROWS), block(size)],
        out_specs=(block(rows),) * far,
        compiler_params=params(12),
        cost_estimate=cost(0, 4e6),
    )(keep, got, mid, near)


def home_kernel(rows, keep_ref, got_ref, mid_ref, *refs):
    smalls, (message_ref, base_ref) = refs[:-2], refs[-2:]
    total = keep_ref[...].astype(F32) + got_ref[...].astype(F32) + mid_ref[...].astype(F32)
    base_ref[...] = total[:rows]
    message_ref[SMALL_ROWS:, :] = total[rows:].astype(BF)
    small = smalls[0][...].astype(F32)
    for term in smalls[1:]:
        small = small + term[...].astype(F32)
    message_ref[:SMALL_ROWS, :] = small.astype(BF)


def home_message(far, rows, keep, got, mid, smalls):
    at = block(2 * rows, far)
    return pl.pallas_call(
        functools.partial(home_kernel, rows),
        grid=(1,),
        out_shape=(shape((SMALL_ROWS + rows, HID)), shape((rows, HID), F32)),
        in_specs=[at, at, block(2 * rows)] + [block(SMALL_ROWS)] * len(smalls),
        out_specs=(block(SMALL_ROWS + rows), block(rows)),
        compiler_params=params(8),
        cost_estimate=cost(0, 2e6),
    )(keep, got, mid, *smalls)


def total_kernel(*refs):
    total = refs[0][...].astype(F32)
    for term in refs[1:-1]:
        total = total + term[...].astype(F32)
    refs[-1][...] = total


def totalled(*terms):
    return pl.pallas_call(
        total_kernel,
        out_shape=shape(terms[0].shape, F32),
        in_specs=[VSPEC] * len(terms),
        out_specs=VSPEC,
        compiler_params=params(4),
        cost_estimate=cost(10e9, 1e6),
    )(*terms)


def last_kernel(rows1, rows2, paired, ids_ref, *refs):
    if paired:
        part_ref, sent_ref, near_ref = refs[:3]
        total = part_ref[...] + near_ref[SMALL_ROWS:, :].astype(F32)
        small = sent_ref[:SMALL_ROWS, :].astype(F32) + near_ref[:SMALL_ROWS, :].astype(F32)
    else:
        total, small = refs[0][...], refs[1][...]
    w1_ref, w2_ref, o1_ref, o2_ref, sg_ref, ss_ref, og_ref, os_ref, gate_ref, t1_ref, t2_ref, t3_ref = refs[-12:]
    cut = SLOTS * rows1
    for s in range(EXPERTS):
        w1_ref[s] = total[s * rows1 : (s + 1) * rows1]
        w2_ref[s] = total[cut + s * rows2 : cut + (s + 1) * rows2]
    o1_ref[...] = total[EXPERTS * rows1 : cut]
    o2_ref[...] = total[cut + EXPERTS * rows2 :]
    tiny = jnp.concatenate([small[:, :LANES], small[:, LANES:]], axis=0)
    t1_ref[...] = tiny[T1_AT : T1_AT + HID]
    t2_ref[...] = tiny[T2_AT : T2_AT + TOWER2]
    gates = []
    for g in range(GATES):
        at = GATE_AT + 4 * g
        gates.append(jnp.concatenate([tiny[at + p : at + p + 1] for p in range(D // LANES)], axis=1))
    turned = ids_ref[0] != 0
    gate_ref[0:1, :] = gates[0]
    gate_ref[1:2, :] = gates[1]
    gate_ref[2:3, :] = jnp.where(turned, gates[3], gates[2])
    gate_ref[3:4, :] = jnp.where(turned, gates[2], gates[3])
    for kind, (spec, own) in enumerate(((sg_ref, og_ref), (ss_ref, os_ref))):
        for s in range(SLOTS):
            at = MISC_AT + 2 * (kind * SLOTS + s)
            row = jnp.concatenate([tiny[at : at + 1], tiny[at + 1 : at + 2]], axis=1)
            if s < EXPERTS:
                spec[s : s + 1, :] = row
            else:
                own[...] = row
    t3_ref[...] = tiny[MISC_AT + 12 : MISC_AT + 13, :TOWER2]


def finish(ids, terms, rows1, rows2):
    outs = (
        shape((EXPERTS, rows1, HID), F32),
        shape((EXPERTS, rows2, HID), F32),
        shape((rows1, HID), F32),
        shape((rows2, HID), F32),
        shape((EXPERTS, HID), F32),
        shape((EXPERTS, HID), F32),
        shape((1, HID), F32),
        shape((1, HID), F32),
        shape((GATES, D), F32),
        shape((HID, TOWER1), F32),
        shape((TOWER2, TOWER1), F32),
        shape((1, TOWER2), F32),
    )
    return pl.pallas_call(
        functools.partial(last_kernel, rows1, rows2, len(terms) == 3),
        out_shape=outs,
        in_specs=[SSPEC] + [VSPEC] * len(terms),
        out_specs=(VSPEC,) * len(outs),
        compiler_params=params(8),
        cost_estimate=cost(0, 2e6),
    )(ids, *terms)


def per_device(
    entries,
    lengths,
    labels,
    spec_w1,
    spec_w2,
    spec_gain,
    spec_shift,
    shared_w1,
    shared_w2,
    shared_gain,
    shared_shift,
    gate_w,
    tower_w1,
    tower_w2,
    tower_w3,
):
    position = lax.axis_index("task")
    n = lax.axis_size("dp")
    ids = jnp.stack([position, lax.axis_index("dp")]).astype(jnp.int32)
    rows1, rows2 = spec_w1.shape[2], spec_w2.shape[2]
    direct = rows2 % 16 == 0 and n % 4 == 0 and n & (n - 1) == 0
    pack = jnp.concatenate(
        [part.reshape(-1, HID) for part in (spec_w1, shared_w1, spec_w2, shared_w2)], axis=0
    )
    if direct:
        quarter = n // 4
        far = [pack] + [flipped(pack, 4 * k) for k in range(1, quarter)]

    rows = entries.shape[0]
    starts, ends, meta = bags(lengths, rows // ROWS)
    small = pack_small(
        ids,
        labels,
        spec_gain[0],
        spec_shift[0],
        shared_gain,
        shared_shift,
        gate_w[0].T,
        tower_w1[0],
        tower_w2[0].T,
        tower_w3,
    )
    other_small = sibling(small)
    turned = entries.T
    x_first = pool(0, 2, ids, meta, starts, ends, turned)

    if direct:
        zc = stacked(far)
        r1 = tied(crossed(zc, (1, 2)), x_first)
        r2 = crossed(tied(zc, x_first), (2, 1))
        x_second = pool(1, 2, ids, meta, starts, ends, turned, other_small)
        r3 = tied(crossed(r1, (2, 1)), x_second)
        own = [zc, r2, r1, r3]
        given = tuple(tuple((one, two, k) for k in range(quarter)) for one, two in ((0, 0), (0, 1), (1, 0), (1, 1)))
        far_ones = [(two, k) for two in range(2) for k in range(1, quarter)]
        home_ones = [(0, 0), (1, 0)]
        send = [(1, *piece) for piece in far_ones]
        keep = [(0, *piece) for piece in far_ones + home_ones] + [(1, *piece) for piece in home_ones]
        plan, used1, used2 = ((0, tuple(keep)), (1, tuple(send))), rows1, rows2
    else:
        x_second = pool(1, 2, ids, meta, starts, ends, turned)
        every = lax.all_gather(pack, "dp", axis=0)
        cut = SLOTS * rows1
        w1 = every[:, :cut].reshape(n, SLOTS, rows1, HID).swapaxes(0, 1).reshape(-1, HID)
        w2 = every[:, cut:].reshape(n, SLOTS, rows2, HID).swapaxes(0, 1).reshape(-1, HID)
        own = [jnp.concatenate([w1, w2], axis=0)[None]]
        given, plan, used1, used2 = ((None,),), ((1, (None,)),), D, HID
    other = [sibling(group) for group in own]
    started = front(ids, [x_first, x_second], own, given, used1, used2)
    dx, e, f, own_small, *oth_grads = layer(ids, started, other, small, other_small, given, plan, used1, used2)
    got = [sibling(grad) for grad in oth_grads[::-1]][::-1]
    own_grads = back(ids, started[0], started[4], e, f, own_small, plan, used1, used2)
    other_dx = sibling(dx)
    turned, predictions, expanded = expand(ids, meta, starts, ends, dx, other_dx, rows)
    piece = SLOTS * (rows1 + rows2)
    if direct:
        keep, send = own_grads
        far, cut = quarter - 1, (quarter - 1) * piece
        send = summed(send, got[1])
        mid = tied(crossed(send, (1, 2)), expanded)
        home = slice(2 * cut + 2 * piece, 2 * cut + 4 * piece)
        home = summed(keep[home], got[0][home])
        late = slice(cut, 2 * cut)
        near = crossed(summed(keep[late], got[0][late], mid[SMALL_ROWS + cut :]), (2, 1))
        small = small_sum(send, mid)
        home_mid = tied(crossed(home, (1, 2)), expanded)
        mask = n // 2
        while mask > 4:
            small = summed(small, flipped(small, mask))
            mask //= 2
        smalls = [flipped(small, mask)]
        parts = far_messages(far, piece, keep, got[0], mid, near)
        smalls = [small] + [tied(term, parts[0]) for term in smalls]
        message, base = home_message(far, piece, keep, got[0], home_mid, smalls)
        parts = [flipped(part, 4 * (k + 1)) for k, part in enumerate(parts)]
        grads = finish(ids, [totalled(base, *parts), message, crossed(message, (2, 1))], rows1, rows2)
    else:
        whole = own_grads[0].astype(F32) + got[0].astype(F32)
        small = lax.psum(whole[:SMALL_ROWS], "dp")
        whole = whole[SMALL_ROWS:]
        cut = SLOTS * D
        g1 = lax.psum_scatter(whole[:cut].reshape(SLOTS, D, HID), "dp", scatter_dimension=1, tiled=True)
        g2 = lax.psum_scatter(whole[cut:].reshape(SLOTS, HID, HID), "dp", scatter_dimension=1, tiled=True)
        part = jnp.concatenate([g1.reshape(-1, HID), g2.reshape(-1, HID)], axis=0)
        grads = finish(ids, [part, small], rows1, rows2)
    w1, w2, o1, o2, sg, ss, og, os, gate, t1, t2, t3 = grads
    entry_grads = turned.T
    return (
        predictions,
        entry_grads,
        w1[None],
        w2[None],
        sg[None],
        ss[None],
        o1[None],
        o2[None],
        og,
        os,
        gate.T[None],
        t1[None],
        t2.T[None],
        t3,
    )


def solution(mesh):
    placed = (
        P("dp", None),
        P("dp", None),
        P("task", "dp"),
        P("task", None, "dp", None),
        P("task", None, "dp", None),
        P("task", None, None),
        P("task", None, None),
        P("task", "dp", None),
        P("task", "dp", None),
        P("task", None),
        P("task", None),
        P("task", None, None),
        P("task", None, None),
        P("task", None, None),
        P("task", None),
    )
    return jax.shard_map(
        per_device,
        mesh=mesh,
        in_specs=placed,
        out_specs=(
            P("task", "dp"),
            P("dp", None),
            P("task", None, "dp", None),
            P("task", None, "dp", None),
            P("task", None, None),
            P("task", None, None),
            P("task", "dp", None),
            P("task", "dp", None),
            P("task", None),
            P("task", None),
            P("task", None, None),
            P("task", None, None),
            P("task", None, None),
            P("task", None),
        ),
        check_vma=False,
    )
```

```python
import functools

import jax
import jax.numpy as jnp
from jax import lax
from jax.experimental import pallas as pl
from jax.experimental.pallas import tpu as pltpu
from jax.sharding import PartitionSpec as P

EXPERTS = 2
GATES = 4
D = 512
HID = 256
TOWER1 = 128
TOWER2 = 64
EMB = 64
FEATS = 8
LANES = 128
BAGS = 128
EVB = BAGS // FEATS
ROWS = 128
EPSILON = 1e-05
K0 = 0.7978845608028654
K1 = K0 * 0.044715
SLOTS = 3
BIG = 2 * SLOTS
WIDE = BIG * HID
HALF = SLOTS * HID
PIECE = 32
SPAN = 256
BF = jnp.bfloat16
F32 = jnp.float32

T1_AT = 0
T2_AT = T1_AT + HID
GATE_AT = T2_AT + TOWER2
MISC_AT = GATE_AT + GATES * (D // LANES)
LABEL_AT = MISC_AT + 16
G_ROWS = LABEL_AT
SMALL_ROWS = G_ROWS // 2


def nn(left, right):
    return jnp.dot(left, right, preferred_element_type=F32)


def nt(left, right):
    return lax.dot_general(left, right, (((1,), (1,)), ((), ())), preferred_element_type=F32)


def tn(left, right):
    return lax.dot_general(left, right, (((0,), (0,)), ((), ())), preferred_element_type=F32)


def params(mib, **kwargs):
    return pltpu.CompilerParams(vmem_limit_bytes=mib * 1024 * 1024, **kwargs)


def cost(flops, moved):
    return pl.CostEstimate(flops=int(flops), bytes_accessed=int(moved), transcendentals=0)


def shape(dims, kind=BF):
    return jax.ShapeDtypeStruct(dims, kind)


VSPEC = pl.BlockSpec(memory_space=pltpu.VMEM)
SSPEC = pl.BlockSpec(memory_space=pltpu.SMEM)
ASPEC = pl.BlockSpec(memory_space=pl.ANY)


def line(ref, row):
    both = ref[row : row + 1, :].astype(F32)
    return [both[:, :LANES], both[:, LANES:]]


def bags_kernel(blocks, chunks, len_ref, st_ref, en_ref, meta_ref):
    k = lax.broadcasted_iota(jnp.int32, (BAGS, BAGS), 0)
    j = lax.broadcasted_iota(jnp.int32, (BAGS, BAGS), 1)
    natural = (j % EVB) * FEATS + j // EVB
    before = jnp.where(k < natural, 1.0, 0.0).astype(BF)
    same = jnp.where(k == natural, 1.0, 0.0).astype(BF)
    lens_f = jnp.concatenate(
        [len_ref[:, b * BAGS : (b + 1) * BAGS] for b in range(blocks)], axis=0
    ).astype(F32)
    lens = lens_f.astype(BF)
    in_block = nn(lens, before)
    own = nn(lens, same)
    sums = jnp.sum(lens_f, axis=1, keepdims=True)
    high = jnp.floor(sums * (1.0 / 128.0))
    low = sums - high * 128.0
    bi = lax.broadcasted_iota(jnp.int32, (blocks, blocks), 0)
    bj = lax.broadcasted_iota(jnp.int32, (blocks, blocks), 1)
    lower = jnp.where(bj < bi, 1.0, 0.0).astype(BF)
    offset = 128.0 * nn(lower, jnp.broadcast_to(high, (blocks, BAGS)).astype(BF)) + nn(
        lower, jnp.broadcast_to(low, (blocks, BAGS)).astype(BF)
    )
    starts = offset + in_block
    st_ref[pl.ds(0, blocks), :] = starts.astype(jnp.int32)
    en_ref[pl.ds(0, blocks), :] = (starts + own).astype(jnp.int32)
    past = jnp.full((8, BAGS), chunks * ROWS, jnp.int32)
    st_ref[pl.ds(blocks, 8), :] = past
    en_ref[pl.ds(blocks, 8), :] = past
    lanes = meta_ref.shape[1]
    begins = jnp.concatenate([offset] * (lanes // BAGS), axis=1)
    row = lax.broadcasted_iota(jnp.int32, (blocks, lanes), 0)
    col = lax.broadcasted_iota(jnp.int32, (blocks, lanes), 1)
    begin = jnp.sum(jnp.where(row == col, begins, 0.0), axis=0, keepdims=True)
    spot = lax.broadcasted_iota(jnp.int32, (1, lanes), 1)
    begin = jnp.where(spot >= blocks, float(chunks * ROWS), begin)
    reached = jnp.where(begins <= (col * ROWS).astype(F32), 1.0, 0.0)
    first = jnp.sum(reached, axis=0, keepdims=True) - 1.0
    meta_ref[0:1, :] = begin.astype(jnp.int32)
    meta_ref[1:2, :] = first.astype(jnp.int32)


def small_kernel(
    ids_ref,
    label_ref,
    sgain_ref,
    sshift_ref,
    ogain_ref,
    oshift_ref,
    gate_ref,
    t1_ref,
    t2_ref,
    t3_ref,
    small_ref,
):
    small_ref[T1_AT : T1_AT + HID, :] = t1_ref[...]
    small_ref[T2_AT : T2_AT + TOWER2, :] = t2_ref[...]
    gate = gate_ref[...].astype(F32)
    turned = jnp.concatenate([gate[0:2], gate[3:4], gate[2:3]], axis=0)
    gate = jnp.where(ids_ref[0] == 0, gate, turned)
    lines = [gate[g : g + 1, p * LANES : (p + 1) * LANES] for g in range(GATES) for p in range(D // LANES)]
    lines += line(sgain_ref, 0) + line(sgain_ref, 1) + line(ogain_ref, 0)
    lines += line(sshift_ref, 0) + line(sshift_ref, 1) + line(oshift_ref, 0)
    lines += [jnp.concatenate([t3_ref[...].astype(F32)] * 2, axis=1), jnp.zeros((3, LANES), F32)]
    events = label_ref.shape[1]
    lines += [label_ref[:, p * LANES : (p + 1) * LANES].astype(F32) for p in range(events // LANES)]
    lines += [jnp.zeros((16 - events // LANES, LANES), F32)]
    small_ref[pl.ds(GATE_AT, 48), :] = jnp.concatenate(lines, axis=0).astype(BF)


def bags(lengths, chunks):
    blocks = lengths.shape[1] // BAGS
    lanes = -(-max(blocks + 1, chunks) // LANES) * LANES
    bounds = shape((blocks + 8, BAGS), jnp.int32)
    return pl.pallas_call(
        functools.partial(bags_kernel, blocks, chunks),
        out_shape=(bounds, bounds, shape((2, lanes), jnp.int32)),
        in_specs=[VSPEC],
        out_specs=(VSPEC,) * 3,
        compiler_params=params(4),
        cost_estimate=cost(1e9, 1e6),
    )(lengths)


def pack_small(ids, *arrays):
    return pl.pallas_call(
        small_kernel,
        out_shape=shape((LABEL_AT + 16, LANES)),
        in_specs=[SSPEC] + [VSPEC] * len(arrays),
        out_specs=VSPEC,
        compiler_params=params(56),
        cost_estimate=cost(1e9, 1e6),
    )(ids, *arrays)


def one_hot(starts, ends, base):
    row = lax.broadcasted_iota(jnp.int32, (ROWS, 2 * BAGS), 0).astype(F32).astype(BF)
    low = jnp.clip(starts - base, 0, ROWS).astype(F32).astype(BF)
    high = jnp.clip(ends - base, 0, ROWS).astype(F32).astype(BF)
    return jnp.where((row >= low) & (row < high), jnp.ones((), BF), jnp.zeros((), BF))


def window(ref, block):
    first = ref[pl.ds(block, 1), :]
    second = ref[pl.ds(block + 1, 1), :]
    return jnp.concatenate([first, second], axis=1)


def pool_kernel(skip, count, half_blocks, chunks, ids_ref, meta_ref, st_ref, en_ref, ent_ref, *refs):
    x_ref, acc_ref = refs[-2:]
    base_block = ids_ref[0] * half_blocks + skip

    def clear(i, carry):
        at = pl.multiple_of((base_block + i) * BAGS, BAGS)
        acc_ref[:, pl.ds(at, BAGS)] = jnp.zeros((EMB, BAGS), F32)
        return carry

    lax.fori_loop(0, count, clear, 0, unroll=True)

    low_chunk = meta_ref[0, base_block] // ROWS
    high_chunk = (meta_ref[0, base_block + count] + ROWS - 1) // ROWS
    step = 9

    def chunk(i, carry):
        for u in range(step):
            c = low_chunk + i * step + u
            inside = jnp.minimum(c, chunks - 1)
            block = meta_ref[1, inside]
            at = pl.multiple_of(inside * ROWS, ROWS)
            picked = one_hot(window(st_ref, block), window(en_ref, block), c * ROWS)
            part = nn(ent_ref[:, pl.ds(at, ROWS)], picked)
            to = pl.multiple_of(block * BAGS, BAGS)
            acc_ref[:, pl.ds(to, 2 * BAGS)] += part
        return carry

    lax.fori_loop(0, (high_chunk - low_chunk + step - 1) // step, chunk, 0)

    def place(i, carry):
        at = pl.multiple_of((base_block + i) * BAGS, BAGS)
        to = pl.multiple_of(i * EVB, EVB)
        block = acc_ref[:, pl.ds(at, BAGS)].T
        for pair in range(FEATS // 2):
            left = block[2 * pair * EVB : (2 * pair + 1) * EVB]
            right = block[(2 * pair + 1) * EVB : (2 * pair + 2) * EVB]
            x_ref[pl.ds(to, EVB), pair * 2 * EMB : (pair + 1) * 2 * EMB] = jnp.concatenate(
                [left, right], axis=1
            ).astype(BF)
        return carry

    lax.fori_loop(0, count, place, 0, unroll=12)


def pool(part, parts, ids, meta, starts, ends, entries, *after):
    blocks = starts.shape[0] - 8
    half_blocks = blocks // 2
    count = half_blocks // parts
    chunks = entries.shape[1] // ROWS
    return pl.pallas_call(
        functools.partial(pool_kernel, part * count, count, half_blocks, chunks),
        out_shape=shape((count * EVB, D)),
        in_specs=[SSPEC, SSPEC, VSPEC, VSPEC, VSPEC] + [ASPEC] * len(after),
        out_specs=VSPEC,
        scratch_shapes=[pltpu.VMEM((EMB, (blocks + 1) * BAGS), F32)],
        compiler_params=params(16),
        cost_estimate=cost(10e9, 5e6),
    )(ids, meta, starts, ends, entries, *after)


def expand_kernel(half_blocks, group, ids_ref, meta_ref, st_ref, en_ref, own_ref, other_ref, out_ref, pred_ref, token_ref, rows_ref):
    position = ids_ref[0]
    step = pl.program_id(0)
    events = half_blocks * EVB

    @pl.when(step == 0)
    def _():
        for source, half in ((own_ref, position), (other_ref, 1 - position)):

            def place(i, carry):
                at = pl.multiple_of(i * EVB, EVB)
                to = pl.multiple_of((half * half_blocks + i) * BAGS, BAGS)
                for pair in range(FEATS // 2):
                    tile = source[pl.ds(at, EVB), pair * 2 * EMB : (pair + 1) * 2 * EMB]
                    rows_ref[pl.ds(to + 2 * pair * EVB, EVB), :] = tile[:, :EMB]
                    rows_ref[pl.ds(to + (2 * pair + 1) * EVB, EVB), :] = tile[:, EMB:]
                return carry

            lax.fori_loop(0, half_blocks, place, 0, unroll=48)
        rows_ref[pl.ds(2 * half_blocks * BAGS, BAGS), :] = jnp.zeros((BAGS, EMB), BF)
        own = own_ref[events : events + 16, : 2 * LANES].astype(F32)
        other = other_ref[events : events + 16, : 2 * LANES].astype(F32)
        mine = (own[:, :LANES] + own[:, LANES:])[:8]
        theirs = (other[:, :LANES] + other[:, LANES:])[8:]
        halves = (jnp.where(position == 0, mine, theirs), jnp.where(position == 0, theirs, mine))
        tiles = events // LANES
        token_ref[...] = mine
        pred_ref[...] = jnp.concatenate([half[k : k + 1] for half in halves for k in range(tiles)], axis=1)

    for u in range(group):
        c = step * group + u
        block = meta_ref[1, c]
        picked = one_hot(window(st_ref, block), window(en_ref, block), c * ROWS)
        at = pl.multiple_of(block * BAGS, BAGS)
        out_ref[:, u * ROWS : (u + 1) * ROWS] = nn(picked, rows_ref[pl.ds(at, 2 * BAGS), :]).astype(BF).T


def expand(ids, meta, starts, ends, own, other, rows):
    blocks = starts.shape[0] - 8
    chunks = rows // ROWS
    group = 72
    while chunks % group:
        group -= 1
    return pl.pallas_call(
        functools.partial(expand_kernel, blocks // 2, group),
        grid=(chunks // group,),
        out_shape=(shape((EMB, rows)), shape((1, blocks * EVB), F32), shape((8, LANES), F32)),
        in_specs=[SSPEC, SSPEC, VSPEC, VSPEC, VSPEC, VSPEC],
        out_specs=(
            pl.BlockSpec((EMB, group * ROWS), lambda i: (0, i)),
            pl.BlockSpec((1, blocks * EVB), lambda i: (0, 0)),
            pl.BlockSpec((8, LANES), lambda i: (0, 0)),
        ),
        scratch_shapes=[pltpu.VMEM(((blocks + 1) * BAGS, EMB), BF)],
        compiler_params=params(24, dimension_semantics=("arbitrary",)),
        cost_estimate=cost(12e9, 6e6),
    )(ids, meta, starts, ends, own, other)


def gelu_twice(v):
    cube = K1 * (v * v)
    bend = jnp.tanh(v * (cube + K0))
    rise = 1.0 + bend
    act = v * rise
    slope = rise + act * (1.0 - bend) * (3.0 * cube + K0)
    return act, slope


def gelu_both(v):
    act, slope = gelu_twice(v)
    return 0.5 * act, 0.5 * slope


def wide(block, row):
    return jnp.concatenate([block[row : row + 1, :], block[row + 1 : row + 2, :]], axis=1)


def by_eight(value):
    return jnp.sum(value.reshape(-1, 8, value.shape[-1]), axis=0)


def plus(total, term):
    return term if total is None else total + term


def pieces_of(m):
    return [slice(at, at + PIECE) for at in range(m * HID, (m + 1) * HID, PIECE)]


def col_sum(value):
    return jnp.sum(value, axis=0, keepdims=True)


def lane_tiles(events, body):
    def step(j, carry):
        body(j, pl.ds(pl.multiple_of(j * LANES, LANES), LANES))
        return carry

    lax.fori_loop(0, events // LANES, step, 0)


def part(m):
    return slice(m * HID, (m + 1) * HID)


def pick(own, other, rows):
    if rows.start < HALF:
        return own.at[rows]
    return other.at[slice(rows.start - HALF, rows.stop - HALF)]


def spans_of(events):
    span = next(size for size in (SPAN, 2 * LANES, LANES) if events % size == 0)
    return [slice(at, at + span) for at in range(0, events, span)]


def rows_of(ids_ref, t, piece, rows1, rows2):
    if piece is None:
        return pl.ds(0, rows1), pl.ds(0, rows2)
    where = ids_ref[0] if t == 0 else 1 - ids_ref[0]
    d = ids_ref[1] ^ (4 * piece[2])
    if piece[1]:
        d = d ^ (2 - where)
    if piece[0]:
        d = d ^ (1 + where)
    return (
        pl.ds(pl.multiple_of(d * rows1, rows1), rows1),
        pl.ds(pl.multiple_of(d * rows2, rows2), rows2),
    )


def assemble(ids_ref, t, groups, given, rows1, rows2, w1_ref, w2_ref):
    for group, pieces in zip(groups, given):
        for g, piece in enumerate(pieces):
            one, two = rows_of(ids_ref, t, piece, rows1, rows2)
            for s in range(SLOTS):
                w1_ref[one, part(s)] = group[g, s * rows1 : (s + 1) * rows1, :]
                low = SLOTS * rows1 + s * rows2
                w2_ref[s, two, :] = (0.5 * group[g, low : low + rows2, :].astype(F32)).astype(BF)


def put(ids_ref, t, s, outs, plan, rows1, rows2, held_ref, first, value):
    held_ref[...] = (value if first else 0.5 * value).astype(BF)
    for out, (small_first, pieces) in zip(outs, plan):
        for g, piece in enumerate(pieces):
            mine = rows_of(ids_ref, t, piece, rows1, rows2)[0 if first else 1]
            at = g * SLOTS * (rows1 + rows2) + (SMALL_ROWS if small_first else 0)
            at, size = (at + s * rows1, rows1) if first else (at + SLOTS * rows1 + s * rows2, rows2)
            out[at : at + size, :] = held_ref[mine, :]


def first_layer(s, w1_ref, x_ref, pc_ref):
    pc_ref[part(s), :] = tn(w1_ref[:, part(s)], x_ref[...])


def first_gelu(s, pc_ref, h_ref):
    for here in spans_of(pc_ref.shape[1]):
        for rows in pieces_of(s):
            act, slope = gelu_twice(pc_ref[rows, here])
            pc_ref[rows, here] = slope
            h_ref[rows, here] = act.astype(BF)


def front_kernel(xs, given, rows1, rows2, ids_ref, *refs):
    refs = list(refs)
    take = lambda n: [refs.pop(0) for _ in range(n)]
    x_parts, groups = take(xs), take(len(given))
    x_ref, w1_ref, w2_ref, pc_ref, h_ref = refs
    size = x_ref.shape[1] // xs
    for k, piece in enumerate(x_parts):
        x_ref[:, k * size : (k + 1) * size] = piece[...].T
    assemble(ids_ref, 0, groups, given, rows1, rows2, w1_ref, w2_ref)
    first_layer(0, w1_ref, x_ref, pc_ref)
    for s in range(SLOTS):
        if s + 1 < SLOTS:
            first_layer(s + 1, w1_ref, x_ref, pc_ref)
        first_gelu(s, pc_ref, h_ref)


def front(ids, x_parts, groups, given, rows1, rows2):
    events = sum(part.shape[0] for part in x_parts)
    outs = (
        shape((D, events)),
        shape((D, HALF)),
        shape((SLOTS, HID, HID)),
        shape((HALF, events), F32),
        shape((HALF, events)),
    )
    return pl.pallas_call(
        functools.partial(front_kernel, len(x_parts), given, rows1, rows2),
        out_shape=outs,
        in_specs=[SSPEC] + [VSPEC] * (len(x_parts) + len(groups)),
        out_specs=(VSPEC,) * len(outs),
        compiler_params=params(16),
        cost_estimate=cost(6e9, 4e6),
    )(ids, *x_parts, *groups)


def back_kernel(plan, rows1, rows2, ids_ref, x_ref, h_ref, e_ref, f_ref, small_ref, *refs):
    outs, (g1_ref, g2_ref) = refs[:-2], refs[-2:]
    for s in range(SLOTS):
        g2 = nt(h_ref[part(s), :], e_ref[part(s), :])
        put(ids_ref, 0, s, outs, plan, rows1, rows2, g2_ref.at[s % 2], False, g2)
        g1 = nt(x_ref[...], f_ref[part(s), :])
        put(ids_ref, 0, s, outs, plan, rows1, rows2, g1_ref.at[s % 2], True, g1)
    for out, (small_first, _) in zip(outs, plan):
        if small_first:
            out[:SMALL_ROWS, :] = small_ref[...]


def grad_shapes(plan, rows1, rows2):
    rows = SLOTS * (rows1 + rows2)
    return tuple(shape((len(pieces) * rows + small * SMALL_ROWS, HID)) for small, pieces in plan)


def back(ids, x, h, e, f, small, plan, rows1, rows2):
    outs = grad_shapes(plan, rows1, rows2)
    return pl.pallas_call(
        functools.partial(back_kernel, plan, rows1, rows2),
        out_shape=outs,
        in_specs=[SSPEC] + [VSPEC] * 5,
        out_specs=(VSPEC,) * len(outs),
        scratch_shapes=[pltpu.VMEM((2, D, HID), BF), pltpu.VMEM((2, HID, HID), BF)],
        compiler_params=params(16),
        cost_estimate=cost(6e9, 4e6),
    )(ids, x, h, e, f, small)


def main_kernel(given, plan, rows1, rows2, ids_ref, *refs):
    refs = list(refs)
    take = lambda n: [refs.pop(0) for _ in range(n)]
    x_ref, w1own_ref, w2own_ref, pcown_ref, hown_ref = take(5)
    oth_groups = take(len(given))
    packs = take(2)
    dx_ref, eown_ref, fown_ref, small_ref = take(4)
    oth_outs = take(len(plan))
    wc_ref, w2_ref, gain_ref, third_ref, lab_ref, pc_ref, pb_ref, s2_ref, y_ref, h_ref, e_ref, fc_ref = take(12)
    scale_ref, lg_ref, prob_ref, q_ref, pt_ref, u1_ref, p4_ref, e2_ref, e1_ref, du_ref, dm_ref, dmb_ref = take(12)
    ds_ref, dn_ref, acc3_ref, pred_ref, g1_ref, g2_ref, dp_ref = take(7)
    position = ids_ref[0]
    events = x_ref.shape[1]

    def second_weights(m):
        return w2own_ref[m] if m < SLOTS else w2_ref[m - SLOTS]

    assemble(ids_ref, 1, oth_groups, given, rows1, rows2, wc_ref, w2_ref)
    lines = []
    for t in range(2):
        block = packs[t][GATE_AT : GATE_AT + 16, :].astype(F32)
        for g in range(GATES):
            lines.append(
                jnp.concatenate([block[4 * g + p : 4 * g + p + 1, :] for p in range(D // LANES)], axis=1)
            )
        lines.append(jnp.zeros((8 - GATES, D), F32))
    gates = jnp.concatenate(lines, axis=0).astype(BF)
    wc_ref[:, HALF:] = jnp.concatenate([gates, jnp.zeros((LANES - 16, D), BF)], axis=0).T
    fc_ref[HALF:, :] = jnp.zeros((LANES, events), BF)
    acc3_ref[...] = jnp.zeros_like(acc3_ref)
    miscs = [packs[t][MISC_AT : MISC_AT + 16, :].astype(F32) for t in range(2)]
    for t in range(2):
        misc = miscs[t]
        for s in range(SLOTS):
            for kind in range(2):
                for half in range(2):
                    at = 2 * (kind * SLOTS + s) + half
                    to = ((kind * 2 + t) * SLOTS + s) * HID + half * LANES
                    gain_ref[to : to + LANES, :] = jnp.broadcast_to(misc[at : at + 1, :], (LANES, LANES)).T
        third = jnp.broadcast_to(misc[12:13, :], (LANES, LANES)).T
        third_ref[t * TOWER2 : (t + 1) * TOWER2, :] = third[:TOWER2]
        lab_ref[t * 16 : (t + 1) * 16, :] = packs[t][LABEL_AT : LABEL_AT + 16, :].astype(F32)

    lg_ref[...] = nn(gates, x_ref[...])
    spans = spans_of(events)

    def second_gelu(m, here):
        total = None
        for rows in pieces_of(m):
            act, slope = gelu_twice(pb_ref[rows, here])
            pb_ref[rows, here] = act
            s2_ref[rows, here] = slope
            total = plus(total, by_eight(act))
        mean = col_sum(total) * (1.0 / HID)
        total = None
        for rows in pieces_of(m):
            centred = pb_ref[rows, here] - mean
            pb_ref[rows, here] = centred
            total = plus(total, by_eight(centred * centred))
        scale = lax.rsqrt(col_sum(total) * (1.0 / HID) + 4.0 * EPSILON)
        scale_ref[m : m + 1, here] = scale
        for rows in pieces_of(m):
            normed = pb_ref[rows, here] * scale
            pb_ref[rows, here] = normed
            for lanes in range(here.start, here.stop, LANES):
                block = slice(lanes, lanes + LANES)
                out = pb_ref[rows, block] * gain_ref[rows, :] + gain_ref[slice(WIDE + rows.start, WIDE + rows.stop), :]
                if m % SLOTS == SLOTS - 1:
                    out = out.astype(BF).astype(F32)
                y_ref[rows, block] = out

    turn = [m for s in range(SLOTS) for m in (s, SLOTS + s)]
    first_layer(0, wc_ref, x_ref, pc_ref)
    for i, m in enumerate(turn):
        s = m - SLOTS
        if s >= 0:
            if s + 1 < SLOTS:
                first_layer(s + 1, wc_ref, x_ref, pc_ref)
            first_gelu(s, pc_ref, h_ref)
        pb_ref[part(m), :] = tn(second_weights(m), pick(hown_ref, h_ref, part(m))[...])
        if i:
            for here in spans:
                second_gelu(turn[i - 1], here)
    for here in spans:
        second_gelu(turn[-1], here)
    orders = [(t * SLOTS, t * SLOTS + 1, t * SLOTS + 2, (1 - t) * SLOTS + 2) for t in range(2)]

    prob_ref[...] = jnp.ones_like(prob_ref)

    def mix(j, here):
        for t in range(2):
            logits = [lg_ref[8 * t + k : 8 * t + k + 1, here] for k in range(GATES)]
            top = jnp.maximum(jnp.maximum(logits[0], logits[1]), jnp.maximum(logits[2], logits[3]))
            raised = [jnp.exp(logit - top) for logit in logits]
            scale = 1.0 / (raised[0] + raised[1] + raised[2] + raised[3])
            mixture = None
            for k in range(GATES):
                prob = raised[k] * scale
                prob_ref[8 * t + k : 8 * t + k + 1, here] = prob
                term = prob * y_ref[part(orders[t][k]), here]
                mixture = term if mixture is None else mixture + term
            q_ref[part(t), here] = mixture.astype(BF)

    lane_tiles(events, mix)
    for t in range(2):
        pt_ref[t * TOWER1 : (t + 1) * TOWER1, :] = tn(packs[t][T1_AT : T1_AT + HID, :], q_ref[part(t), :])

    def tower_gelu(j, here):
        act, slope = gelu_both(pt_ref[:, here])
        pt_ref[:, here] = slope
        u1_ref[:, here] = act.astype(BF)

    lane_tiles(events, tower_gelu)
    for t in range(2):
        p4_ref[t * TOWER2 : (t + 1) * TOWER2, :] = nn(
            packs[t][T2_AT : T2_AT + TOWER2, :], u1_ref[t * TOWER1 : (t + 1) * TOWER1, :]
        )

    def head(j, here):
        act, slope = gelu_both(p4_ref[:, here])
        u2 = act.astype(BF).astype(F32)
        product = u2 * third_ref[...]
        deltas = []
        for t in range(2):
            logit = col_sum(product[t * TOWER2 : (t + 1) * TOWER2])
            prediction = 1.0 / (1.0 + jnp.exp(-logit))
            pred_ref[pl.ds(8 * t + j, 1), :] = prediction
            label = lab_ref[pl.ds(t * 16 + position * (events // LANES) + j, 1), :]
            deltas.append(jnp.broadcast_to(prediction - label, (TOWER2, LANES)))
        delta = jnp.concatenate(deltas, axis=0)
        acc3_ref[...] += delta * u2
        e2_ref[:, here] = (slope * (delta * third_ref[...])).astype(BF)

    lane_tiles(events, head)
    for t in range(2):
        du_ref[t * TOWER1 : (t + 1) * TOWER1, :] = tn(
            packs[t][T2_AT : T2_AT + TOWER2, :], e2_ref[t * TOWER2 : (t + 1) * TOWER2, :]
        )

    def tower_back(j, here):
        e1_ref[:, here] = (pt_ref[:, here] * du_ref[:, here]).astype(BF)

    lane_tiles(events, tower_back)
    for t in range(2):
        mixed = nn(packs[t][T1_AT : T1_AT + HID, :], e1_ref[t * TOWER1 : (t + 1) * TOWER1, :])
        dm_ref[part(t), :] = mixed
        dmb_ref[part(t), :] = mixed.astype(BF)
        rows = [wide(miscs[t], 2 * (SLOTS + s)) for s in range(EXPERTS)] + [jnp.zeros((8 - EXPERTS, HID), F32)]
        ds_ref[8 * t : 8 * t + 8, :] = nn(jnp.concatenate(rows, axis=0).astype(BF), dmb_ref[part(t), :])

    def probs_of(t, k, here):
        return prob_ref[8 * t + k : 8 * t + k + 1, here]

    def shared_probs(here):
        for t in range(2):
            for k in range(EXPERTS, GATES):
                total = None
                for mine, rows in zip(pieces_of(t), pieces_of(orders[t][k])):
                    total = plus(total, by_eight(dm_ref[mine, here] * y_ref[rows, here]))
                dp_ref[8 * t + k : 8 * t + k + 1, here] = col_sum(total)

    def norm_back(m, here):
        t, s = divmod(m, SLOTS)
        one, two = None, None
        for rows in pieces_of(m):
            mine = slice(rows.start - m * HID + t * HID, rows.stop - m * HID + t * HID)
            for lanes in range(here.start, here.stop, LANES):
                block = slice(lanes, lanes + LANES)
                up = dm_ref[mine, block]
                if s == SLOTS - 1:
                    theirs = slice(mine.start + (1 - 2 * t) * HID, mine.stop + (1 - 2 * t) * HID)
                    up = probs_of(t, s, block) * up + probs_of(1 - t, SLOTS, block) * dm_ref[theirs, block]
                y_ref[rows, block] = up * gain_ref[rows, :]
            d_normed = y_ref[rows, here]
            product = d_normed * pb_ref[rows, here]
            dn_ref[rows, here] = product.astype(BF)
            one = plus(one, by_eight(d_normed))
            two = plus(two, by_eight(product))
        one, two = col_sum(one), col_sum(two)
        outer = scale_ref[m : m + 1, here]
        if s < EXPERTS:
            outer = outer * probs_of(t, s, here)
            dp_ref[8 * t + s : 8 * t + s + 1, here] = two + ds_ref[8 * t + s : 8 * t + s + 1, here]
        one, two = one * (1.0 / HID), two * (1.0 / HID)
        for rows in pieces_of(m):
            inner = y_ref[rows, here] - one - pb_ref[rows, here] * two
            pick(eown_ref, e_ref, rows)[:, here] = (s2_ref[rows, here] * outer * inner).astype(BF)

    for here in spans:
        shared_probs(here)
    turn = [m for s in range(SLOTS) for m in (SLOTS + s, s)]
    for here in spans:
        norm_back(turn[0], here)
    for i, m in enumerate(turn):
        y_ref[part(m), :] = nn(second_weights(m), pick(eown_ref, e_ref, part(m))[...])
        s = m - SLOTS
        if s >= 0:
            g2 = nt(h_ref[part(s), :], e_ref[part(s), :])
            put(ids_ref, 1, s, oth_outs, plan, rows1, rows2, g2_ref.at[s % 2], False, g2)
        if i + 1 < BIG:
            for here in spans:
                norm_back(turn[i + 1], here)
        for here in spans:
            for rows in pieces_of(m):
                value = pick(pcown_ref, pc_ref, rows)[:, here] * y_ref[rows, here]
                pick(fown_ref, fc_ref, rows)[:, here] = value.astype(BF)
        if s >= 0:
            g1 = nt(x_ref[...], fc_ref[part(s), :])
            put(ids_ref, 1, s, oth_outs, plan, rows1, rows2, g1_ref.at[s % 2], True, g1)
    codes = []
    for t in range(2):
        probs = [probs_of(t, k, slice(None)) for k in range(GATES)]
        d_probs = [dp_ref[8 * t + k : 8 * t + k + 1, :] for k in range(GATES)]
        weighted = probs[0] * d_probs[0]
        for k in range(1, GATES):
            weighted = weighted + probs[k] * d_probs[k]
        codes += [probs[k] * (d_probs[k] - weighted) for k in range(GATES)]
        codes.append(jnp.zeros((8 - GATES, events), F32))
    fc_ref[HALF : HALF + 16, :] = jnp.concatenate(codes, axis=0).astype(BF)
    dx = nn(w1own_ref[...], fown_ref[...]) + nn(wc_ref[...], fc_ref[...])
    dx_ref[:events, :] = dx.astype(BF).T
    pred = pred_ref[...]
    high = pred.astype(BF)
    low = (pred - high.astype(F32)).astype(BF)
    dx_ref[events:, :] = jnp.concatenate([high, low, high, low], axis=1)

    gate_grad = nt(fc_ref[HALF : HALF + 16, :], x_ref[...])
    weights = prob_ref[...].astype(BF)
    shifts = [nt(weights, dmb_ref[part(t), :]) for t in range(2)]
    third_grad = col_sum(acc3_ref[...].T)
    for t in range(2):
        tower = slice(t * TOWER1, (t + 1) * TOWER1)
        half = slice(t * TOWER2, (t + 1) * TOWER2)
        lines = []
        for g in range(GATES):
            row = gate_grad[8 * t + g : 8 * t + g + 1, :]
            lines += [row[:, p * LANES : (p + 1) * LANES] for p in range(D // LANES)]
        for s in range(SLOTS):
            at = 8 * t + (s if s < EXPERTS else GATES)
            row = nt(weights, dn_ref[part(t * SLOTS + s), :])[at : at + 1, :] / wide(miscs[t], 2 * s)
            lines += [row[:, :LANES], row[:, LANES:]]
        for s in range(SLOTS):
            row = shifts[t][8 * t + s : 8 * t + s + 1, :]
            if s == SLOTS - 1:
                row = row + shifts[1 - t][8 * (1 - t) + SLOTS : 8 * (1 - t) + SLOTS + 1, :]
            lines += [row[:, :LANES], row[:, LANES:]]
        lines.append(third_grad if t == 0 else pltpu.roll(third_grad, TOWER2, 1))
        lines.append(jnp.zeros((3, LANES), F32))
        small = jnp.concatenate(
            [
                nt(q_ref[part(t), :], e1_ref[tower, :]),
                nt(e2_ref[half, :], u1_ref[tower, :]),
                jnp.concatenate(lines, axis=0),
            ],
            axis=0,
        )
        small = jnp.concatenate([small[:SMALL_ROWS], small[SMALL_ROWS:]], axis=1).astype(BF)
        if t == 0:
            small_ref[...] = small
            continue
        for out, (small_first, _) in zip(oth_outs, plan):
            if small_first:
                out[:SMALL_ROWS, :] = small


def layer(ids, started, oth_groups, own_pack, oth_pack, given, plan, rows1, rows2):
    events = started[0].shape[1]
    half = shape((HALF, events))
    results = (shape((events + 16, D)), half, half, shape((SMALL_ROWS, HID))) + grad_shapes(plan, rows1, rows2)
    scratch = [
        ((D, HALF + LANES), BF),
        ((SLOTS, HID, HID), BF),
        ((2 * WIDE, LANES), F32),
        ((2 * TOWER2, LANES), F32),
        ((32, LANES), F32),
        ((HALF, events), F32),
        ((WIDE, events), F32),
        ((WIDE, events), F32),
        ((WIDE, events), F32),
        ((HALF, events), BF),
        ((HALF, events), BF),
        ((HALF + LANES, events), BF),
        ((8, events), F32),
        ((16, events), F32),
        ((16, events), F32),
        ((2 * HID, events), BF),
        ((2 * TOWER1, events), F32),
        ((2 * TOWER1, events), BF),
        ((2 * TOWER2, events), F32),
        ((2 * TOWER2, events), BF),
        ((2 * TOWER1, events), BF),
        ((2 * TOWER1, events), F32),
        ((2 * HID, events), F32),
        ((2 * HID, events), BF),
        ((16, events), F32),
        ((WIDE, events), BF),
        ((2 * TOWER2, LANES), F32),
        ((16, LANES), F32),
        ((2, D, HID), BF),
        ((2, HID, HID), BF),
        ((16, events), F32),
    ]
    arrays = [*started, *oth_groups, own_pack, oth_pack]
    return pl.pallas_call(
        functools.partial(main_kernel, given, plan, rows1, rows2),
        out_shape=results,
        in_specs=[SSPEC] + [VSPEC] * len(arrays),
        out_specs=(VSPEC,) * len(results),
        scratch_shapes=[pltpu.VMEM(dims, kind) for dims, kind in scratch],
        compiler_params=params(42),
        cost_estimate=cost(events * BIG * 196608 * 6, 10e6),
    )(ids, *arrays)


def sibling(value):
    return lax.ppermute(value, "task", [(0, 1), (1, 0)])


def flipped(value, mask):
    pairs = [(i, i ^ mask) for i in range(lax.axis_size("dp"))]
    return lax.ppermute(value, "dp", pairs)


def crossed(value, masks):
    n = lax.axis_size("dp")
    pairs = [(t * n + i, t * n + (i ^ masks[t])) for t in range(2) for i in range(n)]
    return lax.ppermute(value, ("task", "dp"), pairs)


def stack_kernel(count, *refs):
    out, sems = refs[-2:]
    copies = [pltpu.make_async_copy(refs[k], out.at[k], sems.at[k]) for k in range(count)]
    for copy in copies:
        copy.start()
    for copy in copies:
        copy.wait()


def stacked(pieces):
    return pl.pallas_call(
        functools.partial(stack_kernel, len(pieces)),
        out_shape=shape((len(pieces),) + pieces[0].shape, pieces[0].dtype),
        in_specs=[ASPEC] * len(pieces),
        out_specs=VSPEC,
        scratch_shapes=[pltpu.SemaphoreType.DMA((len(pieces),))],
        compiler_params=params(4),
        cost_estimate=cost(0, 1e6),
    )(*pieces)


def summed(*terms):
    total = terms[0].astype(F32)
    for term in terms[1:]:
        total = total + term.astype(F32)
    return total.astype(BF)


def small_sum_kernel(one_ref, two_ref, *refs):
    out_ref = refs[-1]
    out_ref[...] = (one_ref[...].astype(F32) + two_ref[...].astype(F32)).astype(BF)


def small_sum(one, two, *after):
    lead = pl.BlockSpec((SMALL_ROWS, HID), lambda i: (0, 0))
    return pl.pallas_call(
        small_sum_kernel,
        grid=(1,),
        out_shape=shape((SMALL_ROWS, HID)),
        in_specs=[lead, lead] + [ASPEC] * len(after),
        out_specs=lead,
        compiler_params=params(4),
        cost_estimate=cost(8e9, 1e6),
    )(one, two, *after)


def tie_kernel(*refs):
    pass


def tied(value, after):
    return pl.pallas_call(
        tie_kernel,
        out_shape=shape(value.shape, value.dtype),
        in_specs=[ASPEC, ASPEC],
        out_specs=ASPEC,
        input_output_aliases={0: 0},
        compiler_params=params(1),
        cost_estimate=cost(0, 1),
    )(value, after)


def far_kernel(rows, keep_ref, got_ref, mid_ref, near_ref, *outs):
    for k, out in enumerate(outs):
        here = slice(k * rows, (k + 1) * rows)
        total = keep_ref[here, :].astype(F32) + got_ref[here, :].astype(F32)
        at = SMALL_ROWS + k * rows
        total = total + mid_ref[at : at + rows, :].astype(F32)
        out[...] = (total + near_ref[here, :].astype(F32)).astype(BF)


def block(rows, at=0):
    return pl.BlockSpec((rows, HID), lambda i: (at, 0))


def far_messages(far, rows, keep, got, mid, near):
    size = far * rows
    return pl.pallas_call(
        functools.partial(far_kernel, rows),
        grid=(1,),
        out_shape=(shape((rows, HID)),) * far,
        in_specs=[block(size), block(size), block(size + SMALL_ROWS), block(size)],
        out_specs=(block(rows),) * far,
        compiler_params=params(12),
        cost_estimate=cost(0, 4e6),
    )(keep, got, mid, near)


def home_kernel(rows, keep_ref, got_ref, mid_ref, *refs):
    smalls, (message_ref, base_ref) = refs[:-2], refs[-2:]
    total = keep_ref[...].astype(F32) + got_ref[...].astype(F32) + mid_ref[...].astype(F32)
    base_ref[...] = total[:rows]
    message_ref[SMALL_ROWS:, :] = total[rows:].astype(BF)
    small = smalls[0][...].astype(F32)
    for term in smalls[1:]:
        small = small + term[...].astype(F32)
    message_ref[:SMALL_ROWS, :] = small.astype(BF)


def home_message(far, rows, keep, got, mid, smalls):
    at = block(2 * rows, far)
    return pl.pallas_call(
        functools.partial(home_kernel, rows),
        grid=(1,),
        out_shape=(shape((SMALL_ROWS + rows, HID)), shape((rows, HID), F32)),
        in_specs=[at, at, block(2 * rows)] + [block(SMALL_ROWS)] * len(smalls),
        out_specs=(block(SMALL_ROWS + rows), block(rows)),
        compiler_params=params(8),
        cost_estimate=cost(0, 2e6),
    )(keep, got, mid, *smalls)


def total_kernel(*refs):
    total = refs[0][...].astype(F32)
    for term in refs[1:-1]:
        total = total + term[...].astype(F32)
    refs[-1][...] = total


def totalled(*terms):
    return pl.pallas_call(
        total_kernel,
        out_shape=shape(terms[0].shape, F32),
        in_specs=[VSPEC] * len(terms),
        out_specs=VSPEC,
        compiler_params=params(4),
        cost_estimate=cost(10e9, 1e6),
    )(*terms)


def last_kernel(rows1, rows2, paired, ids_ref, *refs):
    if paired:
        part_ref, sent_ref, near_ref = refs[:3]
        total = part_ref[...] + near_ref[SMALL_ROWS:, :].astype(F32)
        small = sent_ref[:SMALL_ROWS, :].astype(F32) + near_ref[:SMALL_ROWS, :].astype(F32)
    else:
        total, small = refs[0][...], refs[1][...]
    w1_ref, w2_ref, o1_ref, o2_ref, sg_ref, ss_ref, og_ref, os_ref, gate_ref, t1_ref, t2_ref, t3_ref = refs[-12:]
    cut = SLOTS * rows1
    for s in range(EXPERTS):
        w1_ref[s] = total[s * rows1 : (s + 1) * rows1]
        w2_ref[s] = total[cut + s * rows2 : cut + (s + 1) * rows2]
    o1_ref[...] = total[EXPERTS * rows1 : cut]
    o2_ref[...] = total[cut + EXPERTS * rows2 :]
    tiny = jnp.concatenate([small[:, :LANES], small[:, LANES:]], axis=0)
    t1_ref[...] = tiny[T1_AT : T1_AT + HID]
    t2_ref[...] = tiny[T2_AT : T2_AT + TOWER2]
    gates = []
    for g in range(GATES):
        at = GATE_AT + 4 * g
        gates.append(jnp.concatenate([tiny[at + p : at + p + 1] for p in range(D // LANES)], axis=1))
    turned = ids_ref[0] != 0
    gate_ref[0:1, :] = gates[0]
    gate_ref[1:2, :] = gates[1]
    gate_ref[2:3, :] = jnp.where(turned, gates[3], gates[2])
    gate_ref[3:4, :] = jnp.where(turned, gates[2], gates[3])
    for kind, (spec, own) in enumerate(((sg_ref, og_ref), (ss_ref, os_ref))):
        for s in range(SLOTS):
            at = MISC_AT + 2 * (kind * SLOTS + s)
            row = jnp.concatenate([tiny[at : at + 1], tiny[at + 1 : at + 2]], axis=1)
            if s < EXPERTS:
                spec[s : s + 1, :] = row
            else:
                own[...] = row
    t3_ref[...] = tiny[MISC_AT + 12 : MISC_AT + 13, :TOWER2]


def finish(ids, terms, rows1, rows2):
    outs = (
        shape((EXPERTS, rows1, HID), F32),
        shape((EXPERTS, rows2, HID), F32),
        shape((rows1, HID), F32),
        shape((rows2, HID), F32),
        shape((EXPERTS, HID), F32),
        shape((EXPERTS, HID), F32),
        shape((1, HID), F32),
        shape((1, HID), F32),
        shape((GATES, D), F32),
        shape((HID, TOWER1), F32),
        shape((TOWER2, TOWER1), F32),
        shape((1, TOWER2), F32),
    )
    return pl.pallas_call(
        functools.partial(last_kernel, rows1, rows2, len(terms) == 3),
        out_shape=outs,
        in_specs=[SSPEC] + [VSPEC] * len(terms),
        out_specs=(VSPEC,) * len(outs),
        compiler_params=params(8),
        cost_estimate=cost(0, 2e6),
    )(ids, *terms)


def per_device(
    entries,
    lengths,
    labels,
    spec_w1,
    spec_w2,
    spec_gain,
    spec_shift,
    shared_w1,
    shared_w2,
    shared_gain,
    shared_shift,
    gate_w,
    tower_w1,
    tower_w2,
    tower_w3,
):
    position = lax.axis_index("task")
    n = lax.axis_size("dp")
    ids = jnp.stack([position, lax.axis_index("dp")]).astype(jnp.int32)
    rows1, rows2 = spec_w1.shape[2], spec_w2.shape[2]
    direct = rows2 % 16 == 0 and n % 4 == 0 and n & (n - 1) == 0
    pack = jnp.concatenate(
        [part.reshape(-1, HID) for part in (spec_w1, shared_w1, spec_w2, shared_w2)], axis=0
    )
    if direct:
        quarter = n // 4
        far = [pack] + [flipped(pack, 4 * k) for k in range(1, quarter)]

    rows = entries.shape[0]
    starts, ends, meta = bags(lengths, rows // ROWS)
    small = pack_small(
        ids,
        labels,
        spec_gain[0],
        spec_shift[0],
        shared_gain,
        shared_shift,
        gate_w[0].T,
        tower_w1[0],
        tower_w2[0].T,
        tower_w3,
    )
    other_small = sibling(small)
    turned = entries.T
    x_first = pool(0, 2, ids, meta, starts, ends, turned)

    if direct:
        zc = stacked(far)
        r1 = tied(crossed(zc, (1, 2)), x_first)
        r2 = crossed(tied(zc, x_first), (2, 1))
        x_second = pool(1, 2, ids, meta, starts, ends, turned, other_small)
        r3 = tied(crossed(r1, (2, 1)), x_second)
        own = [zc, r2, r1, r3]
        given = tuple(tuple((one, two, k) for k in range(quarter)) for one, two in ((0, 0), (0, 1), (1, 0), (1, 1)))
        far_ones = [(two, k) for two in range(2) for k in range(1, quarter)]
        home_ones = [(0, 0), (1, 0)]
        send = [(1, *piece) for piece in far_ones]
        keep = [(0, *piece) for piece in far_ones + home_ones] + [(1, *piece) for piece in home_ones]
        plan, used1, used2 = ((0, tuple(keep)), (1, tuple(send))), rows1, rows2
    else:
        x_second = pool(1, 2, ids, meta, starts, ends, turned)
        every = lax.all_gather(pack, "dp", axis=0)
        cut = SLOTS * rows1
        w1 = every[:, :cut].reshape(n, SLOTS, rows1, HID).swapaxes(0, 1).reshape(-1, HID)
        w2 = every[:, cut:].reshape(n, SLOTS, rows2, HID).swapaxes(0, 1).reshape(-1, HID)
        own = [jnp.concatenate([w1, w2], axis=0)[None]]
        given, plan, used1, used2 = ((None,),), ((1, (None,)),), D, HID
    other = [sibling(group) for group in own]
    started = front(ids, [x_first, x_second], own, given, used1, used2)
    dx, e, f, own_small, *oth_grads = layer(ids, started, other, small, other_small, given, plan, used1, used2)
    got = [sibling(grad) for grad in oth_grads[::-1]][::-1]
    own_grads = back(ids, started[0], started[4], e, f, own_small, plan, used1, used2)
    other_dx = sibling(dx)
    turned, predictions, expanded = expand(ids, meta, starts, ends, dx, other_dx, rows)
    piece = SLOTS * (rows1 + rows2)
    if direct:
        keep, send = own_grads
        far, cut = quarter - 1, (quarter - 1) * piece
        send = summed(send, got[1])
        mid = tied(crossed(send, (1, 2)), expanded)
        home = slice(2 * cut + 2 * piece, 2 * cut + 4 * piece)
        home = summed(keep[home], got[0][home])
        late = slice(cut, 2 * cut)
        near = crossed(summed(keep[late], got[0][late], mid[SMALL_ROWS + cut :]), (2, 1))
        small = small_sum(send, mid)
        home_mid = tied(crossed(home, (1, 2)), expanded)
        mask = n // 2
        while mask > 4:
            small = summed(small, flipped(small, mask))
            mask //= 2
        smalls = [flipped(small, mask)]
        parts = far_messages(far, piece, keep, got[0], mid, near)
        smalls = [small] + [tied(term, parts[0]) for term in smalls]
        message, base = home_message(far, piece, keep, got[0], home_mid, smalls)
        parts = [flipped(part, 4 * (k + 1)) for k, part in enumerate(parts)]
        grads = finish(ids, [totalled(base, *parts), message, crossed(message, (2, 1))], rows1, rows2)
    else:
        whole = own_grads[0].astype(F32) + got[0].astype(F32)
        small = lax.psum(whole[:SMALL_ROWS], "dp")
        whole = whole[SMALL_ROWS:]
        cut = SLOTS * D
        g1 = lax.psum_scatter(whole[:cut].reshape(SLOTS, D, HID), "dp", scatter_dimension=1, tiled=True)
        g2 = lax.psum_scatter(whole[cut:].reshape(SLOTS, HID, HID), "dp", scatter_dimension=1, tiled=True)
        part = jnp.concatenate([g1.reshape(-1, HID), g2.reshape(-1, HID)], axis=0)
        grads = finish(ids, [part, small], rows1, rows2)
    w1, w2, o1, o2, sg, ss, og, os, gate, t1, t2, t3 = grads
    entry_grads = turned.T
    return (
        predictions,
        entry_grads,
        w1[None],
        w2[None],
        sg[None],
        ss[None],
        o1[None],
        o2[None],
        og,
        os,
        gate.T[None],
        t1[None],
        t2.T[None],
        t3,
    )


def solution(mesh):
    placed = (
        P("dp", None),
        P("dp", None),
        P("task", "dp"),
        P("task", None, "dp", None),
        P("task", None, "dp", None),
        P("task", None, None),
        P("task", None, None),
        P("task", "dp", None),
        P("task", "dp", None),
        P("task", None),
        P("task", None),
        P("task", None, None),
        P("task", None, None),
        P("task", None, None),
        P("task", None),
    )
    return jax.shard_map(
        per_device,
        mesh=mesh,
        in_specs=placed,
        out_specs=(
            P("task", "dp"),
            P("dp", None),
            P("task", None, "dp", None),
            P("task", None, "dp", None),
            P("task", None, None),
            P("task", None, None),
            P("task", "dp", None),
            P("task", "dp", None),
            P("task", None),
            P("task", None),
            P("task", None, None),
            P("task", None, None),
            P("task", None, None),
            P("task", None),
        ),
        check_vma=False,
    )
```
